32 devices in a mesh: section: 2 (over core), seq: 16 (over z, y, x).
Axes of the slice: x: 2, y: 2, z: 4, core: 2. Of those that a mesh axis runs over, the one named last changes fastest.
Arguments:
- down_input: bfloat16 [64, 6144], P(None, 'seq'), may hold values from -6 to 6
- up_input: bfloat16 [64, 6144], P(None, 'seq'), may hold values from -6 to 6
- down_cot: bfloat16 [64, 6144], P(None, 'seq'), may hold values from -6 to 6
- up_cot: bfloat16 [64, 6144], P(None, 'seq'), may hold values from -6 to 6
- section_weights: bfloat16 [2, 2, 6144, 6144], P('section', None, 'seq'), as said below
- section_gains: float32 [2, 2, 6144], P('section', None, 'seq'), as said below
Outputs:
- down_outputs: bfloat16 [2, 64, 6144], P('section', None, 'seq')
- up_outputs: bfloat16 [2, 64, 6144], P('section', None, 'seq')
- grad_first: float32 [2, 6144, 3072], P('section', 'seq')
- grad_second: float32 [2, 6144, 3072], P('section', 'seq')
- gain_grads: float32 [2, 6144], P('section', 'seq')
The draws below stay inside these ranges and needn't reach their ends.
Inputs may be any that keep to these rules, and one draw needn't show every extreme that they name: For every i, section_weights[i, 1] equals section_weights[1 - i, 0]. For every i, section_gains[i, 1] equals section_gains[1 - i, 0]; all entries lie in 0.3 to 3.
All inputs are finite; a program needn't handle non-finite values.
Results may differ from the reference program's by a relative error of at most 0.024.
Values may be sent and summed in bfloat16 or wider, within the bound.
No kernel may reach another device: no remote copies, remote signals or barrier semaphores. Data moves between devices by JAX's collectives and lax.ppermute only.
A program may use at most 128 MiB of HBM per device.

```python
import jax
import jax.numpy as jnp
from jax import lax

D = 6144
TOK = 64
SECTIONS = 2
N_SEQ = 16


def draw_section_weights(key, part):
    key = jax.random.fold_in(key, 11)
    values = jax.random.normal(key, (SECTIONS, D, D), jnp.float32) * D ** (-0.5)
    return jnp.stack([values, values[::-1]], axis=1).astype(jnp.bfloat16)


def draw_section_gains(key, part):
    key = jax.random.fold_in(key, 12)
    values = jnp.exp(jax.random.uniform(key, (SECTIONS, D), jnp.float32, -1.2039728, 1.0986123))
    return jnp.stack([values, values[::-1]], axis=1)


def levels(own_key, shape, cuts, least, high):
    gain, own = 1.0, jax.random.fold_in(own_key, 6)
    for position, parts in cuts:
        steps = jnp.exp(jax.random.uniform(jax.random.fold_in(own, position), (parts,), jnp.float32, least / len(cuts), high / len(cuts)))
        gain = gain * jnp.repeat(steps, shape[position] // parts).reshape([-1 if axis == position else 1 for axis in range(len(shape))])
    return gain


def gaussian(rng, extent, scale, limit, cuts=(), held_as=jnp.bfloat16):
    drawn = scale * jax.random.normal(rng, extent, jnp.float32)
    if cuts:
        drawn = drawn * levels(rng, extent, cuts, -0.22, 0.18)
    return jnp.clip(drawn, -limit, limit).astype(held_as)


def setup_inputs(seed: int = 0) -> dict:
    streams_of = jax.random.split(jax.random.key(seed), 7)
    return {
        "down_input": gaussian(streams_of[0], (TOK, D), 1.0, 6.0, ((1, 16),)),
        "up_input": gaussian(streams_of[1], (TOK, D), 1.0, 6.0, ((1, 16),)),
        "down_cot": gaussian(streams_of[2], (TOK, D), 1.0, 6.0, ((1, 16),)),
        "up_cot": gaussian(streams_of[3], (TOK, D), 1.0, 6.0, ((1, 16),)),
        "section_weights": draw_section_weights(jax.random.fold_in(streams_of[6], 71), 0),
        "section_gains": draw_section_gains(jax.random.fold_in(streams_of[6], 71), 0),
    }


EPS = 1e-05

def gelu_exact(values):
    return jax.nn.gelu(values, approximate=False)

def rounded(values):
    return lax.optimization_barrier(values.astype(jnp.bfloat16)).astype(jnp.float32)

def forward_section(inputs, gain_row, weight):
    wide_in = inputs.astype(jnp.float32)
    row_mean = lax.optimization_barrier(jnp.mean(wide_in, axis=1, keepdims=True))
    row_var = lax.optimization_barrier(jnp.mean(wide_in * wide_in, axis=1, keepdims=True)) - row_mean * row_mean
    row_scale = lax.rsqrt(row_var + EPS)
    normal_hat = (wide_in - row_mean) * row_scale
    normed = (normal_hat * gain_row[None, :]).astype(jnp.bfloat16)
    hidden = lax.dot_general(normed, weight, (((1,), (1,)), ((), ())), preferred_element_type=jnp.float32)
    outputs = (wide_in + gelu_exact(hidden)).astype(jnp.bfloat16)
    return (outputs, (normal_hat, row_scale, normed, hidden))

def backward_section(grad_out, saved, gain_row, weight):
    normal_hat, row_scale, normed, hidden = saved
    grad_wide = grad_out.astype(jnp.float32)
    unused, pullback = jax.vjp(gelu_exact, hidden)
    grad_hidden = pullback(grad_wide)[0].astype(jnp.bfloat16)
    tokens = grad_hidden.shape[0]
    model_width = weight.shape[0]
    block_rows = model_width // N_SEQ
    blocks_grad = grad_hidden.astype(jnp.float32).reshape(tokens, N_SEQ, block_rows)
    blocks_weight = weight.astype(jnp.float32).reshape(N_SEQ, block_rows, model_width)
    partial_sums = jnp.einsum('tjf,jfd->jtd', blocks_grad, blocks_weight)
    partial_sums = rounded(partial_sums)
    grad_normed = lax.optimization_barrier(jnp.sum(partial_sums, axis=0))
    grad_hat = grad_normed * gain_row[None, :]
    first_mean = lax.optimization_barrier(jnp.mean(grad_hat, axis=1, keepdims=True))
    second_mean = lax.optimization_barrier(jnp.mean(grad_hat * normal_hat, axis=1, keepdims=True))
    grad_in = (grad_wide + row_scale * (grad_hat - first_mean - normal_hat * second_mean)).astype(jnp.bfloat16)
    grad_gain = lax.optimization_barrier(jnp.sum(grad_normed * normal_hat, axis=0))
    grad_weight = jnp.dot(grad_hidden.T, normed, preferred_element_type=jnp.float32)
    return (grad_in, grad_weight, grad_gain)

def reference(down_input, up_input, down_cot, up_cot, section_weights, section_gains):
    weights = section_weights[:, 0]
    gains = section_gains[:, 0]

    def run_forward(inputs):
        outputs_list = []
        saved_list = []
        current = inputs
        for section_index in range(SECTIONS):
            current, saved = forward_section(current, gains[section_index], weights[section_index])
            outputs_list.append(current)
            saved_list.append(saved)
        return (outputs_list, saved_list)
    down_list, down_saved = run_forward(down_input)
    up_list, up_saved = run_forward(up_input)

    def run_backward(cotangent, saved_list):
        weight_grads = [None] * SECTIONS
        gain_list = [None] * SECTIONS
        current = cotangent
        for section_index in reversed(range(SECTIONS)):
            current, grad_weight, grad_gain = backward_section(current, saved_list[section_index], gains[section_index], weights[section_index])
            weight_grads[section_index] = rounded(grad_weight)
            gain_list[section_index] = rounded(grad_gain)
        return (weight_grads, gain_list)
    down_grads, down_gain_grads = run_backward(down_cot, down_saved)
    up_grads, up_gain_grads = run_backward(up_cot, up_saved)
    half_cols = D // 2
    totals = [down_grads[index] + up_grads[index] for index in range(SECTIONS)]
    grad_first = jnp.stack([totals[index][:, :half_cols] for index in range(SECTIONS)])
    grad_second = jnp.stack([totals[SECTIONS - 1 - index][:, half_cols:] for index in range(SECTIONS)])
    gain_grads = jnp.stack([down_gain_grads[index] + up_gain_grads[index] for index in range(SECTIONS)])
    down_outputs = jnp.stack(down_list)
    up_outputs = jnp.stack(up_list[::-1])
    return (down_outputs, up_outputs, grad_first, grad_second, gain_grads)
```

```python
import functools
import math

import jax
import jax.numpy as jnp
from jax import lax
from jax.experimental import pallas as pl
from jax.experimental.pallas import tpu as pltpu
from jax.sharding import PartitionSpec as P

EPS = 1e-05
F32 = jnp.float32
BF16 = jnp.bfloat16
LANES = 128
PAD_ROWS = 16
SQRT_HALF = math.sqrt(0.5)
INV_SQRT_2PI = 1.0 / math.sqrt(2.0 * math.pi)
VMEM_LIMIT = 48 * 1024 * 1024

ANY = pl.BlockSpec(memory_space=pl.ANY)
VMEM = pl.BlockSpec(memory_space=pltpu.VMEM)
SMEM = pl.BlockSpec(memory_space=pltpu.SMEM)


def from_xor(value, distance):
    size = lax.axis_size("seq")
    return lax.ppermute(value, "seq", [(i, i ^ distance) for i in range(size)])


def swapped(value):
    size = lax.axis_size("section")
    return lax.ppermute(value, "section", [(i, size - 1 - i) for i in range(size)])


def bit_groups(low, count):
    bits = [1 << b for b in range(low, count)][::-1]
    groups = []
    while bits:
        pair, bits = bits[:2], bits[2:]
        groups.append(tuple(pair) if len(pair) == 1 else (pair[0], pair[1], pair[0] ^ pair[1]))
    return groups


def offsets_of(groups):
    offsets = [0]
    for group in groups:
        offsets = [o ^ d for d in (0,) + group for o in offsets]
    return offsets


def gather_xor(block, groups):
    held = block[None]
    for group in groups:
        held = jnp.concatenate([held] + [from_xor(held, d) for d in group], axis=0)
    return held


def reduce_round(held, group):
    sent = [from_xor(held[n + 1], d) for n, d in enumerate(group)]
    return [held[0]] + sent


def gelu_and_slope(z):
    cdf = 0.5 * (1.0 + lax.erf(z * SQRT_HALF))
    slope = cdf + z * (jnp.exp(-0.5 * z * z) * INV_SQRT_2PI)
    return z * cdf, slope


def column_to_row(column):
    tokens = column.shape[0]
    rows = lax.broadcasted_iota(jnp.int32, (tokens, LANES), 0)
    lanes = lax.broadcasted_iota(jnp.int32, (tokens, LANES), 1)
    return jnp.sum(jnp.where(rows == lanes, column, 0.0), axis=0, keepdims=True)


def row_to_column(row, tokens):
    rows = lax.broadcasted_iota(jnp.int32, (tokens, LANES), 0)
    lanes = lax.broadcasted_iota(jnp.int32, (tokens, LANES), 1)
    return jnp.sum(jnp.where(rows == lanes, row, 0.0), axis=1, keepdims=True)


def two_terms(value):
    high = value.astype(BF16)
    return high, (value - high.astype(F32)).astype(BF16)


def three_terms(value):
    high, rest = value.astype(BF16), None
    rest = value - high.astype(F32)
    middle = rest.astype(BF16)
    return high, middle, (rest - middle.astype(F32)).astype(BF16)


def sums_block(first_sum, second_sum):
    row = lax.broadcasted_iota(jnp.int32, (PAD_ROWS, LANES), 0)
    block = jnp.zeros((PAD_ROWS, LANES), F32)
    n = 0
    for column in (first_sum, second_sum):
        for term in two_terms(column_to_row(column)):
            block = jnp.where(row == n, term.astype(F32), block)
            n += 1
    return block.astype(BF16)


def split_packed(total, tokens, width):
    chunks = width // LANES
    du = jnp.concatenate([total[c * tokens : (c + 1) * tokens] for c in range(chunks)], axis=1)
    tail = total[chunks * tokens : chunks * tokens + PAD_ROWS]
    first = row_to_column(tail[0:1] + tail[1:2], tokens)
    second = row_to_column(tail[2:3] + tail[3:4], tokens)
    return du, first, second


def input_gradient(du, first_sum, second_sum, dy, block, mean, scale, gain, model_width):
    hat = (block.astype(F32) - mean) * scale
    gained = du * gain
    dx = dy.astype(F32) + scale * (
        gained - first_sum / model_width - hat * (second_sum / model_width)
    )
    return dx.astype(BF16), jnp.sum(du * hat, axis=0, keepdims=True)


def weight_copies(weights, index, held, sems, chunks):
    width = held.shape[1] // chunks
    return [
        pltpu.make_async_copy(
            weights.at[0, index, :, pl.ds(c * width, width)],
            held.at[:, pl.ds(c * width, width)],
            sems.at[c],
        )
        for c in range(chunks)
    ]


def section_kernel(offsets, dims, forward, unpack, backward, send_order, *refs):
    tokens, block, model_width, chunks = dims
    refs = list(refs)
    take = refs.pop
    scalars = take(0)
    weights = take(0)
    pieces = take(0) if forward else None
    own = take(0) if forward else None
    gains = None if unpack else take(0)
    dy_ref = take(0) if backward else None
    z_ref = None if forward else take(0)
    if forward:
        u_out, stat_out, z_out, y_out = take(0), take(0), take(0), take(0)
    if unpack:
        gains = take(0)
    if backward:
        dz_out, sent_out = take(0), take(0)
    held, sems = refs
    me, windex = scalars[0], scalars[1]
    copies = weight_copies(weights, windex, held, sems, chunks)
    for copy in copies:
        copy.start()
    wide = block
    per = model_width // chunks
    if forward:
        total = jnp.zeros((tokens, LANES), F32)
        squares = jnp.zeros((tokens, LANES), F32)
        for e in range(len(offsets)):
            for c in range(wide // LANES):
                part = pieces[e, 0:tokens, c * LANES : (c + 1) * LANES].astype(F32)
                total = total + part
                squares = squares + part * part
        mean = jnp.sum(total, axis=1, keepdims=True) / model_width
        var = jnp.sum(squares, axis=1, keepdims=True) / model_width - mean * mean
        scale = lax.rsqrt(var + EPS)
        lane = lax.broadcasted_iota(jnp.int32, (tokens, LANES), 1)
        stat_out[...] = jnp.where(lane == 0, mean, scale)
        for e, offset in enumerate(offsets):
            column = pl.multiple_of((me ^ offset) * wide, LANES)
            if unpack:
                terms = pieces[e, tokens : tokens + PAD_ROWS, :].astype(F32)
                gains[0:1, pl.ds(column, wide)] = terms[0:1] + terms[1:2] + terms[2:3]
                gains[1:2, pl.ds(column, wide)] = terms[3:4] + terms[4:5] + terms[5:6]
            gain = gains[pl.ds(windex, 1), pl.ds(column, wide)]
            hat = (pieces[e, 0:tokens, :].astype(F32) - mean) * scale
            u_out[:, pl.ds(column, wide)] = (hat * gain).astype(BF16)
        z = None
        for c, copy in enumerate(copies):
            copy.wait()
            part = lax.dot_general(
                u_out[:, c * per : (c + 1) * per],
                held[:, c * per : (c + 1) * per],
                (((1,), (1,)), ((), ())),
                preferred_element_type=F32,
            )
            z = part if z is None else z + part
        gelu, slope = gelu_and_slope(z)
        z_out[...] = z
        y_out[...] = (own[...].astype(F32) + gelu).astype(BF16)
    if backward:
        if not forward:
            for copy in copies:
                copy.wait()
            z = z_ref[...]
            gelu, slope = gelu_and_slope(z)
        dz = (dy_ref[...].astype(F32) * slope).astype(BF16)
        dz_out[...] = dz
        second = jnp.sum(dz.astype(F32) * z, axis=1, keepdims=True)
        first = jnp.zeros((tokens, LANES), F32)
        for n, offset in enumerate(send_order):
            column = pl.multiple_of((me ^ offset) * wide, LANES)
            part = jnp.dot(dz, held[:, pl.ds(column, wide)], preferred_element_type=F32)
            gained = part * gains[pl.ds(windex, 1), pl.ds(column, wide)]
            for c in range(wide // LANES):
                first = first + gained[:, c * LANES : (c + 1) * LANES]
                sent_out[n, c * tokens : (c + 1) * tokens, :] = part[
                    :, c * LANES : (c + 1) * LANES
                ].astype(BF16)
        tail = sums_block(jnp.sum(first, axis=1, keepdims=True), second)
        rows = tokens * (wide // LANES)
        for n in range(len(send_order)):
            sent_out[n, rows : rows + PAD_ROWS, :] = tail


def section_call(scalars, weights, pieces, own, gains, dy, z, offsets, send_order, wide, unpack):
    forward, backward = pieces is not None, dy is not None
    rows, model_width = weights.shape[2:]
    tokens = (own if forward else dy).shape[0]
    chunks = 4
    operands, specs = [scalars, weights], [SMEM, ANY]
    for value in (pieces, own, gains, dy, z):
        if value is not None:
            operands.append(value)
            specs.append(VMEM)
    outs = []
    if forward:
        outs += [
            jax.ShapeDtypeStruct((tokens, model_width), BF16),
            jax.ShapeDtypeStruct((tokens, LANES), F32),
            jax.ShapeDtypeStruct((tokens, rows), F32),
            jax.ShapeDtypeStruct((tokens, rows), BF16),
        ]
    if unpack:
        outs.append(jax.ShapeDtypeStruct((2, model_width), F32))
    if backward:
        outs += [
            jax.ShapeDtypeStruct((tokens, rows), BF16),
            jax.ShapeDtypeStruct(
                (len(send_order), tokens * (wide // LANES) + PAD_ROWS, LANES), BF16
            ),
        ]
    flops = 2 * tokens * rows * model_width * (int(forward) + int(backward))
    return pl.pallas_call(
        functools.partial(
            section_kernel,
            offsets,
            (tokens, wide, model_width, chunks),
            forward,
            unpack,
            backward,
            send_order,
        ),
        out_shape=outs,
        in_specs=specs,
        out_specs=[VMEM] * len(outs),
        scratch_shapes=[
            pltpu.VMEM((rows, model_width), BF16),
            pltpu.SemaphoreType.DMA((chunks,)),
        ],
        compiler_params=pltpu.CompilerParams(vmem_limit_bytes=VMEM_LIMIT),
        cost_estimate=pl.CostEstimate(
            flops=flops, bytes_accessed=2 * rows * model_width, transcendentals=tokens * rows
        ),
    )(*operands)


def last_kernel(offsets, places, dims, part_count, *refs):
    tokens, wide, model_width, chunks = dims
    scalars, weights, pieces, stat, z_ref, dy_ref = refs[:6]
    refs = refs[6:]
    if part_count:
        parts, (block_ref, next_stat, next_gain), refs = (
            refs[:part_count],
            refs[part_count : part_count + 3],
            refs[part_count + 3 :],
        )
        dz_out, gain_out, next_gain_out, held, sems = refs
    else:
        dz_out, gain_out, held, sems = refs
    me, windex = scalars[0], scalars[1]
    copies = weight_copies(weights, windex, held, sems, chunks)
    for copy in copies:
        copy.start()
    dy = dy_ref[...]
    if part_count:
        total = parts[0][...]
        for part in parts[1:]:
            total = total + part[...].astype(F32)
        du, first, second = split_packed(total, tokens, wide)
        dy, gain_grad = input_gradient(
            du,
            first,
            second,
            dy,
            block_ref[...],
            next_stat[:, 0:1],
            next_stat[:, 1:2],
            next_gain[...],
            model_width,
        )
        next_gain_out[...] = gain_grad
    slope = gelu_and_slope(z_ref[...])[1]
    dz = (dy.astype(F32) * slope).astype(BF16)
    dz_out[...] = dz
    mean, scale = stat[:, 0:1], stat[:, 1:2]
    for copy in copies:
        copy.wait()
    for e, offset in enumerate(offsets):
        column = pl.multiple_of((me ^ offset) * wide, LANES)
        part = jnp.dot(dz, held[:, pl.ds(column, wide)], preferred_element_type=F32)
        hat = (pieces[e, 0:tokens, :].astype(F32) - mean) * scale
        a, b = places[e]
        gain_out[a, b : b + 1, :] = jnp.sum(part * hat, axis=0, keepdims=True)


def last_call(scalars, weights, pieces, stat, z, dy, finish, offsets, send_order, wide, first_size):
    rows, model_width = weights.shape[2:]
    tokens = dy.shape[0]
    chunks = 4
    rest = len(offsets) // first_size
    places = [divmod(send_order.index(o), rest) for o in offsets]
    operands = [scalars, weights, pieces, stat, z, dy]
    outs = [
        jax.ShapeDtypeStruct((tokens, rows), BF16),
        jax.ShapeDtypeStruct((first_size, rest, wide), F32),
    ]
    part_count = 0
    if finish is not None:
        parts, others = finish
        part_count = len(parts)
        operands += list(parts) + list(others)
        outs.append(jax.ShapeDtypeStruct((1, rows), F32))
    return pl.pallas_call(
        functools.partial(
            last_kernel, offsets, places, (tokens, wide, model_width, chunks), part_count
        ),
        out_shape=outs,
        in_specs=[SMEM, ANY] + [VMEM] * (len(operands) - 2),
        out_specs=[VMEM] * len(outs),
        scratch_shapes=[
            pltpu.VMEM((rows, model_width), BF16),
            pltpu.SemaphoreType.DMA((chunks,)),
        ],
        compiler_params=pltpu.CompilerParams(vmem_limit_bytes=VMEM_LIMIT),
        cost_estimate=pl.CostEstimate(
            flops=2 * tokens * rows * model_width,
            bytes_accessed=2 * rows * model_width,
            transcendentals=tokens * rows,
        ),
    )(*operands)


def weight_grad_kernel(dz_first, dz_second, u_first, u_second, first_out, second_out):
    contract = (((0,), (0,)), ((), ()))
    first_out[...] = lax.dot_general(
        dz_first[...], u_first[...], contract, preferred_element_type=F32
    )
    second_out[...] = lax.dot_general(
        dz_second[...], u_second[...], contract, preferred_element_type=F32
    )


def weight_grad_call(dz_first, dz_second, u_first, u_second):
    depth, rows = dz_first.shape
    columns = u_first.shape[1]
    tile = columns // 6
    whole = pl.BlockSpec((depth, rows), lambda i: (0, 0))
    narrow = pl.BlockSpec((depth, tile), lambda i: (0, i))
    out = pl.BlockSpec((rows, tile), lambda i: (0, i))
    return pl.pallas_call(
        weight_grad_kernel,
        grid=(6,),
        out_shape=[jax.ShapeDtypeStruct((rows, columns), F32)] * 2,
        in_specs=[whole, whole, narrow, narrow],
        out_specs=[out, out],
        compiler_params=pltpu.CompilerParams(vmem_limit_bytes=VMEM_LIMIT),
        cost_estimate=pl.CostEstimate(
            flops=4 * depth * rows * columns, bytes_accessed=8 * rows * columns, transcendentals=0
        ),
    )(dz_first, dz_second, u_first, u_second)


def keep_live(live, record, previous):
    if previous is None or live is None:
        return record
    return jax.tree.map(lambda fresh, older: jnp.where(live, fresh, older), record, previous)


def per_device(down_input, up_input, down_cot, up_cot, section_weights, section_gains):
    sections = lax.axis_size("section")
    middle = sections // 2
    position = lax.axis_index("section")
    seq_size = lax.axis_size("seq")
    seq_index = lax.axis_index("seq")
    lower = position < middle
    tokens, block = down_input.shape
    model_width = section_weights.shape[3]
    half = model_width // 2
    merged = 0
    while (block << merged) % LANES:
        merged += 1
    wide = block << merged
    bit_count = seq_size.bit_length() - 1
    groups = bit_groups(merged, bit_count)
    back_groups = groups[::-1]
    offsets = [o >> merged for o in offsets_of(groups)]
    send_order = [0]
    for group in groups:
        send_order = [o ^ (d >> merged) for d in (0,) + group for o in send_order]
    me = (seq_index >> merged).astype(jnp.int32)
    first_index = jnp.where(lower, 0, 1).astype(jnp.int32)
    turn = jnp.minimum(position, sections - 1 - position)

    def index_at(step):
        return first_index if step < middle else 1 - first_index

    def scalars_at(step):
        return jnp.stack([me, index_at(step)]).astype(jnp.int32)

    def live_at(step):
        if sections == 2:
            return None
        return turn == min(step, sections - 1 - step)

    def joined_halves(value, axis):
        for bit in range(merged):
            other = from_xor(value, 1 << bit)
            upper = (seq_index >> bit) & 1
            value = jnp.where(
                upper == 1,
                jnp.concatenate([other, value], axis=axis),
                jnp.concatenate([value, other], axis=axis),
            )
        return value

    def own_part(value, width, bit):
        start = ((seq_index >> bit) & 1) * width
        return (
            lax.dynamic_slice_in_dim(value, start, width, axis=1),
            lax.dynamic_slice_in_dim(value, width - start, width, axis=1),
        )

    def gathered(value):
        return gather_xor(joined_halves(value, 1), groups)

    def moved(value, step, later):
        low = min(step, sections - 1 - step)
        new = min(later, sections - 1 - later)
        if low == new:
            return value
        route = [(low, new), (sections - 1 - low, sections - 1 - new)]
        return lax.ppermute(value, "section", route)

    def reduced(sent):
        parts = None
        for n, group in enumerate(back_groups):
            sent = sent.reshape((len(group) + 1, -1) + sent.shape[1:])
            parts = reduce_round(sent, group)
            if n + 1 < len(back_groups):
                total = functools.reduce(jnp.add, [p.astype(F32) for p in parts])
                sent = total.astype(BF16)
                kept = total[0]
        parts = [kept if len(back_groups) > 1 else parts[0][0].astype(F32)] + [
            p[0] for p in parts[1:]
        ]
        return parts

    def finished(parts):
        total = functools.reduce(jnp.add, [p.astype(F32) for p in parts])
        du, first, second = split_packed(total, tokens, wide)
        for bit in reversed(range(merged)):
            width = du.shape[1] // 2
            mine, theirs = own_part(du, width, bit)
            tail = jnp.concatenate(two_terms(first) + two_terms(second), axis=1)
            message = jnp.concatenate([theirs.astype(BF16), tail], axis=1)
            message = from_xor(message, 1 << bit).astype(F32)
            du = mine + message[:, :width]
            first = first + message[:, width : width + 1] + message[:, width + 1 : width + 2]
            second = second + message[:, width + 2 : width + 3] + message[:, width + 3 :]
        return du, first, second

    own_gains = section_gains[0]
    state = jnp.where(lower, down_input, up_input)
    grad = jnp.where(lower, down_cot, up_cot)
    gain_rows = jnp.stack(three_terms(own_gains[0]) + three_terms(own_gains[1]))
    gain_rows = jnp.pad(gain_rows, ((0, PAD_ROWS - gain_rows.shape[0]), (0, 0)))
    first_record = second_record = None
    gains = None
    for step in range(sections):
        last = step == sections - 1
        payload = jnp.concatenate([state, gain_rows], axis=0) if step == 0 else state
        pieces = gathered(payload)
        result = section_call(
            scalars_at(step),
            section_weights,
            pieces,
            state,
            gains,
            grad if last else None,
            None,
            offsets,
            send_order,
            wide,
            step == 0,
        )
        u, stat, z, y = result[:4]
        if step == 0:
            gains = result[4]
        record = (state, pieces[:, :tokens] if sections > 2 else pieces, u, stat, z, y)
        if step < middle:
            first_record = keep_live(live_at(step), record, first_record)
        else:
            second_record = keep_live(live_at(step), record, second_record)
        if last:
            dz, sent = result[-2:]
        else:
            state = moved(y, step, step + 1)
    u_a, y_a = first_record[2], first_record[5]
    u_b, y_b = second_record[2], second_record[5]
    y_other = swapped(y_b)
    down_out = jnp.where(lower, y_a, y_other)
    up_out = jnp.where(lower, y_other, y_a)
    u_first = jnp.where(lower, u_a[:, :half], u_b[:, :half])
    u_second = jnp.where(lower, u_b[:, half:], u_a[:, half:])
    other_first = swapped(jnp.where(lower, u_b[:, :half], u_a[:, :half]))
    other_second = swapped(jnp.where(lower, u_a[:, half:], u_b[:, half:]))
    u_first = jnp.concatenate([u_first, other_first], axis=0)
    u_second = jnp.concatenate([u_second, other_second], axis=0)

    dz_a = dz_b = gain_b = gain_a = None
    for step in reversed(range(1, sections)):
        source, _, _, stat, z, _ = second_record if step >= middle else first_record
        if step < sections - 1:
            dz, sent = section_call(
                scalars_at(step),
                section_weights,
                None,
                None,
                gains,
                grad,
                z,
                offsets,
                send_order,
                wide,
                False,
            )
        parts = reduced(sent)
        gain_row = lax.dynamic_slice_in_dim(own_gains, index_at(step), 1, axis=0)
        if step >= middle:
            dz_b = keep_live(live_at(step), dz, dz_b)
        else:
            dz_a = keep_live(live_at(step), dz, dz_a)
        finish = None
        if sections == 2 and not merged:
            finish = (parts, (source, stat, gain_row))
        else:
            du, first, second = finished(parts)
            new_grad, gain_grad = input_gradient(
                du,
                first,
                second,
                grad,
                source,
                stat[:, 0:1],
                stat[:, 1:2],
                gain_row,
                model_width,
            )
            if step >= middle:
                gain_b = keep_live(live_at(step), gain_grad, gain_b)
            else:
                gain_a = keep_live(live_at(step), gain_grad, gain_a)
            grad = moved(new_grad, step, step - 1)
    _, pieces, _, stat, z, _ = first_record
    first_size = len(back_groups[0]) + 1
    result = last_call(
        scalars_at(0),
        section_weights,
        pieces,
        stat,
        z,
        grad,
        finish,
        offsets,
        send_order,
        wide,
        first_size,
    )
    dz, gain_parts = result[:2]
    if finish is not None:
        gain_b = result[2]
    dz_a = keep_live(live_at(0), dz, dz_a)
    for n, group in enumerate(back_groups):
        if n:
            gain_parts = gain_parts.reshape((len(group) + 1, -1) + gain_parts.shape[1:])
        gain_parts = functools.reduce(jnp.add, reduce_round(gain_parts, group))
    gain = gain_parts.reshape(1, wide)
    for bit in reversed(range(merged)):
        mine, theirs = own_part(gain, gain.shape[1] // 2, bit)
        gain = mine + from_xor(theirs, 1 << bit)
    gain_a = keep_live(live_at(0), gain, gain_a)

    dz_a_other = swapped(dz_a)
    dz_b_other = swapped(dz_b)
    dz_first = jnp.where(
        lower,
        jnp.concatenate([dz_a, dz_a_other], axis=0),
        jnp.concatenate([dz_b, dz_b_other], axis=0),
    )
    dz_second = jnp.where(
        lower,
        jnp.concatenate([dz_b, dz_b_other], axis=0),
        jnp.concatenate([dz_a, dz_a_other], axis=0),
    )
    grad_first, grad_second = weight_grad_call(dz_first, dz_second, u_first, u_second)
    gain_other = swapped(jnp.where(lower, gain_b, gain_a))
    gain_total = jnp.where(lower, gain_a, gain_b) + gain_other
    return (
        down_out[None],
        up_out[None],
        grad_first[None],
        grad_second[None],
        gain_total,
    )


def solution(mesh):
    in_specs = (
        P(None, "seq"),
        P(None, "seq"),
        P(None, "seq"),
        P(None, "seq"),
        P("section", None, "seq", None),
        P("section", None, "seq"),
    )
    out_specs = (
        P("section", None, "seq"),
        P("section", None, "seq"),
        P("section", "seq", None),
        P("section", "seq", None),
        P("section", "seq"),
    )
    return jax.shard_map(
        per_device, mesh=mesh, in_specs=in_specs, out_specs=out_specs, check_vma=False
    )
```

```python
import functools
import math

import jax
import jax.numpy as jnp
from jax import lax
from jax.experimental import pallas as pl
from jax.experimental.pallas import tpu as pltpu
from jax.sharding import PartitionSpec as P

EPS = 1e-05
F32 = jnp.float32
BF16 = jnp.bfloat16
LANES = 128
PAD_ROWS = 8
SQRT_HALF = math.sqrt(0.5)
INV_SQRT_2PI = 1.0 / math.sqrt(2.0 * math.pi)
VMEM_LIMIT = 32 * 1024 * 1024

VMEM = pl.BlockSpec(memory_space=pltpu.VMEM)
SMEM = pl.BlockSpec(memory_space=pltpu.SMEM)


def from_xor(value, distance):
    size = lax.axis_size("seq")
    return lax.ppermute(value, "seq", [(i, i ^ distance) for i in range(size)])


def swapped(value):
    size = lax.axis_size("section")
    return lax.ppermute(value, "section", [(i, size - 1 - i) for i in range(size)])


def bit_groups(low, count):
    bits = [1 << b for b in range(low, count)][::-1]
    groups = []
    while bits:
        pair, bits = bits[:2], bits[2:]
        groups.append(tuple(pair) if len(pair) == 1 else (pair[0], pair[1], pair[0] ^ pair[1]))
    return groups


def offsets_of(groups):
    offsets = [0]
    for group in groups:
        offsets = [o ^ d for d in (0,) + group for o in offsets]
    return offsets


def gather_xor(block, groups):
    held = block[None]
    for group in groups:
        held = jnp.concatenate([held] + [from_xor(held, d) for d in group], axis=0)
    return held


def reduce_round(held, group):
    sent = [from_xor(held[n + 1], d) for n, d in enumerate(group)]
    return [held[0]] + sent


def gelu_and_slope(z):
    cdf = 0.5 * (1.0 + lax.erf(z * SQRT_HALF))
    slope = cdf + z * (jnp.exp(-0.5 * z * z) * INV_SQRT_2PI)
    return z * cdf, slope


def column_to_row(column):
    tokens = column.shape[0]
    rows = lax.broadcasted_iota(jnp.int32, (tokens, LANES), 0)
    lanes = lax.broadcasted_iota(jnp.int32, (tokens, LANES), 1)
    return jnp.sum(jnp.where(rows == lanes, column, 0.0), axis=0, keepdims=True)


def row_to_column(row, tokens):
    rows = lax.broadcasted_iota(jnp.int32, (tokens, LANES), 0)
    lanes = lax.broadcasted_iota(jnp.int32, (tokens, LANES), 1)
    return jnp.sum(jnp.where(rows == lanes, row, 0.0), axis=1, keepdims=True)


def two_terms(value):
    high = value.astype(BF16)
    return high, (value - high.astype(F32)).astype(BF16)


def three_terms(value):
    high, rest = value.astype(BF16), None
    rest = value - high.astype(F32)
    middle = rest.astype(BF16)
    return high, middle, (rest - middle.astype(F32)).astype(BF16)


def sums_block(first_sum, second_sum):
    row = lax.broadcasted_iota(jnp.int32, (PAD_ROWS, LANES), 0)
    block = jnp.zeros((PAD_ROWS, LANES), F32)
    n = 0
    for column in (first_sum, second_sum):
        for term in two_terms(column_to_row(column)):
            block = jnp.where(row == n, term.astype(F32), block)
            n += 1
    return block.astype(BF16)


def split_packed(total, tokens, width):
    chunks = width // LANES
    du = jnp.concatenate([total[c * tokens : (c + 1) * tokens] for c in range(chunks)], axis=1)
    tail = total[chunks * tokens : chunks * tokens + PAD_ROWS]
    first = row_to_column(tail[0:1] + tail[1:2], tokens)
    second = row_to_column(tail[2:3] + tail[3:4], tokens)
    return du, first, second


def input_gradient(du, first_sum, second_sum, dy, block, mean, scale, gain, model_width):
    hat = (block.astype(F32) - mean) * scale
    gained = du * gain
    dx = dy.astype(F32) + scale * (
        gained - first_sum / model_width - hat * (second_sum / model_width)
    )
    return dx.astype(BF16), jnp.sum(du * hat, axis=0, keepdims=True)


def section_kernel(offsets, dims, forward, unpack, backward, send_order, *refs):
    tokens, block, model_width = dims
    refs = list(refs)
    take = refs.pop
    scalars = take(0)
    weights = take(0)
    pieces = take(0) if forward else None
    own = take(0) if forward else None
    gains = None if unpack else take(0)
    dy_ref = take(0) if backward else None
    z_ref = None if forward else take(0)
    if forward:
        u_out, stat_out, z_out, y_out = take(0), take(0), take(0), take(0)
    if unpack:
        gains = take(0)
    if backward:
        dz_out, sent_out = take(0), take(0)
    me, windex = scalars[0], scalars[1]
    held = weights.at[0, windex]
    wide = block
    if forward:
        total = jnp.zeros((tokens, LANES), F32)
        squares = jnp.zeros((tokens, LANES), F32)
        for e in range(len(offsets)):
            for c in range(wide // LANES):
                part = pieces[e, 0:tokens, c * LANES : (c + 1) * LANES].astype(F32)
                total = total + part
                squares = squares + part * part
        mean = jnp.sum(total, axis=1, keepdims=True) / model_width
        var = jnp.sum(squares, axis=1, keepdims=True) / model_width - mean * mean
        scale = lax.rsqrt(var + EPS)
        lane = lax.broadcasted_iota(jnp.int32, (tokens, LANES), 1)
        stat_out[...] = jnp.where(lane == 0, mean, scale)
        for e, offset in enumerate(offsets):
            column = pl.multiple_of((me ^ offset) * wide, LANES)
            if unpack:
                terms = pieces[e, tokens : tokens + PAD_ROWS, :].astype(F32)
                gains[0:1, pl.ds(column, wide)] = terms[0:1] + terms[1:2] + terms[2:3]
                gains[1:2, pl.ds(column, wide)] = terms[3:4] + terms[4:5] + terms[5:6]
            gain = gains[pl.ds(windex, 1), pl.ds(column, wide)]
            hat = (pieces[e, 0:tokens, :].astype(F32) - mean) * scale
            u_out[:, pl.ds(column, wide)] = (hat * gain).astype(BF16)
        z = lax.dot_general(
            u_out[...], held[...], (((1,), (1,)), ((), ())), preferred_element_type=F32
        )
        gelu, slope = gelu_and_slope(z)
        z_out[...] = z
        y_out[...] = (own[...].astype(F32) + gelu).astype(BF16)
    if backward:
        if not forward:
            z = z_ref[...]
            gelu, slope = gelu_and_slope(z)
        dz = (dy_ref[...].astype(F32) * slope).astype(BF16)
        dz_out[...] = dz
        second = jnp.sum(dz.astype(F32) * z, axis=1, keepdims=True)
        first = jnp.zeros((tokens, LANES), F32)
        for n, offset in enumerate(send_order):
            column = pl.multiple_of((me ^ offset) * wide, LANES)
            part = jnp.dot(dz, held[:, pl.ds(column, wide)], preferred_element_type=F32)
            gained = part * gains[pl.ds(windex, 1), pl.ds(column, wide)]
            for c in range(wide // LANES):
                first = first + gained[:, c * LANES : (c + 1) * LANES]
                sent_out[n, c * tokens : (c + 1) * tokens, :] = part[
                    :, c * LANES : (c + 1) * LANES
                ].astype(BF16)
        tail = sums_block(jnp.sum(first, axis=1, keepdims=True), second)
        rows = tokens * (wide // LANES)
        for n in range(len(send_order)):
            sent_out[n, rows : rows + PAD_ROWS, :] = tail


def section_call(scalars, weights, pieces, own, gains, dy, z, offsets, send_order, wide, unpack):
    forward, backward = pieces is not None, dy is not None
    rows, model_width = weights.shape[2:]
    tokens = (own if forward else dy).shape[0]
    operands, specs = [scalars, weights], [SMEM, VMEM]
    for value in (pieces, own, gains, dy, z):
        if value is not None:
            operands.append(value)
            specs.append(VMEM)
    outs = []
    if forward:
        outs += [
            jax.ShapeDtypeStruct((tokens, model_width), BF16),
            jax.ShapeDtypeStruct((tokens, LANES), F32),
            jax.ShapeDtypeStruct((tokens, rows), F32),
            jax.ShapeDtypeStruct((tokens, rows), BF16),
        ]
    if unpack:
        outs.append(jax.ShapeDtypeStruct((2, model_width), F32))
    if backward:
        outs += [
            jax.ShapeDtypeStruct((tokens, rows), BF16),
            jax.ShapeDtypeStruct(
                (len(send_order), tokens * (wide // LANES) + PAD_ROWS, LANES), BF16
            ),
        ]
    flops = 2 * tokens * rows * model_width * (int(forward) + int(backward))
    return pl.pallas_call(
        functools.partial(
            section_kernel,
            offsets,
            (tokens, wide, model_width),
            forward,
            unpack,
            backward,
            send_order,
        ),
        out_shape=outs,
        in_specs=specs,
        out_specs=[VMEM] * len(outs),
        compiler_params=pltpu.CompilerParams(vmem_limit_bytes=VMEM_LIMIT),
        cost_estimate=pl.CostEstimate(
            flops=flops, bytes_accessed=2 * rows * model_width, transcendentals=tokens * rows
        ),
    )(*operands)


def last_kernel(offsets, places, dims, part_count, *refs):
    tokens, wide, model_width = dims
    scalars, weights, pieces, stat, z_ref, dy_ref = refs[:6]
    refs = refs[6:]
    if part_count:
        parts, (block_ref, next_stat, next_gain), refs = (
            refs[:part_count],
            refs[part_count : part_count + 3],
            refs[part_count + 3 :],
        )
        dz_out, gain_out, next_gain_out = refs
    else:
        dz_out, gain_out = refs
    me, windex = scalars[0], scalars[1]
    held = weights.at[0, windex]
    dy = dy_ref[...]
    if part_count:
        total = parts[0][...]
        for part in parts[1:]:
            total = total + part[...].astype(F32)
        du, first, second = split_packed(total, tokens, wide)
        dy, gain_grad = input_gradient(
            du,
            first,
            second,
            dy,
            block_ref[...],
            next_stat[:, 0:1],
            next_stat[:, 1:2],
            next_gain[...],
            model_width,
        )
        next_gain_out[...] = gain_grad
    slope = gelu_and_slope(z_ref[...])[1]
    dz = (dy.astype(F32) * slope).astype(BF16)
    dz_out[...] = dz
    mean, scale = stat[:, 0:1], stat[:, 1:2]
    for e, offset in enumerate(offsets):
        column = pl.multiple_of((me ^ offset) * wide, LANES)
        part = jnp.dot(dz, held[:, pl.ds(column, wide)], preferred_element_type=F32)
        hat = (pieces[e, 0:tokens, :].astype(F32) - mean) * scale
        a, b = places[e]
        gain_out[a, b : b + 1, :] = jnp.sum(part * hat, axis=0, keepdims=True)


def last_call(scalars, weights, pieces, stat, z, dy, finish, offsets, send_order, wide, first_size):
    rows, model_width = weights.shape[2:]
    tokens = dy.shape[0]
    rest = len(offsets) // first_size
    places = [divmod(send_order.index(o), rest) for o in offsets]
    operands = [scalars, weights, pieces, stat, z, dy]
    outs = [
        jax.ShapeDtypeStruct((tokens, rows), BF16),
        jax.ShapeDtypeStruct((first_size, rest, wide), F32),
    ]
    part_count = 0
    if finish is not None:
        parts, others = finish
        part_count = len(parts)
        operands += list(parts) + list(others)
        outs.append(jax.ShapeDtypeStruct((1, rows), F32))
    return pl.pallas_call(
        functools.partial(
            last_kernel, offsets, places, (tokens, wide, model_width), part_count
        ),
        out_shape=outs,
        in_specs=[SMEM] + [VMEM] * (len(operands) - 1),
        out_specs=[VMEM] * len(outs),
        compiler_params=pltpu.CompilerParams(vmem_limit_bytes=VMEM_LIMIT),
        cost_estimate=pl.CostEstimate(
            flops=2 * tokens * rows * model_width,
            bytes_accessed=2 * rows * model_width,
            transcendentals=tokens * rows,
        ),
    )(*operands)


def weight_grad_kernel(take_early, tile, *refs):
    scalars, early, early_other, late, late_other, u_own, u_other, _, out, order, depth = refs
    tokens = early.shape[0]
    step = pl.program_id(0)

    @pl.when(step == 0)
    def _():
        pick = scalars[1] == (0 if take_early else 1)
        depth[0:tokens] = jnp.where(pick, early[...], late[...])
        depth[tokens:] = jnp.where(pick, early_other[...], late_other[...])
        order[...] = jnp.zeros_like(order)

    columns = pl.ds(pl.multiple_of(step * tile, LANES), tile)
    both = jnp.concatenate([u_own[:, columns], u_other[:, columns]], axis=0)
    out[...] = lax.dot_general(
        depth[...], both, (((0,), (0,)), ((), ())), preferred_element_type=F32
    )


def weight_grad_call(scalars, first, dz_a, dz_a_other, dz_b, dz_b_other, u_own, u_other, after):
    tokens, rows = dz_a.shape
    columns = u_own.shape[1]
    steps = 6
    tile = columns // steps
    return pl.pallas_call(
        functools.partial(weight_grad_kernel, first, tile),
        grid=(steps,),
        out_shape=[
            jax.ShapeDtypeStruct((rows, columns), F32),
            jax.ShapeDtypeStruct((8, LANES), F32),
        ],
        in_specs=[SMEM] + [VMEM] * 7,
        out_specs=[pl.BlockSpec((rows, tile), lambda i: (0, i)), VMEM],
        scratch_shapes=[pltpu.VMEM((2 * tokens, rows), BF16)],
        compiler_params=pltpu.CompilerParams(vmem_limit_bytes=VMEM_LIMIT),
        cost_estimate=pl.CostEstimate(
            flops=4 * tokens * rows * columns, bytes_accessed=4 * rows * columns, transcendentals=0
        ),
    )(scalars, dz_a, dz_a_other, dz_b, dz_b_other, u_own, u_other, after)


def pack_kernel(scalars, down_input, up_input, down_cot, up_cot, gains, state, cot, payload):
    lower = scalars[1] == 0
    tokens = state.shape[0]
    value = jnp.where(lower, down_input[...], up_input[...])
    state[...] = value
    payload[0:tokens] = value
    cot[...] = jnp.where(lower, down_cot[...], up_cot[...])
    row = lax.broadcasted_iota(jnp.int32, (PAD_ROWS, value.shape[1]), 0)
    block = jnp.zeros((PAD_ROWS, value.shape[1]), F32)
    n = 0
    for section in range(2):
        for term in three_terms(gains[section : section + 1, :]):
            block = jnp.where(row == n, term.astype(F32), block)
            n += 1
    payload[tokens:] = block.astype(BF16)


def pack_call(scalars, down_input, up_input, down_cot, up_cot, gains):
    tokens, block = down_input.shape
    return pl.pallas_call(
        pack_kernel,
        out_shape=[
            jax.ShapeDtypeStruct((tokens, block), BF16),
            jax.ShapeDtypeStruct((tokens, block), BF16),
            jax.ShapeDtypeStruct((tokens + PAD_ROWS, block), BF16),
        ],
        in_specs=[SMEM] + [VMEM] * 5,
        out_specs=[VMEM] * 3,
        compiler_params=pltpu.CompilerParams(vmem_limit_bytes=VMEM_LIMIT),
    )(scalars, down_input, up_input, down_cot, up_cot, gains)


def keep_live(live, record, previous):
    if previous is None or live is None:
        return record
    return jax.tree.map(lambda fresh, older: jnp.where(live, fresh, older), record, previous)


def per_device(down_input, up_input, down_cot, up_cot, section_weights, section_gains):
    sections = lax.axis_size("section")
    middle = sections // 2
    position = lax.axis_index("section")
    seq_size = lax.axis_size("seq")
    seq_index = lax.axis_index("seq")
    lower = position < middle
    tokens, block = down_input.shape
    model_width = section_weights.shape[3]
    half = model_width // 2
    merged = 0
    while (block << merged) % LANES:
        merged += 1
    wide = block << merged
    bit_count = seq_size.bit_length() - 1
    groups = bit_groups(merged, bit_count)
    back_groups = [group[::-1] for group in groups[::-1]]
    offsets = [o >> merged for o in offsets_of(groups)]
    send_order = [o >> merged for o in offsets_of(back_groups[::-1])]
    me = (seq_index >> merged).astype(jnp.int32)
    first_index = jnp.where(lower, 0, 1).astype(jnp.int32)
    turn = jnp.minimum(position, sections - 1 - position)

    def index_at(step):
        return first_index if step < middle else 1 - first_index

    def scalars_at(step):
        return jnp.stack([me, index_at(step)]).astype(jnp.int32)

    def live_at(step):
        if sections == 2:
            return None
        return turn == min(step, sections - 1 - step)

    def joined_halves(value, axis):
        for bit in range(merged):
            other = from_xor(value, 1 << bit)
            upper = (seq_index >> bit) & 1
            value = jnp.where(
                upper == 1,
                jnp.concatenate([other, value], axis=axis),
                jnp.concatenate([value, other], axis=axis),
            )
        return value

    def own_part(value, width, bit):
        start = ((seq_index >> bit) & 1) * width
        return (
            lax.dynamic_slice_in_dim(value, start, width, axis=1),
            lax.dynamic_slice_in_dim(value, width - start, width, axis=1),
        )

    def gathered(value):
        return gather_xor(joined_halves(value, 1), groups)

    def moved(value, step, later):
        low = min(step, sections - 1 - step)
        new = min(later, sections - 1 - later)
        if low == new:
            return value
        route = [(low, new), (sections - 1 - low, sections - 1 - new)]
        return lax.ppermute(value, "section", route)

    def reduced(sent):
        parts = None
        for n, group in enumerate(back_groups):
            sent = sent.reshape((len(group) + 1, -1) + sent.shape[1:])
            parts = reduce_round(sent, group)
            if n + 1 < len(back_groups):
                total = functools.reduce(jnp.add, [p.astype(F32) for p in parts])
                sent = total.astype(BF16)
                kept = total[0]
        parts = [kept if len(back_groups) > 1 else parts[0][0].astype(F32)] + [
            p[0] for p in parts[1:]
        ]
        return parts

    def finished(parts):
        total = functools.reduce(jnp.add, [p.astype(F32) for p in parts])
        du, first, second = split_packed(total, tokens, wide)
        for bit in reversed(range(merged)):
            width = du.shape[1] // 2
            mine, theirs = own_part(du, width, bit)
            tail = jnp.concatenate(two_terms(first) + two_terms(second), axis=1)
            message = jnp.concatenate([theirs.astype(BF16), tail], axis=1)
            message = from_xor(message, 1 << bit).astype(F32)
            du = mine + message[:, :width]
            first = first + message[:, width : width + 1] + message[:, width + 1 : width + 2]
            second = second + message[:, width + 2 : width + 3] + message[:, width + 3 :]
        return du, first, second

    own_gains = section_gains[0]
    state, grad, packed = pack_call(
        scalars_at(0), down_input, up_input, down_cot, up_cot, own_gains
    )
    first_record = second_record = None
    gains = None
    for step in range(sections):
        last = step == sections - 1
        pieces = gathered(packed if step == 0 else state)
        result = section_call(
            scalars_at(step),
            section_weights,
            pieces,
            state,
            gains,
            grad if last else None,
            None,
            offsets,
            send_order,
            wide,
            step == 0,
        )
        u, stat, z, y = result[:4]
        if step == 0:
            gains = result[4]
        record = (state, pieces[:, :tokens] if sections > 2 else pieces, u, stat, z, y)
        if step < middle:
            first_record = keep_live(live_at(step), record, first_record)
        else:
            second_record = keep_live(live_at(step), record, second_record)
        if last:
            dz, sent = result[-2:]
        else:
            state = moved(y, step, step + 1)
    u_a, y_a = first_record[2], first_record[5]
    u_b, y_b = second_record[2], second_record[5]
    y_other = swapped(y_b)
    down_out = jnp.where(lower, y_a, y_other)
    up_out = jnp.where(lower, y_other, y_a)
    u_first = jnp.where(lower, u_a[:, :half], u_b[:, :half])
    u_second = jnp.where(lower, u_b[:, half:], u_a[:, half:])
    other_first = swapped(jnp.where(lower, u_b[:, :half], u_a[:, :half]))
    other_second = swapped(jnp.where(lower, u_a[:, half:], u_b[:, half:]))
    dz_a = dz_b = gain_b = gain_a = None
    for step in reversed(range(1, sections)):
        source, _, _, stat, z, _ = second_record if step >= middle else first_record
        if step < sections - 1:
            dz, sent = section_call(
                scalars_at(step),
                section_weights,
                None,
                None,
                gains,
                grad,
                z,
                offsets,
                send_order,
                wide,
                False,
            )
        parts = reduced(sent)
        gain_row = lax.dynamic_slice_in_dim(own_gains, index_at(step), 1, axis=0)
        if step >= middle:
            dz_b = keep_live(live_at(step), dz, dz_b)
        else:
            dz_a = keep_live(live_at(step), dz, dz_a)
        finish = None
        if sections == 2 and not merged:
            finish = (parts, (source, stat, gain_row))
        else:
            du, first, second = finished(parts)
            new_grad, gain_grad = input_gradient(
                du,
                first,
                second,
                grad,
                source,
                stat[:, 0:1],
                stat[:, 1:2],
                gain_row,
                model_width,
            )
            if step >= middle:
                gain_b = keep_live(live_at(step), gain_grad, gain_b)
            else:
                gain_a = keep_live(live_at(step), gain_grad, gain_a)
            grad = moved(new_grad, step, step - 1)
    _, pieces, _, stat, z, _ = first_record
    first_size = len(back_groups[0]) + 1
    result = last_call(
        scalars_at(0),
        section_weights,
        pieces,
        stat,
        z,
        grad,
        finish,
        offsets,
        send_order,
        wide,
        first_size,
    )
    dz, gain_parts = result[:2]
    if finish is not None:
        gain_b = result[2]
    dz_a = keep_live(live_at(0), dz, dz_a)
    dz_a_other = swapped(dz_a)
    dz_b_other = swapped(dz_b)
    dz_all = (dz_a, dz_a_other, dz_b, dz_b_other)
    grads = []
    token = jnp.zeros((8, LANES), F32)
    halves = [(True, u_first, other_first), (False, u_second, other_second)]
    for n, group in enumerate(back_groups):
        if n:
            gain_parts = gain_parts.reshape((len(group) + 1, -1) + gain_parts.shape[1:])
        parts = reduce_round(gain_parts, group)
        if halves:
            first, mine, theirs = halves.pop(0)
            grad_half, token = weight_grad_call(
                scalars_at(0), first, *dz_all, mine, theirs, token
            )
            grads.append(grad_half)
            parts.append(token[0, 0])
        gain_parts = functools.reduce(jnp.add, parts)
    for first, mine, theirs in halves:
        grads.append(weight_grad_call(scalars_at(0), first, *dz_all, mine, theirs, token)[0])
    grad_first, grad_second = grads
    gain = gain_parts.reshape(1, wide)
    for bit in reversed(range(merged)):
        mine, theirs = own_part(gain, gain.shape[1] // 2, bit)
        gain = mine + from_xor(theirs, 1 << bit)
    gain_a = keep_live(live_at(0), gain, gain_a)
    gain_other = swapped(jnp.where(lower, gain_b, gain_a))
    gain_total = jnp.where(lower, gain_a, gain_b) + gain_other
    return (
        down_out[None],
        up_out[None],
        grad_first[None],
        grad_second[None],
        gain_total,
    )


def solution(mesh):
    in_specs = (
        P(None, "seq"),
        P(None, "seq"),
        P(None, "seq"),
        P(None, "seq"),
        P("section", None, "seq", None),
        P("section", None, "seq"),
    )
    out_specs = (
        P("section", None, "seq"),
        P("section", None, "seq"),
        P("section", "seq", None),
        P("section", "seq", None),
        P("section", "seq"),
    )
    return jax.shard_map(
        per_device, mesh=mesh, in_specs=in_specs, out_specs=out_specs, check_vma=False
    )
```

```python
import functools
import math

import jax
import jax.numpy as jnp
from jax import lax
from jax.experimental import pallas as pl
from jax.experimental.pallas import tpu as pltpu
from jax.sharding import PartitionSpec as P

EPS = 1e-05
F32 = jnp.float32
BF16 = jnp.bfloat16
LANES = 128
PAD_ROWS = 8
SQRT_HALF = math.sqrt(0.5)
INV_SQRT_2PI = 1.0 / math.sqrt(2.0 * math.pi)
VMEM_LIMIT = 32 * 1024 * 1024

VMEM = pl.BlockSpec(memory_space=pltpu.VMEM)
ANY = pl.BlockSpec(memory_space=pl.ANY)
SMEM = pl.BlockSpec(memory_space=pltpu.SMEM)


def from_xor(value, distance):
    size = lax.axis_size("seq")
    return lax.ppermute(value, "seq", [(i, i ^ distance) for i in range(size)])


def swapped(value):
    size = lax.axis_size("section")
    return lax.ppermute(value, "section", [(i, size - 1 - i) for i in range(size)])


def bit_groups(low, count):
    bits = [1 << b for b in range(low, count)][::-1]
    groups = []
    while bits:
        pair, bits = bits[:2], bits[2:]
        groups.append(tuple(pair) if len(pair) == 1 else (pair[0], pair[1], pair[0] ^ pair[1]))
    return groups


def offsets_of(groups):
    offsets = [0]
    for group in groups:
        offsets = [o ^ d for d in (0,) + group for o in offsets]
    return offsets


def gather_xor(block, groups):
    held = block[None]
    for n, group in enumerate(groups):
        if n <= 1:
            early = held
        held = jnp.concatenate([held] + [from_xor(held, d) for d in group], axis=0)
    return held, early


def reduce_round(held, group):
    sent = [from_xor(held[n + 1], d) for n, d in enumerate(group)]
    return [held[0]] + sent


def gelu_and_slope(z):
    cdf = 0.5 * (1.0 + lax.erf(z * SQRT_HALF))
    slope = cdf + z * (jnp.exp(-0.5 * z * z) * INV_SQRT_2PI)
    return z * cdf, slope


def column_to_row(column):
    tokens = column.shape[0]
    rows = lax.broadcasted_iota(jnp.int32, (tokens, LANES), 0)
    lanes = lax.broadcasted_iota(jnp.int32, (tokens, LANES), 1)
    return jnp.sum(jnp.where(rows == lanes, column, 0.0), axis=0, keepdims=True)


def row_to_column(row, tokens):
    rows = lax.broadcasted_iota(jnp.int32, (tokens, LANES), 0)
    lanes = lax.broadcasted_iota(jnp.int32, (tokens, LANES), 1)
    return jnp.sum(jnp.where(rows == lanes, row, 0.0), axis=1, keepdims=True)


def two_terms(value):
    high = value.astype(BF16)
    return high, (value - high.astype(F32)).astype(BF16)


def three_terms(value):
    high, rest = value.astype(BF16), None
    rest = value - high.astype(F32)
    middle = rest.astype(BF16)
    return high, middle, (rest - middle.astype(F32)).astype(BF16)


def sums_block(first_sum, second_sum):
    row = lax.broadcasted_iota(jnp.int32, (PAD_ROWS, LANES), 0)
    block = jnp.zeros((PAD_ROWS, LANES), F32)
    n = 0
    for column in (first_sum, second_sum):
        for term in two_terms(column_to_row(column)):
            block = jnp.where(row == n, term.astype(F32), block)
            n += 1
    return block.astype(BF16)


def split_packed(total, tokens, width):
    chunks = width // LANES
    du = jnp.concatenate([total[c * tokens : (c + 1) * tokens] for c in range(chunks)], axis=1)
    tail = total[chunks * tokens : chunks * tokens + PAD_ROWS]
    first = row_to_column(tail[0:1] + tail[1:2], tokens)
    second = row_to_column(tail[2:3] + tail[3:4], tokens)
    return du, first, second


def input_gradient(du, first_sum, second_sum, dy, block, mean, scale, gain, model_width):
    hat = (block.astype(F32) - mean) * scale
    gained = du * gain
    dx = dy.astype(F32) + scale * (
        gained - first_sum / model_width - hat * (second_sum / model_width)
    )
    return dx.astype(BF16), jnp.sum(du * hat, axis=0, keepdims=True)


def section_kernel(offsets, dims, forward, unpack, backward, send_order, *refs):
    tokens, block, model_width = dims
    refs = list(refs)
    take = refs.pop
    scalars = take(0)
    weights = take(0)
    pieces = take(0) if forward else None
    own = take(0) if forward else None
    gains = None if unpack else take(0)
    dy_ref = take(0) if backward else None
    z_ref = None if forward else take(0)
    if forward:
        u_out, stat_out, z_out, y_out = take(0), take(0), take(0), take(0)
    if unpack:
        gains = take(0)
    if backward:
        dz_out, sent_out = take(0), take(0)
    me, windex = scalars[0], scalars[1]
    held = weights.at[0, windex]
    wide = block
    if forward:
        total = jnp.zeros((tokens, LANES), F32)
        squares = jnp.zeros((tokens, LANES), F32)
        for e in range(len(offsets)):
            for c in range(wide // LANES):
                part = pieces[e, 0:tokens, c * LANES : (c + 1) * LANES].astype(F32)
                total = total + part
                squares = squares + part * part
        mean = jnp.sum(total, axis=1, keepdims=True) / model_width
        var = jnp.sum(squares, axis=1, keepdims=True) / model_width - mean * mean
        scale = lax.rsqrt(var + EPS)
        lane = lax.broadcasted_iota(jnp.int32, (tokens, LANES), 1)
        stat_out[...] = jnp.where(lane == 0, mean, scale)
        for e, offset in enumerate(offsets):
            column = pl.multiple_of((me ^ offset) * wide, LANES)
            if unpack:
                terms = pieces[e, tokens : tokens + PAD_ROWS, :].astype(F32)
                gains[0:1, pl.ds(column, wide)] = terms[0:1] + terms[1:2] + terms[2:3]
                gains[1:2, pl.ds(column, wide)] = terms[3:4] + terms[4:5] + terms[5:6]
            gain = gains[pl.ds(windex, 1), pl.ds(column, wide)]
            hat = (pieces[e, 0:tokens, :].astype(F32) - mean) * scale
            u_out[:, pl.ds(column, wide)] = (hat * gain).astype(BF16)
        z = lax.dot_general(
            u_out[...], held[...], (((1,), (1,)), ((), ())), preferred_element_type=F32
        )
        gelu, slope = gelu_and_slope(z)
        z_out[...] = z
        y_out[...] = (own[...].astype(F32) + gelu).astype(BF16)
    if backward:
        if not forward:
            z = z_ref[...]
            gelu, slope = gelu_and_slope(z)
        dz = (dy_ref[...].astype(F32) * slope).astype(BF16)
        dz_out[...] = dz
        second = jnp.sum(dz.astype(F32) * z, axis=1, keepdims=True)
        first = jnp.zeros((tokens, LANES), F32)
        for n, offset in enumerate(send_order):
            column = pl.multiple_of((me ^ offset) * wide, LANES)
            part = jnp.dot(dz, held[:, pl.ds(column, wide)], preferred_element_type=F32)
            gained = part * gains[pl.ds(windex, 1), pl.ds(column, wide)]
            for c in range(wide // LANES):
                first = first + gained[:, c * LANES : (c + 1) * LANES]
                sent_out[n, c * tokens : (c + 1) * tokens, :] = part[
                    :, c * LANES : (c + 1) * LANES
                ].astype(BF16)
        tail = sums_block(jnp.sum(first, axis=1, keepdims=True), second)
        rows = tokens * (wide // LANES)
        for n in range(len(send_order)):
            sent_out[n, rows : rows + PAD_ROWS, :] = tail


def section_call(scalars, weights, pieces, own, gains, dy, z, offsets, send_order, wide, unpack):
    forward, backward = pieces is not None, dy is not None
    rows, model_width = weights.shape[2:]
    tokens = (own if forward else dy).shape[0]
    operands, specs = [scalars, weights], [SMEM, VMEM]
    for value in (pieces, own, gains, dy, z):
        if value is not None:
            operands.append(value)
            specs.append(VMEM)
    outs = []
    if forward:
        outs += [
            jax.ShapeDtypeStruct((tokens, model_width), BF16),
            jax.ShapeDtypeStruct((tokens, LANES), F32),
            jax.ShapeDtypeStruct((tokens, rows), F32),
            jax.ShapeDtypeStruct((tokens, rows), BF16),
        ]
    if unpack:
        outs.append(jax.ShapeDtypeStruct((2, model_width), F32))
    if backward:
        outs += [
            jax.ShapeDtypeStruct((tokens, rows), BF16),
            jax.ShapeDtypeStruct(
                (len(send_order), tokens * (wide // LANES) + PAD_ROWS, LANES), BF16
            ),
        ]
    flops = 2 * tokens * rows * model_width * (int(forward) + int(backward))
    return pl.pallas_call(
        functools.partial(
            section_kernel,
            offsets,
            (tokens, wide, model_width),
            forward,
            unpack,
            backward,
            send_order,
        ),
        out_shape=outs,
        in_specs=specs,
        out_specs=[VMEM] * len(outs),
        compiler_params=pltpu.CompilerParams(vmem_limit_bytes=VMEM_LIMIT),
        cost_estimate=pl.CostEstimate(
            flops=flops, bytes_accessed=2 * rows * model_width, transcendentals=tokens * rows
        ),
    )(*operands)


def last_kernel(offsets, places, dims, part_count, *refs):
    tokens, wide, model_width, first_size = dims
    scalars, weights, pieces, stat, z_ref, dy_ref = refs[:6]
    refs = refs[6:]
    if part_count:
        parts, (block_ref, next_stat, next_gain), refs = (
            refs[:part_count],
            refs[part_count : part_count + 3],
            refs[part_count + 3 :],
        )
        next_gain_out = refs[-1]
    dz_out, gain_out = refs[0], refs[1 : 1 + first_size]
    me, windex = scalars[0], scalars[1]
    held = weights.at[0, windex]
    dy = dy_ref[...]
    if part_count:
        total = parts[0][...]
        for part in parts[1:]:
            total = total + part[...].astype(F32)
        du, first, second = split_packed(total, tokens, wide)
        dy, gain_grad = input_gradient(
            du,
            first,
            second,
            dy,
            block_ref[...],
            next_stat[:, 0:1],
            next_stat[:, 1:2],
            next_gain[...],
            model_width,
        )
        next_gain_out[...] = gain_grad
    slope = gelu_and_slope(z_ref[...])[1]
    dz = (dy.astype(F32) * slope).astype(BF16)
    dz_out[...] = dz
    mean, scale = stat[:, 0:1], stat[:, 1:2]
    for e, offset in enumerate(offsets):
        column = pl.multiple_of((me ^ offset) * wide, LANES)
        part = jnp.dot(dz, held[:, pl.ds(column, wide)], preferred_element_type=F32)
        hat = (pieces[e, 0:tokens, :].astype(F32) - mean) * scale
        a, b = places[e]
        gain_out[a][b : b + 1, :] = jnp.sum(part * hat, axis=0, keepdims=True)


def last_call(scalars, weights, pieces, stat, z, dy, finish, offsets, send_order, wide, first_size):
    rows, model_width = weights.shape[2:]
    tokens = dy.shape[0]
    rest = len(offsets) // first_size
    places = [divmod(send_order.index(o), rest) for o in offsets]
    operands = [scalars, weights, pieces, stat, z, dy]
    outs = [
        jax.ShapeDtypeStruct((tokens, rows), BF16),
    ] + [jax.ShapeDtypeStruct((rest, wide), F32)] * first_size
    part_count = 0
    if finish is not None:
        parts, others = finish
        part_count = len(parts)
        operands += list(parts) + list(others)
        outs.append(jax.ShapeDtypeStruct((1, rows), F32))
    return pl.pallas_call(
        functools.partial(
            last_kernel,
            offsets,
            places,
            (tokens, wide, model_width, first_size),
            part_count,
        ),
        out_shape=outs,
        in_specs=[SMEM] + [VMEM] * (len(operands) - 1),
        out_specs=[VMEM] * len(outs),
        compiler_params=pltpu.CompilerParams(vmem_limit_bytes=VMEM_LIMIT),
        cost_estimate=pl.CostEstimate(
            flops=2 * tokens * rows * model_width,
            bytes_accessed=2 * rows * model_width,
            transcendentals=tokens * rows,
        ),
    )(*operands)


def weight_grad_kernel(take_early, *refs):
    scalars, early, early_other, late, late_other, u_own, u_other, _, out, order, depth = refs
    tokens = early.shape[0]

    @pl.when(pl.program_id(0) == 0)
    def _():
        pick = scalars[1] == (0 if take_early else 1)
        mine = jnp.where(pick, early[...], late[...])
        theirs = jnp.where(pick, early_other[...], late_other[...])
        depth[...] = jnp.concatenate([mine, theirs], axis=0).T
        order[...] = jnp.zeros_like(order)

    both = jnp.concatenate([u_own[...], u_other[...]], axis=0)
    out[...] = jnp.dot(depth[...], both, preferred_element_type=F32)


def weight_grad_call(scalars, first, dz_a, dz_a_other, dz_b, dz_b_other, u_own, u_other, after):
    tokens, rows = dz_a.shape
    columns = u_own.shape[1]
    steps = 4
    tile = columns // steps
    whole = pl.BlockSpec((tokens, rows), lambda i: (0, 0))
    narrow = pl.BlockSpec((tokens, tile), lambda i: (0, i))
    small = pl.BlockSpec(after.shape, lambda i: (0,) * after.ndim)
    return pl.pallas_call(
        functools.partial(weight_grad_kernel, first),
        grid=(steps,),
        out_shape=[
            jax.ShapeDtypeStruct((rows, columns), F32),
            jax.ShapeDtypeStruct(after.shape, F32),
        ],
        in_specs=[SMEM] + [whole] * 4 + [narrow] * 2 + [small],
        out_specs=[pl.BlockSpec((rows, tile), lambda i: (0, i)), small],
        scratch_shapes=[pltpu.VMEM((rows, 2 * tokens), BF16)],
        compiler_params=pltpu.CompilerParams(vmem_limit_bytes=VMEM_LIMIT),
        cost_estimate=pl.CostEstimate(
            flops=4 * tokens * rows * columns, bytes_accessed=4 * rows * columns, transcendentals=0
        ),
    )(scalars, dz_a, dz_a_other, dz_b, dz_b_other, u_own, u_other, after)


def load_kernel(weights, _, held, sems):
    copies = [
        pltpu.make_async_copy(weights.at[0, n], held.at[0, n], sems.at[n]) for n in range(2)
    ]
    for copy in copies:
        copy.start()
    for copy in copies:
        copy.wait()


def load_call(weights, after):
    return pl.pallas_call(
        load_kernel,
        out_shape=jax.ShapeDtypeStruct(weights.shape, weights.dtype),
        in_specs=[ANY, ANY],
        out_specs=VMEM,
        scratch_shapes=[pltpu.SemaphoreType.DMA((2,))],
        compiler_params=pltpu.CompilerParams(vmem_limit_bytes=VMEM_LIMIT),
        cost_estimate=pl.CostEstimate(
            flops=0, bytes_accessed=2 * weights.size, transcendentals=0
        ),
    )(weights, after)


def pack_kernel(scalars, *refs):
    sources, gains_source, (state, cot, payload), gains, sems = (
        refs[:4],
        refs[4],
        refs[5:8],
        refs[8],
        refs[9],
    )
    tokens = state.shape[0]
    gains_copy = pltpu.make_async_copy(gains_source, gains, sems.at[0])
    gains_copy.start()
    for n in range(2):

        @pl.when(scalars[1] == n)
        def _():
            pltpu.make_async_copy(sources[n], state, sems.at[1]).start()
            pltpu.make_async_copy(sources[2 + n], cot, sems.at[2]).start()

    gains_copy.wait()
    row = lax.broadcasted_iota(jnp.int32, (PAD_ROWS, state.shape[1]), 0)
    block = jnp.zeros((PAD_ROWS, state.shape[1]), F32)
    n = 0
    for section in range(2):
        for term in three_terms(gains[section : section + 1, :]):
            block = jnp.where(row == n, term.astype(F32), block)
            n += 1
    payload[tokens:] = block.astype(BF16)
    pltpu.make_async_copy(sources[0], state, sems.at[1]).wait()
    payload[0:tokens] = state[...]
    pltpu.make_async_copy(sources[2], cot, sems.at[2]).wait()


def pack_call(scalars, down_input, up_input, down_cot, up_cot, gains):
    tokens, block = down_input.shape
    return pl.pallas_call(
        pack_kernel,
        out_shape=[
            jax.ShapeDtypeStruct((tokens, block), BF16),
            jax.ShapeDtypeStruct((tokens, block), BF16),
            jax.ShapeDtypeStruct((tokens + PAD_ROWS, block), BF16),
        ],
        in_specs=[SMEM] + [ANY] * 5,
        out_specs=[VMEM] * 3,
        scratch_shapes=[pltpu.VMEM(gains.shape, F32), pltpu.SemaphoreType.DMA((3,))],
        compiler_params=pltpu.CompilerParams(vmem_limit_bytes=VMEM_LIMIT),
    )(scalars, down_input, up_input, down_cot, up_cot, gains)


def keep_live(live, record, previous):
    if previous is None or live is None:
        return record
    return jax.tree.map(lambda fresh, older: jnp.where(live, fresh, older), record, previous)


def per_device(down_input, up_input, down_cot, up_cot, section_weights, section_gains):
    sections = lax.axis_size("section")
    middle = sections // 2
    position = lax.axis_index("section")
    seq_size = lax.axis_size("seq")
    seq_index = lax.axis_index("seq")
    lower = position < middle
    tokens, block = down_input.shape
    model_width = section_weights.shape[3]
    half = model_width // 2
    merged = 0
    while (block << merged) % LANES:
        merged += 1
    wide = block << merged
    bit_count = seq_size.bit_length() - 1
    groups = bit_groups(merged, bit_count)
    back_groups = [group[::-1] for group in groups[::-1]]
    offsets = [o >> merged for o in offsets_of(groups)]
    send_order = [o >> merged for o in offsets_of(back_groups[::-1])]
    me = (seq_index >> merged).astype(jnp.int32)
    first_index = jnp.where(lower, 0, 1).astype(jnp.int32)
    turn = jnp.minimum(position, sections - 1 - position)

    def index_at(step):
        return first_index if step < middle else 1 - first_index

    def scalars_at(step):
        return jnp.stack([me, index_at(step)]).astype(jnp.int32)

    def live_at(step):
        if sections == 2:
            return None
        return turn == min(step, sections - 1 - step)

    def joined_halves(value, axis):
        for bit in range(merged):
            other = from_xor(value, 1 << bit)
            upper = (seq_index >> bit) & 1
            value = jnp.where(
                upper == 1,
                jnp.concatenate([other, value], axis=axis),
                jnp.concatenate([value, other], axis=axis),
            )
        return value

    def own_part(value, width, bit):
        start = ((seq_index >> bit) & 1) * width
        return (
            lax.dynamic_slice_in_dim(value, start, width, axis=1),
            lax.dynamic_slice_in_dim(value, width - start, width, axis=1),
        )

    def gathered(value):
        return gather_xor(joined_halves(value, 1), groups)

    def moved(value, step, later):
        low = min(step, sections - 1 - step)
        new = min(later, sections - 1 - later)
        if low == new:
            return value
        route = [(low, new), (sections - 1 - low, sections - 1 - new)]
        return lax.ppermute(value, "section", route)

    def reduced(sent):
        parts = None
        for n, group in enumerate(back_groups):
            sent = sent.reshape((len(group) + 1, -1) + sent.shape[1:])
            parts = reduce_round(sent, group)
            if n + 1 < len(back_groups):
                total = functools.reduce(jnp.add, [p.astype(F32) for p in parts])
                sent = total.astype(BF16)
                kept = total[0]
        parts = [kept if len(back_groups) > 1 else parts[0][0].astype(F32)] + [
            p[0] for p in parts[1:]
        ]
        return parts

    def finished(parts):
        total = functools.reduce(jnp.add, [p.astype(F32) for p in parts])
        du, first, second = split_packed(total, tokens, wide)
        for bit in reversed(range(merged)):
            width = du.shape[1] // 2
            mine, theirs = own_part(du, width, bit)
            tail = jnp.concatenate(two_terms(first) + two_terms(second), axis=1)
            message = jnp.concatenate([theirs.astype(BF16), tail], axis=1)
            message = from_xor(message, 1 << bit).astype(F32)
            du = mine + message[:, :width]
            first = first + message[:, width : width + 1] + message[:, width + 1 : width + 2]
            second = second + message[:, width + 2 : width + 3] + message[:, width + 3 :]
        return du, first, second

    own_gains = section_gains[0]
    state, grad, packed = pack_call(
        scalars_at(0), down_input, up_input, down_cot, up_cot, own_gains
    )
    first_record = second_record = None
    gains = None
    for step in range(sections):
        last = step == sections - 1
        pieces, partly = gathered(packed if step == 0 else state)
        if step == 0:
            weights = load_call(section_weights, partly)
        result = section_call(
            scalars_at(step),
            weights,
            pieces,
            state,
            gains,
            grad if last else None,
            None,
            offsets,
            send_order,
            wide,
            step == 0,
        )
        u, stat, z, y = result[:4]
        if step == 0:
            gains = result[4]
        record = (state, pieces[:, :tokens] if sections > 2 else pieces, u, stat, z, y)
        if step < middle:
            first_record = keep_live(live_at(step), record, first_record)
        else:
            second_record = keep_live(live_at(step), record, second_record)
        if last:
            dz, sent = result[-2:]
        else:
            state = moved(y, step, step + 1)
    u_a, y_a = first_record[2], first_record[5]
    u_b, y_b = second_record[2], second_record[5]
    y_other = swapped(y_b)
    down_out = jnp.where(lower, y_a, y_other)
    up_out = jnp.where(lower, y_other, y_a)
    u_first = jnp.where(lower, u_a[:, :half], u_b[:, :half])
    u_second = jnp.where(lower, u_b[:, half:], u_a[:, half:])
    other_first = swapped(jnp.where(lower, u_b[:, :half], u_a[:, :half]))
    other_second = swapped(jnp.where(lower, u_a[:, half:], u_b[:, half:]))
    dz_a = dz_b = gain_b = gain_a = None
    for step in reversed(range(1, sections)):
        source, _, _, stat, z, _ = second_record if step >= middle else first_record
        if step < sections - 1:
            dz, sent = section_call(
                scalars_at(step),
                weights,
                None,
                None,
                gains,
                grad,
                z,
                offsets,
                send_order,
                wide,
                False,
            )
        parts = reduced(sent)
        gain_row = lax.dynamic_slice_in_dim(own_gains, index_at(step), 1, axis=0)
        if step >= middle:
            dz_b = keep_live(live_at(step), dz, dz_b)
        else:
            dz_a = keep_live(live_at(step), dz, dz_a)
        finish = None
        if sections == 2 and not merged:
            finish = (parts, (source, stat, gain_row))
        else:
            du, first, second = finished(parts)
            new_grad, gain_grad = input_gradient(
                du,
                first,
                second,
                grad,
                source,
                stat[:, 0:1],
                stat[:, 1:2],
                gain_row,
                model_width,
            )
            if step >= middle:
                gain_b = keep_live(live_at(step), gain_grad, gain_b)
            else:
                gain_a = keep_live(live_at(step), gain_grad, gain_a)
            grad = moved(new_grad, step, step - 1)
    _, pieces, _, stat, z, _ = first_record
    first_size = len(back_groups[0]) + 1
    result = last_call(
        scalars_at(0),
        weights,
        pieces,
        stat,
        z,
        grad,
        finish,
        offsets,
        send_order,
        wide,
        first_size,
    )
    dz, gain_parts = result[0], result[1 : 1 + first_size]
    if finish is not None:
        gain_b = result[-1]
    dz_a = keep_live(live_at(0), dz, dz_a)
    dz_a_other = swapped(dz_a)
    dz_b_other = swapped(dz_b)
    dz_all = (dz_a, dz_a_other, dz_b, dz_b_other)
    grads = []
    halves = [(True, u_first, other_first), (False, u_second, other_second)]
    for n, group in enumerate(back_groups):
        if n:
            gain_parts = gain_parts.reshape((len(group) + 1, -1) + gain_parts.shape[1:])
        parts = reduce_round(gain_parts, group)
        if halves:
            first, mine, theirs = halves.pop(0)
            grad_half, token = weight_grad_call(
                scalars_at(0), first, *dz_all, mine, theirs, parts[0]
            )
            grads.append(grad_half)
            parts.append(token)
        gain_parts = functools.reduce(jnp.add, parts)
    for first, mine, theirs in halves:
        grads.append(weight_grad_call(scalars_at(0), first, *dz_all, mine, theirs, token)[0])
    grad_first, grad_second = grads
    gain = gain_parts.reshape(1, wide)
    for bit in reversed(range(merged)):
        mine, theirs = own_part(gain, gain.shape[1] // 2, bit)
        gain = mine + from_xor(theirs, 1 << bit)
    gain_a = keep_live(live_at(0), gain, gain_a)
    gain_other = swapped(jnp.where(lower, gain_b, gain_a))
    gain_total = jnp.where(lower, gain_a, gain_b) + gain_other
    return (
        down_out[None],
        up_out[None],
        grad_first[None],
        grad_second[None],
        gain_total,
    )


def solution(mesh):
    in_specs = (
        P(None, "seq"),
        P(None, "seq"),
        P(None, "seq"),
        P(None, "seq"),
        P("section", None, "seq", None),
        P("section", None, "seq"),
    )
    out_specs = (
        P("section", None, "seq"),
        P("section", None, "seq"),
        P("section", "seq", None),
        P("section", "seq", None),
        P("section", "seq"),
    )
    return jax.shard_map(
        per_device, mesh=mesh, in_specs=in_specs, out_specs=out_specs, check_vma=False
    )
```

```python
import functools
import math

import jax
import jax.numpy as jnp
from jax import lax
from jax.experimental import pallas as pl
from jax.experimental.pallas import tpu as pltpu
from jax.sharding import PartitionSpec as P

EPS = 1e-05
F32 = jnp.float32
BF16 = jnp.bfloat16
LANES = 128
PAD_ROWS = 8
SQRT_HALF = math.sqrt(0.5)
INV_SQRT_2PI = 1.0 / math.sqrt(2.0 * math.pi)
VMEM_LIMIT = 32 * 1024 * 1024

VMEM = pl.BlockSpec(memory_space=pltpu.VMEM)
HBM = pl.BlockSpec(memory_space=pltpu.HBM)
ANY = pl.BlockSpec(memory_space=pl.ANY)
SMEM = pl.BlockSpec(memory_space=pltpu.SMEM)


def from_xor(value, distance):
    size = lax.axis_size("seq")
    return lax.ppermute(value, "seq", [(i, i ^ distance) for i in range(size)])


def swapped(value):
    size = lax.axis_size("section")
    return lax.ppermute(value, "section", [(i, size - 1 - i) for i in range(size)])


def bit_groups(low, count):
    bits = [1 << b for b in range(low, count)][::-1]
    groups = []
    while bits:
        pair, bits = bits[:2], bits[2:]
        groups.append(tuple(pair) if len(pair) == 1 else (pair[0], pair[1], pair[0] ^ pair[1]))
    groups[0] = groups[0][::-1]
    return groups


def offsets_of(groups):
    offsets = [0]
    for group in groups:
        offsets = [o ^ d for d in (0,) + group for o in offsets]
    return offsets


def gather_xor(block, groups):
    held = block[None]
    for n, group in enumerate(groups):
        if n <= 1:
            early = held
        held = jnp.concatenate([held] + [from_xor(held, d) for d in group], axis=0)
    return held, early


def reduce_round(held, group):
    sent = [from_xor(held[n + 1], d) for n, d in enumerate(group)]
    return [held[0]] + sent


def in_hbm(value):
    return pltpu.with_memory_space_constraint(value, pltpu.HBM)


def gelu_and_slope(z):
    cdf = 0.5 * (1.0 + lax.erf(z * SQRT_HALF))
    slope = cdf + z * (jnp.exp(-0.5 * z * z) * INV_SQRT_2PI)
    return z * cdf, slope


def column_to_row(column):
    tokens = column.shape[0]
    rows = lax.broadcasted_iota(jnp.int32, (tokens, LANES), 0)
    lanes = lax.broadcasted_iota(jnp.int32, (tokens, LANES), 1)
    return jnp.sum(jnp.where(rows == lanes, column, 0.0), axis=0, keepdims=True)


def row_to_column(row, tokens):
    rows = lax.broadcasted_iota(jnp.int32, (tokens, LANES), 0)
    lanes = lax.broadcasted_iota(jnp.int32, (tokens, LANES), 1)
    return jnp.sum(jnp.where(rows == lanes, row, 0.0), axis=1, keepdims=True)


def two_terms(value):
    high = value.astype(BF16)
    return high, (value - high.astype(F32)).astype(BF16)


def three_terms(value):
    high, rest = value.astype(BF16), None
    rest = value - high.astype(F32)
    middle = rest.astype(BF16)
    return high, middle, (rest - middle.astype(F32)).astype(BF16)


def sums_block(first_sum, second_sum):
    row = lax.broadcasted_iota(jnp.int32, (PAD_ROWS, LANES), 0)
    block = jnp.zeros((PAD_ROWS, LANES), F32)
    n = 0
    for column in (first_sum, second_sum):
        for term in two_terms(column_to_row(column)):
            block = jnp.where(row == n, term.astype(F32), block)
            n += 1
    return block.astype(BF16)


def split_packed(total, tokens, width):
    chunks = width // LANES
    du = jnp.concatenate([total[c * tokens : (c + 1) * tokens] for c in range(chunks)], axis=1)
    tail = total[chunks * tokens : chunks * tokens + PAD_ROWS]
    first = row_to_column(tail[0:1] + tail[1:2], tokens)
    second = row_to_column(tail[2:3] + tail[3:4], tokens)
    return du, first, second


def input_gradient(du, first_sum, second_sum, dy, block, mean, scale, gain, model_width):
    hat = (block.astype(F32) - mean) * scale
    gained = du * gain
    dx = dy.astype(F32) + scale * (
        gained - first_sum / model_width - hat * (second_sum / model_width)
    )
    return dx.astype(BF16), jnp.sum(du * hat, axis=0, keepdims=True)


def section_kernel(offsets, dims, forward, unpack, backward, send_order, *refs):
    tokens, block, model_width = dims
    refs = list(refs)
    take = refs.pop
    scalars = take(0)
    weights = take(0)
    pieces = take(0) if forward else None
    own = take(0) if forward else None
    gains = None if unpack else take(0)
    dy_ref = take(0) if backward else None
    z_ref = None if forward else take(0)
    if forward:
        u_out, stat_out, z_out, y_out = take(0), take(0), take(0), take(0)
    if unpack:
        gains = take(0)
    if backward:
        dz_out, sent_out = take(0), take(0)
    me, windex = scalars[0], scalars[1]
    held = weights.at[0, windex]
    wide = block
    if forward:
        total = jnp.zeros((tokens, LANES), F32)
        squares = jnp.zeros((tokens, LANES), F32)
        for e in range(len(offsets)):
            for c in range(wide // LANES):
                part = pieces[e, 0:tokens, c * LANES : (c + 1) * LANES].astype(F32)
                total = total + part
                squares = squares + part * part
        mean = jnp.sum(total, axis=1, keepdims=True) / model_width
        var = jnp.sum(squares, axis=1, keepdims=True) / model_width - mean * mean
        scale = lax.rsqrt(var + EPS)
        lane = lax.broadcasted_iota(jnp.int32, (tokens, LANES), 1)
        stat_out[...] = jnp.where(lane == 0, mean, scale)
        for e, offset in enumerate(offsets):
            column = pl.multiple_of((me ^ offset) * wide, LANES)
            if unpack:
                terms = pieces[e, tokens : tokens + PAD_ROWS, :].astype(F32)
                gains[0:1, pl.ds(column, wide)] = terms[0:1] + terms[1:2] + terms[2:3]
                gains[1:2, pl.ds(column, wide)] = terms[3:4] + terms[4:5] + terms[5:6]
            gain = gains[pl.ds(windex, 1), pl.ds(column, wide)]
            hat = (pieces[e, 0:tokens, :].astype(F32) - mean) * scale
            u_out[:, pl.ds(column, wide)] = (hat * gain).astype(BF16)
        z = lax.dot_general(
            u_out[...], held[...], (((1,), (1,)), ((), ())), preferred_element_type=F32
        )
        gelu, slope = gelu_and_slope(z)
        z_out[...] = z
        y_out[...] = (own[...].astype(F32) + gelu).astype(BF16)
    if backward:
        if not forward:
            z = z_ref[...]
            gelu, slope = gelu_and_slope(z)
        dz = (dy_ref[...].astype(F32) * slope).astype(BF16)
        dz_out[...] = dz
        second = jnp.sum(dz.astype(F32) * z, axis=1, keepdims=True)
        first = jnp.zeros((tokens, LANES), F32)
        for n, offset in enumerate(send_order):
            column = pl.multiple_of((me ^ offset) * wide, LANES)
            part = jnp.dot(dz, held[:, pl.ds(column, wide)], preferred_element_type=F32)
            gained = part * gains[pl.ds(windex, 1), pl.ds(column, wide)]
            for c in range(wide // LANES):
                first = first + gained[:, c * LANES : (c + 1) * LANES]
                sent_out[n, c * tokens : (c + 1) * tokens, :] = part[
                    :, c * LANES : (c + 1) * LANES
                ].astype(BF16)
        tail = sums_block(jnp.sum(first, axis=1, keepdims=True), second)
        rows = tokens * (wide // LANES)
        for n in range(len(send_order)):
            sent_out[n, rows : rows + PAD_ROWS, :] = tail


def section_call(scalars, weights, pieces, own, gains, dy, z, offsets, send_order, wide, unpack):
    forward, backward = pieces is not None, dy is not None
    rows, model_width = weights.shape[2:]
    tokens = (own if forward else dy).shape[0]
    operands, specs = [scalars, weights], [SMEM, VMEM]
    for value in (pieces, own, gains, dy, z):
        if value is not None:
            operands.append(value)
            specs.append(VMEM)
    outs = []
    if forward:
        outs += [
            jax.ShapeDtypeStruct((tokens, model_width), BF16),
            jax.ShapeDtypeStruct((tokens, LANES), F32),
            jax.ShapeDtypeStruct((tokens, rows), F32),
            jax.ShapeDtypeStruct((tokens, rows), BF16),
        ]
    if unpack:
        outs.append(jax.ShapeDtypeStruct((2, model_width), F32))
    if backward:
        outs += [
            jax.ShapeDtypeStruct((tokens, rows), BF16),
            jax.ShapeDtypeStruct(
                (len(send_order), tokens * (wide // LANES) + PAD_ROWS, LANES), BF16
            ),
        ]
    flops = 2 * tokens * rows * model_width * (int(forward) + int(backward))
    return pl.pallas_call(
        functools.partial(
            section_kernel,
            offsets,
            (tokens, wide, model_width),
            forward,
            unpack,
            backward,
            send_order,
        ),
        out_shape=outs,
        in_specs=specs,
        out_specs=[VMEM] * len(outs),
        compiler_params=pltpu.CompilerParams(vmem_limit_bytes=VMEM_LIMIT),
        cost_estimate=pl.CostEstimate(
            flops=flops, bytes_accessed=2 * rows * model_width, transcendentals=tokens * rows
        ),
    )(*operands)


def last_kernel(offsets, places, dims, part_count, *refs):
    tokens, wide, model_width, first_size = dims
    scalars, weights, pieces, stat, z_ref, dy_ref = refs[:6]
    refs = refs[6:]
    if part_count:
        parts, (block_ref, next_stat, next_gain), refs = (
            refs[:part_count],
            refs[part_count : part_count + 3],
            refs[part_count + 3 :],
        )
        next_gain_out = refs[-1]
    dz_out, gain_out = refs[0], refs[1 : 1 + first_size]
    me, windex = scalars[0], scalars[1]
    held = weights.at[0, windex]
    dy = dy_ref[...]
    if part_count:
        total = parts[0][...]
        for part in parts[1:]:
            total = total + part[...].astype(F32)
        du, first, second = split_packed(total, tokens, wide)
        dy, gain_grad = input_gradient(
            du,
            first,
            second,
            dy,
            block_ref[...],
            next_stat[:, 0:1],
            next_stat[:, 1:2],
            next_gain[...],
            model_width,
        )
        next_gain_out[...] = gain_grad
    slope = gelu_and_slope(z_ref[...])[1]
    dz = (dy.astype(F32) * slope).astype(BF16)
    dz_out[...] = dz
    mean, scale = stat[:, 0:1], stat[:, 1:2]
    for e, offset in enumerate(offsets):
        column = pl.multiple_of((me ^ offset) * wide, LANES)
        part = jnp.dot(dz, held[:, pl.ds(column, wide)], preferred_element_type=F32)
        hat = (pieces[e, 0:tokens, :].astype(F32) - mean) * scale
        a, b = places[e]
        gain_out[a][b : b + 1, :] = jnp.sum(part * hat, axis=0, keepdims=True)


def last_call(scalars, weights, pieces, stat, z, dy, finish, offsets, send_order, wide, first_size):
    rows, model_width = weights.shape[2:]
    tokens = dy.shape[0]
    rest = len(offsets) // first_size
    places = [divmod(send_order.index(o), rest) for o in offsets]
    operands = [scalars, weights, pieces, stat, z, dy]
    outs = [
        jax.ShapeDtypeStruct((tokens, rows), BF16),
    ] + [jax.ShapeDtypeStruct((rest, wide), F32)] * first_size
    part_count = 0
    if finish is not None:
        parts, others = finish
        part_count = len(parts)
        operands += list(parts) + list(others)
        outs.append(jax.ShapeDtypeStruct((1, rows), F32))
    return pl.pallas_call(
        functools.partial(
            last_kernel,
            offsets,
            places,
            (tokens, wide, model_width, first_size),
            part_count,
        ),
        out_shape=outs,
        in_specs=[SMEM] + [VMEM] * (len(operands) - 1),
        out_specs=[VMEM] * len(outs),
        compiler_params=pltpu.CompilerParams(vmem_limit_bytes=VMEM_LIMIT),
        cost_estimate=pl.CostEstimate(
            flops=2 * tokens * rows * model_width,
            bytes_accessed=2 * rows * model_width,
            transcendentals=tokens * rows,
        ),
    )(*operands)


def weight_grad_kernel(first_at, tiles, kept, *refs):
    scalars, dz_own, dz_other, u_own, u_other, _ = refs[:6]
    first, second, order, result, sems = refs[6 + kept :]
    tile = u_own.shape[1] // tiles
    depth = jnp.concatenate([dz_own[...], dz_other[...]], axis=0).T
    order[...] = jnp.zeros_like(order)

    def copy(n, target):
        columns = pl.ds(n * tile, tile)
        return pltpu.make_async_copy(result.at[:, columns], target.at[:, columns], sems.at[n])

    for n in range(tiles):
        columns = slice(n * tile, (n + 1) * tile)
        both = jnp.concatenate([u_own[:, columns], u_other[:, columns]], axis=0)
        result[:, columns] = jnp.dot(depth, both, preferred_element_type=F32)

        @pl.when(scalars[1] == first_at)
        def _():
            copy(n, first).start()

        @pl.when(scalars[1] != first_at)
        def _():
            copy(n, second).start()

    for n in range(tiles):
        copy(n, first).wait()


def weight_grad_call(scalars, first_at, dz_own, dz_other, u_own, u_other, after, kept):
    tokens, rows = dz_own.shape
    columns = u_own.shape[1]
    tiles = 4
    return pl.pallas_call(
        functools.partial(weight_grad_kernel, first_at, tiles, len(kept)),
        out_shape=[
            jax.ShapeDtypeStruct((rows, columns), F32),
            jax.ShapeDtypeStruct((rows, columns), F32),
            jax.ShapeDtypeStruct(after.shape, F32),
        ],
        in_specs=[SMEM] + [VMEM] * 5 + [HBM] * len(kept),
        out_specs=[HBM, HBM, VMEM],
        input_output_aliases={6 + n: n for n in range(len(kept))},
        scratch_shapes=[pltpu.VMEM((rows, columns), F32), pltpu.SemaphoreType.DMA((tiles,))],
        compiler_params=pltpu.CompilerParams(vmem_limit_bytes=VMEM_LIMIT),
        cost_estimate=pl.CostEstimate(
            flops=4 * tokens * rows * columns, bytes_accessed=4 * rows * columns, transcendentals=0
        ),
    )(scalars, dz_own, dz_other, u_own, u_other, after, *kept)


def load_kernel(weights, _, held, sems):
    copies = [
        pltpu.make_async_copy(weights.at[0, n], held.at[0, n], sems.at[n]) for n in range(2)
    ]
    for copy in copies:
        copy.start()
    for copy in copies:
        copy.wait()


def load_call(weights, after):
    return pl.pallas_call(
        load_kernel,
        out_shape=jax.ShapeDtypeStruct(weights.shape, weights.dtype),
        in_specs=[HBM, ANY],
        out_specs=VMEM,
        scratch_shapes=[pltpu.SemaphoreType.DMA((2,))],
        compiler_params=pltpu.CompilerParams(vmem_limit_bytes=VMEM_LIMIT),
        cost_estimate=pl.CostEstimate(
            flops=0, bytes_accessed=2 * weights.size, transcendentals=0
        ),
    )(in_hbm(weights), after)


def pack_kernel(scalars, *refs):
    sources, gains_source, (state, cot, payload), gains, sems = (
        refs[:4],
        refs[4],
        refs[5:8],
        refs[8],
        refs[9],
    )
    tokens = state.shape[0]
    gains_copy = pltpu.make_async_copy(gains_source, gains, sems.at[0])
    gains_copy.start()
    for n in range(2):

        @pl.when(scalars[1] == n)
        def _():
            pltpu.make_async_copy(sources[n], state, sems.at[1]).start()
            pltpu.make_async_copy(sources[2 + n], cot, sems.at[2]).start()

    gains_copy.wait()
    row = lax.broadcasted_iota(jnp.int32, (PAD_ROWS, state.shape[1]), 0)
    block = jnp.zeros((PAD_ROWS, state.shape[1]), F32)
    n = 0
    for section in range(2):
        for term in three_terms(gains[section : section + 1, :]):
            block = jnp.where(row == n, term.astype(F32), block)
            n += 1
    payload[tokens:] = block.astype(BF16)
    pltpu.make_async_copy(sources[0], state, sems.at[1]).wait()
    payload[0:tokens] = state[...]
    pltpu.make_async_copy(sources[2], cot, sems.at[2]).wait()


def pack_call(scalars, down_input, up_input, down_cot, up_cot, gains):
    tokens, block = down_input.shape
    return pl.pallas_call(
        pack_kernel,
        out_shape=[
            jax.ShapeDtypeStruct((tokens, block), BF16),
            jax.ShapeDtypeStruct((tokens, block), BF16),
            jax.ShapeDtypeStruct((tokens + PAD_ROWS, block), BF16),
        ],
        in_specs=[SMEM] + [HBM] * 5,
        out_specs=[VMEM] * 3,
        scratch_shapes=[pltpu.VMEM(gains.shape, F32), pltpu.SemaphoreType.DMA((3,))],
        compiler_params=pltpu.CompilerParams(vmem_limit_bytes=VMEM_LIMIT),
    )(scalars, *map(in_hbm, (down_input, up_input, down_cot, up_cot, gains)))


def keep_live(live, record, previous):
    if previous is None or live is None:
        return record
    return jax.tree.map(lambda fresh, older: jnp.where(live, fresh, older), record, previous)


def per_device(down_input, up_input, down_cot, up_cot, section_weights, section_gains):
    sections = lax.axis_size("section")
    middle = sections // 2
    position = lax.axis_index("section")
    seq_size = lax.axis_size("seq")
    seq_index = lax.axis_index("seq")
    lower = position < middle
    tokens, block = down_input.shape
    model_width = section_weights.shape[3]
    half = model_width // 2
    merged = 0
    while (block << merged) % LANES:
        merged += 1
    wide = block << merged
    bit_count = seq_size.bit_length() - 1
    groups = bit_groups(merged, bit_count)
    back_groups = [group[::-1] for group in groups[:0:-1]] + groups[:1]
    offsets = [o >> merged for o in offsets_of(groups)]
    send_order = [o >> merged for o in offsets_of(back_groups[::-1])]
    me = (seq_index >> merged).astype(jnp.int32)
    first_index = jnp.where(lower, 0, 1).astype(jnp.int32)
    turn = jnp.minimum(position, sections - 1 - position)

    def index_at(step):
        return first_index if step < middle else 1 - first_index

    def scalars_at(step):
        return jnp.stack([me, index_at(step)]).astype(jnp.int32)

    def live_at(step):
        if sections == 2:
            return None
        return turn == min(step, sections - 1 - step)

    def joined_halves(value, axis):
        for bit in range(merged):
            other = from_xor(value, 1 << bit)
            upper = (seq_index >> bit) & 1
            value = jnp.where(
                upper == 1,
                jnp.concatenate([other, value], axis=axis),
                jnp.concatenate([value, other], axis=axis),
            )
        return value

    def own_part(value, width, bit):
        start = ((seq_index >> bit) & 1) * width
        return (
            lax.dynamic_slice_in_dim(value, start, width, axis=1),
            lax.dynamic_slice_in_dim(value, width - start, width, axis=1),
        )

    def gathered(value):
        return gather_xor(joined_halves(value, 1), groups)

    def moved(value, step, later):
        low = min(step, sections - 1 - step)
        new = min(later, sections - 1 - later)
        if low == new:
            return value
        route = [(low, new), (sections - 1 - low, sections - 1 - new)]
        return lax.ppermute(value, "section", route)

    def reduced(sent, beside=None):
        parts = grads = None
        for n, group in enumerate(back_groups):
            sent = sent.reshape((len(group) + 1, -1) + sent.shape[1:])
            parts = reduce_round(sent, group)
            if n + 1 < len(back_groups):
                if n == 0 and beside is not None:
                    parts, grads = lax.optimization_barrier((parts, beside()))
                total = functools.reduce(jnp.add, [p.astype(F32) for p in parts])
                sent = total.astype(BF16)
                kept = total[0]
        parts = [kept if len(back_groups) > 1 else parts[0][0].astype(F32)] + [
            p[0] for p in parts[1:]
        ]
        return parts, grads

    def finished(parts):
        total = functools.reduce(jnp.add, [p.astype(F32) for p in parts])
        du, first, second = split_packed(total, tokens, wide)
        for bit in reversed(range(merged)):
            width = du.shape[1] // 2
            mine, theirs = own_part(du, width, bit)
            tail = jnp.concatenate(two_terms(first) + two_terms(second), axis=1)
            message = jnp.concatenate([theirs.astype(BF16), tail], axis=1)
            message = from_xor(message, 1 << bit).astype(F32)
            du = mine + message[:, :width]
            first = first + message[:, width : width + 1] + message[:, width + 1 : width + 2]
            second = second + message[:, width + 2 : width + 3] + message[:, width + 3 :]
        return du, first, second

    own_gains = section_gains[0]
    state, grad, packed = pack_call(
        scalars_at(0), down_input, up_input, down_cot, up_cot, own_gains
    )
    first_record = second_record = None
    gains = None
    for step in range(sections):
        last = step == sections - 1
        pieces, partly = gathered(packed if step == 0 else state)
        if step == 0:
            weights = load_call(section_weights, partly)
        result = section_call(
            scalars_at(step),
            weights,
            pieces,
            state,
            gains,
            grad if last else None,
            None,
            offsets,
            send_order,
            wide,
            step == 0,
        )
        u, stat, z, y = result[:4]
        if step == 0:
            gains = result[4]
        record = (state, pieces[:, :tokens] if sections > 2 else pieces, u, stat, z, y)
        if step < middle:
            first_record = keep_live(live_at(step), record, first_record)
        else:
            second_record = keep_live(live_at(step), record, second_record)
        if last:
            dz, sent = result[-2:]
        else:
            state = moved(y, step, step + 1)
    u_a, y_a = first_record[2], first_record[5]
    u_b, y_b = second_record[2], second_record[5]
    y_other = swapped(y_b)
    down_out = jnp.where(lower, y_a, y_other)
    up_out = jnp.where(lower, y_other, y_a)
    needed_a = jnp.where(lower, u_a[:, :half], u_a[:, half:])
    needed_b = jnp.where(lower, u_b[:, half:], u_b[:, :half])
    other_a = swapped(jnp.where(lower, u_a[:, half:], u_a[:, :half]))
    other_b = swapped(jnp.where(lower, u_b[:, :half], u_b[:, half:]))
    dz_a = dz_b = gain_b = gain_a = None
    for step in reversed(range(1, sections)):
        source, _, _, stat, z, _ = second_record if step >= middle else first_record
        if step < sections - 1:
            dz, sent = section_call(
                scalars_at(step),
                weights,
                None,
                None,
                gains,
                grad,
                z,
                offsets,
                send_order,
                wide,
                False,
            )
        gain_row = lax.dynamic_slice_in_dim(own_gains, index_at(step), 1, axis=0)
        if step >= middle:
            dz_b = keep_live(live_at(step), dz, dz_b)
        else:
            dz_a = keep_live(live_at(step), dz, dz_a)
        beside = None
        if step == middle:
            beside = functools.partial(
                weight_grad_call,
                scalars_at(0),
                1,
                dz_b,
                swapped(dz_b),
                needed_b,
                other_b,
                jnp.zeros((8, LANES)),
                (),
            )
        parts, grads = reduced(sent, beside)
        if grads is not None:
            early_grads = grads[:2]
        finish = None
        if sections == 2 and not merged:
            finish = (parts, (source, stat, gain_row))
        else:
            du, first, second = finished(parts)
            new_grad, gain_grad = input_gradient(
                du,
                first,
                second,
                grad,
                source,
                stat[:, 0:1],
                stat[:, 1:2],
                gain_row,
                model_width,
            )
            if step >= middle:
                gain_b = keep_live(live_at(step), gain_grad, gain_b)
            else:
                gain_a = keep_live(live_at(step), gain_grad, gain_a)
            grad = moved(new_grad, step, step - 1)
    _, pieces, _, stat, z, _ = first_record
    first_size = len(back_groups[0]) + 1
    result = last_call(
        scalars_at(0),
        weights,
        pieces,
        stat,
        z,
        grad,
        finish,
        offsets,
        send_order,
        wide,
        first_size,
    )
    dz, gain_parts = result[0], result[1 : 1 + first_size]
    if finish is not None:
        gain_b = result[-1]
    dz_a = keep_live(live_at(0), dz, dz_a)
    dz_a_other = swapped(dz_a)
    for n, group in enumerate(back_groups):
        if n:
            gain_parts = gain_parts.reshape((len(group) + 1, -1) + gain_parts.shape[1:])
        parts = reduce_round(gain_parts, group)
        if n == 0:
            grad_first, grad_second, token = weight_grad_call(
                scalars_at(0), 0, dz_a, dz_a_other, needed_a, other_a, parts[0], early_grads
            )
            parts.append(token)
        gain_parts = functools.reduce(jnp.add, parts)
    gain = gain_parts.reshape(1, wide)
    for bit in reversed(range(merged)):
        mine, theirs = own_part(gain, gain.shape[1] // 2, bit)
        gain = mine + from_xor(theirs, 1 << bit)
    gain_a = keep_live(live_at(0), gain, gain_a)
    gain_other = swapped(jnp.where(lower, gain_b, gain_a))
    gain_total = jnp.where(lower, gain_a, gain_b) + gain_other
    return (
        down_out[None],
        up_out[None],
        grad_first[None],
        grad_second[None],
        gain_total,
    )


def solution(mesh):
    in_specs = (
        P(None, "seq"),
        P(None, "seq"),
        P(None, "seq"),
        P(None, "seq"),
        P("section", None, "seq", None),
        P("section", None, "seq"),
    )
    out_specs = (
        P("section", None, "seq"),
        P("section", None, "seq"),
        P("section", "seq", None),
        P("section", "seq", None),
        P("section", "seq"),
    )
    return jax.shard_map(
        per_device, mesh=mesh, in_specs=in_specs, out_specs=out_specs, check_vma=False
    )
```

```python
import functools
import math

import jax
import jax.numpy as jnp
from jax import lax
from jax.experimental import pallas as pl
from jax.experimental.pallas import tpu as pltpu
from jax.sharding import PartitionSpec as P

EPS = 1e-05
F32 = jnp.float32
BF16 = jnp.bfloat16
LANES = 128
PAD_ROWS = 8
SQRT_HALF = math.sqrt(0.5)
INV_SQRT_2PI = 1.0 / math.sqrt(2.0 * math.pi)
VMEM_LIMIT = 32 * 1024 * 1024

VMEM = pl.BlockSpec(memory_space=pltpu.VMEM)
HBM = pl.BlockSpec(memory_space=pltpu.HBM)
ANY = pl.BlockSpec(memory_space=pl.ANY)
SMEM = pl.BlockSpec(memory_space=pltpu.SMEM)


def from_xor(value, distance):
    size = lax.axis_size("seq")
    return lax.ppermute(value, "seq", [(i, i ^ distance) for i in range(size)])


def swapped(value):
    size = lax.axis_size("section")
    return lax.ppermute(value, "section", [(i, size - 1 - i) for i in range(size)])


def bit_groups(low, count):
    bits = [1 << b for b in range(low, count)][::-1]
    groups = []
    while bits:
        pair, bits = bits[:2], bits[2:]
        groups.append(tuple(pair) if len(pair) == 1 else (pair[0], pair[1], pair[0] ^ pair[1]))
    groups[0] = groups[0][::-1]
    return groups


def offsets_of(groups):
    offsets = [0]
    for group in groups:
        offsets = [o ^ d for d in (0,) + group for o in offsets]
    return offsets


def gather_xor(block, groups):
    held = block[None]
    for n, group in enumerate(groups):
        if n <= 1:
            early = held
        held = jnp.concatenate([held] + [from_xor(held, d) for d in group], axis=0)
    return held, early


def reduce_round(held, group):
    sent = [from_xor(held[n + 1], d) for n, d in enumerate(group)]
    return [held[0]] + sent


def in_hbm(value):
    return pltpu.with_memory_space_constraint(value, pltpu.HBM)


def gelu_and_slope(z):
    cdf = 0.5 * (1.0 + lax.erf(z * SQRT_HALF))
    slope = cdf + z * (jnp.exp(-0.5 * z * z) * INV_SQRT_2PI)
    return z * cdf, slope


def column_to_row(column):
    tokens = column.shape[0]
    rows = lax.broadcasted_iota(jnp.int32, (tokens, LANES), 0)
    lanes = lax.broadcasted_iota(jnp.int32, (tokens, LANES), 1)
    return jnp.sum(jnp.where(rows == lanes, column, 0.0), axis=0, keepdims=True)


def row_to_column(row, tokens):
    rows = lax.broadcasted_iota(jnp.int32, (tokens, LANES), 0)
    lanes = lax.broadcasted_iota(jnp.int32, (tokens, LANES), 1)
    return jnp.sum(jnp.where(rows == lanes, row, 0.0), axis=1, keepdims=True)


def two_terms(value):
    high = value.astype(BF16)
    return high, (value - high.astype(F32)).astype(BF16)


def three_terms(value):
    high, rest = value.astype(BF16), None
    rest = value - high.astype(F32)
    middle = rest.astype(BF16)
    return high, middle, (rest - middle.astype(F32)).astype(BF16)


def sums_block(first_sum, second_sum):
    row = lax.broadcasted_iota(jnp.int32, (PAD_ROWS, LANES), 0)
    block = jnp.zeros((PAD_ROWS, LANES), F32)
    n = 0
    for column in (first_sum, second_sum):
        for term in two_terms(column_to_row(column)):
            block = jnp.where(row == n, term.astype(F32), block)
            n += 1
    return block.astype(BF16)


def split_packed(total, tokens, width):
    chunks = width // LANES
    du = jnp.concatenate([total[c * tokens : (c + 1) * tokens] for c in range(chunks)], axis=1)
    tail = total[chunks * tokens : chunks * tokens + PAD_ROWS]
    first = row_to_column(tail[0:1] + tail[1:2], tokens)
    second = row_to_column(tail[2:3] + tail[3:4], tokens)
    return du, first, second


def input_gradient(du, first_sum, second_sum, dy, block, mean, scale, gain, model_width):
    hat = (block.astype(F32) - mean) * scale
    gained = du * gain
    dx = dy.astype(F32) + scale * (
        gained - first_sum / model_width - hat * (second_sum / model_width)
    )
    return dx.astype(BF16), jnp.sum(du * hat, axis=0, keepdims=True)


def section_kernel(offsets, dims, forward, unpack, backward, send_order, *refs):
    tokens, block, model_width = dims
    refs = list(refs)
    take = refs.pop
    scalars = take(0)
    weights = take(0)
    pieces = take(0) if forward else None
    own = take(0) if forward else None
    gains = None if unpack else take(0)
    dy_ref = take(0) if backward else None
    z_ref = None if forward else take(0)
    if forward:
        u_out, stat_out, z_out, y_out = take(0), take(0), take(0), take(0)
    if unpack:
        gains = take(0)
    if backward:
        dz_out, sent_out = take(0), take(0)
    me, windex = scalars[0], scalars[1]
    held = weights.at[0, windex]
    wide = block
    if forward:
        total = jnp.zeros((tokens, LANES), F32)
        squares = jnp.zeros((tokens, LANES), F32)
        for e in range(len(offsets)):
            for c in range(wide // LANES):
                part = pieces[e, 0:tokens, c * LANES : (c + 1) * LANES].astype(F32)
                total = total + part
                squares = squares + part * part
        mean = jnp.sum(total, axis=1, keepdims=True) / model_width
        var = jnp.sum(squares, axis=1, keepdims=True) / model_width - mean * mean
        scale = lax.rsqrt(var + EPS)
        lane = lax.broadcasted_iota(jnp.int32, (tokens, LANES), 1)
        stat_out[...] = jnp.where(lane == 0, mean, scale)
        for e, offset in enumerate(offsets):
            column = pl.multiple_of((me ^ offset) * wide, LANES)
            if unpack:
                terms = pieces[e, tokens : tokens + PAD_ROWS, :].astype(F32)
                gains[0:1, pl.ds(column, wide)] = terms[0:1] + terms[1:2] + terms[2:3]
                gains[1:2, pl.ds(column, wide)] = terms[3:4] + terms[4:5] + terms[5:6]
            gain = gains[pl.ds(windex, 1), pl.ds(column, wide)]
            hat = (pieces[e, 0:tokens, :].astype(F32) - mean) * scale
            u_out[:, pl.ds(column, wide)] = (hat * gain).astype(BF16)
        z = lax.dot_general(
            u_out[...], held[...], (((1,), (1,)), ((), ())), preferred_element_type=F32
        )
        gelu, slope = gelu_and_slope(z)
        z_out[...] = z
        y_out[...] = (own[...].astype(F32) + gelu).astype(BF16)
    if backward:
        if not forward:
            z = z_ref[...]
            gelu, slope = gelu_and_slope(z)
        dz = (dy_ref[...].astype(F32) * slope).astype(BF16)
        dz_out[...] = dz
        second = jnp.sum(dz.astype(F32) * z, axis=1, keepdims=True)
        first = jnp.zeros((tokens, LANES), F32)
        for n, offset in enumerate(send_order):
            column = pl.multiple_of((me ^ offset) * wide, LANES)
            part = jnp.dot(dz, held[:, pl.ds(column, wide)], preferred_element_type=F32)
            gained = part * gains[pl.ds(windex, 1), pl.ds(column, wide)]
            for c in range(wide // LANES):
                first = first + gained[:, c * LANES : (c + 1) * LANES]
                sent_out[n, c * tokens : (c + 1) * tokens, :] = part[
                    :, c * LANES : (c + 1) * LANES
                ].astype(BF16)
        tail = sums_block(jnp.sum(first, axis=1, keepdims=True), second)
        rows = tokens * (wide // LANES)
        for n in range(len(send_order)):
            sent_out[n, rows : rows + PAD_ROWS, :] = tail


def section_call(scalars, weights, pieces, own, gains, dy, z, offsets, send_order, wide, unpack):
    forward, backward = pieces is not None, dy is not None
    rows, model_width = weights.shape[2:]
    tokens = (own if forward else dy).shape[0]
    operands, specs = [scalars, weights], [SMEM, VMEM]
    for value in (pieces, own, gains, dy, z):
        if value is not None:
            operands.append(value)
            specs.append(VMEM)
    outs = []
    if forward:
        outs += [
            jax.ShapeDtypeStruct((tokens, model_width), BF16),
            jax.ShapeDtypeStruct((tokens, LANES), F32),
            jax.ShapeDtypeStruct((tokens, rows), F32),
            jax.ShapeDtypeStruct((tokens, rows), BF16),
        ]
    if unpack:
        outs.append(jax.ShapeDtypeStruct((2, model_width), F32))
    if backward:
        outs += [
            jax.ShapeDtypeStruct((tokens, rows), BF16),
            jax.ShapeDtypeStruct(
                (len(send_order), tokens * (wide // LANES) + PAD_ROWS, LANES), BF16
            ),
        ]
    flops = 2 * tokens * rows * model_width * (int(forward) + int(backward))
    return pl.pallas_call(
        functools.partial(
            section_kernel,
            offsets,
            (tokens, wide, model_width),
            forward,
            unpack,
            backward,
            send_order,
        ),
        out_shape=outs,
        in_specs=specs,
        out_specs=[VMEM] * len(outs),
        compiler_params=pltpu.CompilerParams(vmem_limit_bytes=VMEM_LIMIT),
        cost_estimate=pl.CostEstimate(
            flops=flops, bytes_accessed=2 * rows * model_width, transcendentals=tokens * rows
        ),
    )(*operands)


def last_kernel(offsets, places, dims, part_count, *refs):
    tokens, wide, model_width, first_size = dims
    scalars, weights, pieces, stat, z_ref, dy_ref = refs[:6]
    refs = refs[6:]
    if part_count:
        parts, (block_ref, next_stat, next_gain), refs = (
            refs[:part_count],
            refs[part_count : part_count + 3],
            refs[part_count + 3 :],
        )
        next_gain_out = refs[-1]
    dz_out, gain_out = refs[0], refs[1 : 1 + first_size]
    me, windex = scalars[0], scalars[1]
    held = weights.at[0, windex]
    dy = dy_ref[...]
    if part_count:
        total = parts[0][...]
        for part in parts[1:]:
            total = total + part[...].astype(F32)
        du, first, second = split_packed(total, tokens, wide)
        dy, gain_grad = input_gradient(
            du,
            first,
            second,
            dy,
            block_ref[...],
            next_stat[:, 0:1],
            next_stat[:, 1:2],
            next_gain[...],
            model_width,
        )
        next_gain_out[...] = gain_grad
    slope = gelu_and_slope(z_ref[...])[1]
    dz = (dy.astype(F32) * slope).astype(BF16)
    dz_out[...] = dz
    mean, scale = stat[:, 0:1], stat[:, 1:2]
    for e, offset in enumerate(offsets):
        column = pl.multiple_of((me ^ offset) * wide, LANES)
        part = jnp.dot(dz, held[:, pl.ds(column, wide)], preferred_element_type=F32)
        hat = (pieces[e, 0:tokens, :].astype(F32) - mean) * scale
        a, b = places[e]
        gain_out[a][b : b + 1, :] = jnp.sum(part * hat, axis=0, keepdims=True)


def last_call(scalars, weights, pieces, stat, z, dy, finish, offsets, send_order, wide, first_size):
    rows, model_width = weights.shape[2:]
    tokens = dy.shape[0]
    rest = len(offsets) // first_size
    places = [divmod(send_order.index(o), rest) for o in offsets]
    operands = [scalars, weights, pieces, stat, z, dy]
    outs = [
        jax.ShapeDtypeStruct((tokens, rows), BF16),
    ] + [jax.ShapeDtypeStruct((rest, wide), F32)] * first_size
    part_count = 0
    if finish is not None:
        parts, others = finish
        part_count = len(parts)
        operands += list(parts) + list(others)
        outs.append(jax.ShapeDtypeStruct((1, rows), F32))
    return pl.pallas_call(
        functools.partial(
            last_kernel,
            offsets,
            places,
            (tokens, wide, model_width, first_size),
            part_count,
        ),
        out_shape=outs,
        in_specs=[SMEM] + [VMEM] * (len(operands) - 1),
        out_specs=[VMEM] * len(outs),
        compiler_params=pltpu.CompilerParams(vmem_limit_bytes=VMEM_LIMIT),
        cost_estimate=pl.CostEstimate(
            flops=2 * tokens * rows * model_width,
            bytes_accessed=2 * rows * model_width,
            transcendentals=tokens * rows,
        ),
    )(*operands)


def weight_grad_kernel(first_at, tiles, kept, *refs):
    scalars, dz_own, dz_other, u_own, u_other, _ = refs[:6]
    first, second, order, result, sems = refs[6 + kept :]
    tile = u_own.shape[1] // tiles
    depth = jnp.concatenate([dz_own[...], dz_other[...]], axis=0).T
    order[...] = jnp.zeros_like(order)

    def copy(n, target):
        columns = pl.ds(n * tile, tile)
        return pltpu.make_async_copy(result.at[:, columns], target.at[:, columns], sems.at[n])

    for n in range(tiles):
        columns = slice(n * tile, (n + 1) * tile)
        both = jnp.concatenate([u_own[:, columns], u_other[:, columns]], axis=0)
        result[:, columns] = jnp.dot(depth, both, preferred_element_type=F32)

        @pl.when(scalars[1] == first_at)
        def _():
            copy(n, first).start()

        @pl.when(scalars[1] != first_at)
        def _():
            copy(n, second).start()

    for n in range(tiles):
        copy(n, first).wait()


def weight_grad_call(scalars, first_at, dz_own, dz_other, u_own, u_other, after, kept):
    tokens, rows = dz_own.shape
    columns = u_own.shape[1]
    tiles = 4
    return pl.pallas_call(
        functools.partial(weight_grad_kernel, first_at, tiles, len(kept)),
        out_shape=[
            jax.ShapeDtypeStruct((rows, columns), F32),
            jax.ShapeDtypeStruct((rows, columns), F32),
            jax.ShapeDtypeStruct(after.shape, F32),
        ],
        in_specs=[SMEM] + [VMEM] * 5 + [HBM] * len(kept),
        out_specs=[HBM, HBM, VMEM],
        input_output_aliases={6 + n: n for n in range(len(kept))},
        scratch_shapes=[pltpu.VMEM((rows, columns), F32), pltpu.SemaphoreType.DMA((tiles,))],
        compiler_params=pltpu.CompilerParams(vmem_limit_bytes=VMEM_LIMIT),
        cost_estimate=pl.CostEstimate(
            flops=4 * tokens * rows * columns, bytes_accessed=4 * rows * columns, transcendentals=0
        ),
    )(scalars, dz_own, dz_other, u_own, u_other, after, *kept)


def load_kernel(weights, _, held, sems):
    copies = [
        pltpu.make_async_copy(weights.at[0, n], held.at[0, n], sems.at[n]) for n in range(2)
    ]
    for copy in copies:
        copy.start()
    for copy in copies:
        copy.wait()


def load_call(weights, after):
    return pl.pallas_call(
        load_kernel,
        out_shape=jax.ShapeDtypeStruct(weights.shape, weights.dtype),
        in_specs=[HBM, ANY],
        out_specs=VMEM,
        scratch_shapes=[pltpu.SemaphoreType.DMA((2,))],
        compiler_params=pltpu.CompilerParams(vmem_limit_bytes=VMEM_LIMIT),
        cost_estimate=pl.CostEstimate(
            flops=0, bytes_accessed=2 * weights.size, transcendentals=0
        ),
    )(in_hbm(weights), after)


def pack_kernel(scalars, *refs):
    sources, gains_source, (state, cot, payload), gains, sems = (
        refs[:4],
        refs[4],
        refs[5:8],
        refs[8],
        refs[9],
    )
    tokens = state.shape[0]
    gains_copy = pltpu.make_async_copy(gains_source, gains, sems.at[0])
    gains_copy.start()
    for n in range(2):

        @pl.when(scalars[1] == n)
        def _():
            pltpu.make_async_copy(sources[n], state, sems.at[1]).start()
            pltpu.make_async_copy(sources[2 + n], cot, sems.at[2]).start()

    gains_copy.wait()
    row = lax.broadcasted_iota(jnp.int32, (PAD_ROWS, state.shape[1]), 0)
    block = jnp.zeros((PAD_ROWS, state.shape[1]), F32)
    n = 0
    for section in range(2):
        for term in three_terms(gains[section : section + 1, :]):
            block = jnp.where(row == n, term.astype(F32), block)
            n += 1
    payload[tokens:] = block.astype(BF16)
    pltpu.make_async_copy(sources[0], state, sems.at[1]).wait()
    payload[0:tokens] = state[...]
    pltpu.make_async_copy(sources[2], cot, sems.at[2]).wait()


def pack_call(scalars, down_input, up_input, down_cot, up_cot, gains):
    tokens, block = down_input.shape
    return pl.pallas_call(
        pack_kernel,
        out_shape=[
            jax.ShapeDtypeStruct((tokens, block), BF16),
            jax.ShapeDtypeStruct((tokens, block), BF16),
            jax.ShapeDtypeStruct((tokens + PAD_ROWS, block), BF16),
        ],
        in_specs=[SMEM] + [HBM] * 5,
        out_specs=[VMEM] * 3,
        scratch_shapes=[pltpu.VMEM(gains.shape, F32), pltpu.SemaphoreType.DMA((3,))],
        compiler_params=pltpu.CompilerParams(vmem_limit_bytes=VMEM_LIMIT),
    )(scalars, *map(in_hbm, (down_input, up_input, down_cot, up_cot, gains)))


def keep_live(live, record, previous):
    if previous is None or live is None:
        return record
    return jax.tree.map(lambda fresh, older: jnp.where(live, fresh, older), record, previous)


def per_device(down_input, up_input, down_cot, up_cot, section_weights, section_gains):
    sections = lax.axis_size("section")
    middle = sections // 2
    position = lax.axis_index("section")
    seq_size = lax.axis_size("seq")
    seq_index = lax.axis_index("seq")
    lower = position < middle
    tokens, block = down_input.shape
    model_width = section_weights.shape[3]
    half = model_width // 2
    merged = 0
    while (block << merged) % LANES:
        merged += 1
    wide = block << merged
    bit_count = seq_size.bit_length() - 1
    groups = bit_groups(merged, bit_count)
    back_groups = groups[::-1]
    offsets = [o >> merged for o in offsets_of(groups)]
    send_order = [o >> merged for o in offsets_of(back_groups[::-1])]
    me = (seq_index >> merged).astype(jnp.int32)
    first_index = jnp.where(lower, 0, 1).astype(jnp.int32)
    turn = jnp.minimum(position, sections - 1 - position)

    def index_at(step):
        return first_index if step < middle else 1 - first_index

    def scalars_at(step):
        return jnp.stack([me, index_at(step)]).astype(jnp.int32)

    def live_at(step):
        if sections == 2:
            return None
        return turn == min(step, sections - 1 - step)

    def joined_halves(value, axis):
        for bit in range(merged):
            other = from_xor(value, 1 << bit)
            upper = (seq_index >> bit) & 1
            value = jnp.where(
                upper == 1,
                jnp.concatenate([other, value], axis=axis),
                jnp.concatenate([value, other], axis=axis),
            )
        return value

    def own_part(value, width, bit):
        start = ((seq_index >> bit) & 1) * width
        return (
            lax.dynamic_slice_in_dim(value, start, width, axis=1),
            lax.dynamic_slice_in_dim(value, width - start, width, axis=1),
        )

    def gathered(value):
        return gather_xor(joined_halves(value, 1), groups)

    def moved(value, step, later):
        low = min(step, sections - 1 - step)
        new = min(later, sections - 1 - later)
        if low == new:
            return value
        route = [(low, new), (sections - 1 - low, sections - 1 - new)]
        return lax.ppermute(value, "section", route)

    def reduced(sent, beside=None):
        parts = grads = None
        for n, group in enumerate(back_groups):
            sent = sent.reshape((len(group) + 1, -1) + sent.shape[1:])
            parts = reduce_round(sent, group)
            if n + 1 < len(back_groups):
                if n == 0 and beside is not None:
                    parts, grads = lax.optimization_barrier((parts, beside()))
                total = functools.reduce(jnp.add, [p.astype(F32) for p in parts])
                sent = total.astype(BF16)
                kept = total[0]
        parts = [kept if len(back_groups) > 1 else parts[0][0].astype(F32)] + [
            p[0] for p in parts[1:]
        ]
        return parts, grads

    def finished(parts):
        total = functools.reduce(jnp.add, [p.astype(F32) for p in parts])
        du, first, second = split_packed(total, tokens, wide)
        for bit in reversed(range(merged)):
            width = du.shape[1] // 2
            mine, theirs = own_part(du, width, bit)
            tail = jnp.concatenate(two_terms(first) + two_terms(second), axis=1)
            message = jnp.concatenate([theirs.astype(BF16), tail], axis=1)
            message = from_xor(message, 1 << bit).astype(F32)
            du = mine + message[:, :width]
            first = first + message[:, width : width + 1] + message[:, width + 1 : width + 2]
            second = second + message[:, width + 2 : width + 3] + message[:, width + 3 :]
        return du, first, second

    own_gains = section_gains[0]
    state, grad, packed = pack_call(
        scalars_at(0), down_input, up_input, down_cot, up_cot, own_gains
    )
    first_record = second_record = None
    gains = None
    for step in range(sections):
        last = step == sections - 1
        pieces, partly = gathered(packed if step == 0 else state)
        if step == 0:
            weights = load_call(section_weights, partly)
        result = section_call(
            scalars_at(step),
            weights,
            pieces,
            state,
            gains,
            grad if last else None,
            None,
            offsets,
            send_order,
            wide,
            step == 0,
        )
        u, stat, z, y = result[:4]
        if step == 0:
            gains = result[4]
        record = (state, pieces[:, :tokens] if sections > 2 else pieces, u, stat, z, y)
        if step < middle:
            first_record = keep_live(live_at(step), record, first_record)
        else:
            second_record = keep_live(live_at(step), record, second_record)
        if last:
            dz, sent = result[-2:]
        else:
            state = moved(y, step, step + 1)
    u_a, y_a = first_record[2], first_record[5]
    u_b, y_b = second_record[2], second_record[5]
    needed_a = jnp.where(lower, u_a[:, :half], u_a[:, half:])
    needed_b = jnp.where(lower, u_b[:, half:], u_b[:, :half])
    other_a = swapped(jnp.where(lower, u_a[:, half:], u_a[:, :half]))
    other_b = swapped(jnp.where(lower, u_b[:, :half], u_b[:, half:]))
    def early_results(dz):
        y_other = swapped(y_b)
        grads = weight_grad_call(
            scalars_at(0), 1, dz, swapped(dz), needed_b, other_b, jnp.zeros((8, LANES), F32), ()
        )
        return grads, (jnp.where(lower, y_a, y_other), jnp.where(lower, y_other, y_a))

    dz_a = dz_b = gain_b = gain_a = None
    for step in reversed(range(1, sections)):
        source, _, _, stat, z, _ = second_record if step >= middle else first_record
        if step < sections - 1:
            dz, sent = section_call(
                scalars_at(step),
                weights,
                None,
                None,
                gains,
                grad,
                z,
                offsets,
                send_order,
                wide,
                False,
            )
        gain_row = lax.dynamic_slice_in_dim(own_gains, index_at(step), 1, axis=0)
        if step >= middle:
            dz_b = keep_live(live_at(step), dz, dz_b)
        else:
            dz_a = keep_live(live_at(step), dz, dz_a)
        beside = None
        if step == middle:
            beside = functools.partial(early_results, dz_b)
        parts, done = reduced(sent, beside)
        if beside is not None:
            (early_first, early_second, _), (down_out, up_out) = beside() if done is None else done
        finish = None
        if sections == 2 and not merged:
            finish = (parts, (source, stat, gain_row))
        else:
            du, first, second = finished(parts)
            new_grad, gain_grad = input_gradient(
                du,
                first,
                second,
                grad,
                source,
                stat[:, 0:1],
                stat[:, 1:2],
                gain_row,
                model_width,
            )
            if step >= middle:
                gain_b = keep_live(live_at(step), gain_grad, gain_b)
            else:
                gain_a = keep_live(live_at(step), gain_grad, gain_a)
            grad = moved(new_grad, step, step - 1)
    _, pieces, _, stat, z, _ = first_record
    first_size = len(back_groups[0]) + 1
    result = last_call(
        scalars_at(0),
        weights,
        pieces,
        stat,
        z,
        grad,
        finish,
        offsets,
        send_order,
        wide,
        first_size,
    )
    dz, gain_parts = result[0], result[1 : 1 + first_size]
    if finish is not None:
        gain_b = result[-1]
    dz_a = keep_live(live_at(0), dz, dz_a)
    dz_a_other = swapped(dz_a)
    early = (early_first, early_second)
    for n, group in enumerate(back_groups):
        if n:
            gain_parts = gain_parts.reshape((len(group) + 1, -1) + gain_parts.shape[1:])
        parts = reduce_round(gain_parts, group)
        if n == 0:
            grad_first, grad_second, token = weight_grad_call(
                scalars_at(0), 0, dz_a, dz_a_other, needed_a, other_a, parts[0], early
            )
            parts.append(token)
        gain_parts = functools.reduce(jnp.add, parts)
    gain = gain_parts.reshape(1, wide)
    for bit in reversed(range(merged)):
        mine, theirs = own_part(gain, gain.shape[1] // 2, bit)
        gain = mine + from_xor(theirs, 1 << bit)
    gain_a = keep_live(live_at(0), gain, gain_a)
    gain_other = swapped(jnp.where(lower, gain_b, gain_a))
    gain_total = jnp.where(lower, gain_a, gain_b) + gain_other
    return (
        down_out[None],
        up_out[None],
        grad_first[None],
        grad_second[None],
        gain_total,
    )


def solution(mesh):
    in_specs = (
        P(None, "seq"),
        P(None, "seq"),
        P(None, "seq"),
        P(None, "seq"),
        P("section", None, "seq", None),
        P("section", None, "seq"),
    )
    out_specs = (
        P("section", None, "seq"),
        P("section", None, "seq"),
        P("section", "seq", None),
        P("section", "seq", None),
        P("section", "seq"),
    )
    return jax.shard_map(
        per_device, mesh=mesh, in_specs=in_specs, out_specs=out_specs, check_vma=False
    )
```

```python
import functools
import math

import jax
import jax.numpy as jnp
from jax import lax
from jax.experimental import pallas as pl
from jax.experimental.pallas import tpu as pltpu
from jax.sharding import PartitionSpec as P

EPS = 1e-05
F32 = jnp.float32
BF16 = jnp.bfloat16
LANES = 128
PAD_ROWS = 8
SQRT_HALF = math.sqrt(0.5)
INV_SQRT_2PI = 1.0 / math.sqrt(2.0 * math.pi)
VMEM_LIMIT = 32 * 1024 * 1024

VMEM = pl.BlockSpec(memory_space=pltpu.VMEM)
ANY = pl.BlockSpec(memory_space=pl.ANY)
SMEM = pl.BlockSpec(memory_space=pltpu.SMEM)


def from_xor(value, distance):
    size = lax.axis_size("seq")
    return lax.ppermute(value, "seq", [(i, i ^ distance) for i in range(size)])


def swapped(value):
    size = lax.axis_size("section")
    return lax.ppermute(value, "section", [(i, size - 1 - i) for i in range(size)])


def bit_groups(low, count):
    bits = [1 << b for b in range(low, count)][::-1]
    groups = []
    while bits:
        pair, bits = bits[:2], bits[2:]
        groups.append(tuple(pair) if len(pair) == 1 else (pair[0], pair[1], pair[0] ^ pair[1]))
    return groups


def offsets_of(groups):
    offsets = [0]
    for group in groups:
        offsets = [o ^ d for d in (0,) + group for o in offsets]
    return offsets


def gather_xor(block, groups):
    held = block[None]
    for n, group in enumerate(groups):
        if n <= 1:
            early = held
        held = jnp.concatenate([held] + [from_xor(held, d) for d in group], axis=0)
    return held, early


def reduce_round(held, group):
    sent = [from_xor(held[n + 1], d) for n, d in enumerate(group)]
    return [held[0]] + sent


def in_hbm(value):
    return pltpu.with_memory_space_constraint(value, pltpu.HBM)


def gelu_and_slope(z):
    cdf = 0.5 * (1.0 + lax.erf(z * SQRT_HALF))
    slope = cdf + z * (jnp.exp(-0.5 * z * z) * INV_SQRT_2PI)
    return z * cdf, slope


def column_to_row(column):
    tokens = column.shape[0]
    rows = lax.broadcasted_iota(jnp.int32, (tokens, LANES), 0)
    lanes = lax.broadcasted_iota(jnp.int32, (tokens, LANES), 1)
    return jnp.sum(jnp.where(rows == lanes, column, 0.0), axis=0, keepdims=True)


def row_to_column(row, tokens):
    rows = lax.broadcasted_iota(jnp.int32, (tokens, LANES), 0)
    lanes = lax.broadcasted_iota(jnp.int32, (tokens, LANES), 1)
    return jnp.sum(jnp.where(rows == lanes, row, 0.0), axis=1, keepdims=True)


def two_terms(value):
    high = value.astype(BF16)
    return high, (value - high.astype(F32)).astype(BF16)


def three_terms(value):
    high, rest = value.astype(BF16), None
    rest = value - high.astype(F32)
    middle = rest.astype(BF16)
    return high, middle, (rest - middle.astype(F32)).astype(BF16)


def sums_block(first_sum, second_sum):
    row = lax.broadcasted_iota(jnp.int32, (PAD_ROWS, LANES), 0)
    block = jnp.zeros((PAD_ROWS, LANES), F32)
    n = 0
    for column in (first_sum, second_sum):
        for term in two_terms(column_to_row(column)):
            block = jnp.where(row == n, term.astype(F32), block)
            n += 1
    return block.astype(BF16)


def split_packed(total, tokens, width):
    chunks = width // LANES
    du = jnp.concatenate([total[c * tokens : (c + 1) * tokens] for c in range(chunks)], axis=1)
    tail = total[chunks * tokens : chunks * tokens + PAD_ROWS]
    first = row_to_column(tail[0:1] + tail[1:2], tokens)
    second = row_to_column(tail[2:3] + tail[3:4], tokens)
    return du, first, second


def input_gradient(du, first_sum, second_sum, dy, block, mean, scale, gain, model_width):
    hat = (block.astype(F32) - mean) * scale
    gained = du * gain
    dx = dy.astype(F32) + scale * (
        gained - first_sum / model_width - hat * (second_sum / model_width)
    )
    return dx.astype(BF16), jnp.sum(du * hat, axis=0, keepdims=True)


def section_kernel(offsets, dims, forward, unpack, backward, send_order, *refs):
    tokens, block, model_width = dims
    refs = list(refs)
    take = refs.pop
    scalars = take(0)
    weights = take(0)
    pieces = take(0) if forward else None
    own = take(0) if forward else None
    gains = None if unpack else take(0)
    dy_ref = take(0) if backward else None
    z_ref = None if forward else take(0)
    if forward:
        u_out, stat_out, z_out, y_out = take(0), take(0), take(0), take(0)
    if unpack:
        gains = take(0)
    if backward:
        dz_out, sent_out = take(0), take(0)
    me, windex = scalars[0], scalars[1]
    held = weights.at[0, windex]
    wide = block
    if forward:
        total = jnp.zeros((tokens, LANES), F32)
        squares = jnp.zeros((tokens, LANES), F32)
        for e in range(len(offsets)):
            for c in range(wide // LANES):
                part = pieces[e, 0:tokens, c * LANES : (c + 1) * LANES].astype(F32)
                total = total + part
                squares = squares + part * part
        mean = jnp.sum(total, axis=1, keepdims=True) / model_width
        var = jnp.sum(squares, axis=1, keepdims=True) / model_width - mean * mean
        scale = lax.rsqrt(var + EPS)
        lane = lax.broadcasted_iota(jnp.int32, (tokens, LANES), 1)
        stat_out[...] = jnp.where(lane == 0, mean, scale)
        for e, offset in enumerate(offsets):
            column = pl.multiple_of((me ^ offset) * wide, LANES)
            if unpack:
                terms = pieces[e, tokens : tokens + PAD_ROWS, :].astype(F32)
                gains[0:1, pl.ds(column, wide)] = terms[0:1] + terms[1:2] + terms[2:3]
                gains[1:2, pl.ds(column, wide)] = terms[3:4] + terms[4:5] + terms[5:6]
            gain = gains[pl.ds(windex, 1), pl.ds(column, wide)]
            hat = (pieces[e, 0:tokens, :].astype(F32) - mean) * scale
            u_out[:, pl.ds(column, wide)] = (hat * gain).astype(BF16)
        z = lax.dot_general(
            u_out[...], held[...], (((1,), (1,)), ((), ())), preferred_element_type=F32
        )
        gelu, slope = gelu_and_slope(z)
        z_out[...] = z
        y_out[...] = (own[...].astype(F32) + gelu).astype(BF16)
    if backward:
        if not forward:
            z = z_ref[...]
            gelu, slope = gelu_and_slope(z)
        dz = (dy_ref[...].astype(F32) * slope).astype(BF16)
        dz_out[...] = dz
        second = jnp.sum(dz.astype(F32) * z, axis=1, keepdims=True)
        first = jnp.zeros((tokens, LANES), F32)
        for n, offset in enumerate(send_order):
            column = pl.multiple_of((me ^ offset) * wide, LANES)
            part = jnp.dot(dz, held[:, pl.ds(column, wide)], preferred_element_type=F32)
            gained = part * gains[pl.ds(windex, 1), pl.ds(column, wide)]
            for c in range(wide // LANES):
                first = first + gained[:, c * LANES : (c + 1) * LANES]
                sent_out[n, c * tokens : (c + 1) * tokens, :] = part[
                    :, c * LANES : (c + 1) * LANES
                ].astype(BF16)
        tail = sums_block(jnp.sum(first, axis=1, keepdims=True), second)
        rows = tokens * (wide // LANES)
        for n in range(len(send_order)):
            sent_out[n, rows : rows + PAD_ROWS, :] = tail


def section_call(scalars, weights, pieces, own, gains, dy, z, offsets, send_order, wide, unpack):
    forward, backward = pieces is not None, dy is not None
    rows, model_width = weights.shape[2:]
    tokens = (own if forward else dy).shape[0]
    operands, specs = [scalars, weights], [SMEM, VMEM]
    for value in (pieces, own, gains, dy, z):
        if value is not None:
            operands.append(value)
            specs.append(VMEM)
    outs = []
    if forward:
        outs += [
            jax.ShapeDtypeStruct((tokens, model_width), BF16),
            jax.ShapeDtypeStruct((tokens, LANES), F32),
            jax.ShapeDtypeStruct((tokens, rows), F32),
            jax.ShapeDtypeStruct((tokens, rows), BF16),
        ]
    if unpack:
        outs.append(jax.ShapeDtypeStruct((2, model_width), F32))
    if backward:
        outs += [
            jax.ShapeDtypeStruct((tokens, rows), BF16),
            jax.ShapeDtypeStruct(
                (len(send_order), tokens * (wide // LANES) + PAD_ROWS, LANES), BF16
            ),
        ]
    flops = 2 * tokens * rows * model_width * (int(forward) + int(backward))
    return pl.pallas_call(
        functools.partial(
            section_kernel,
            offsets,
            (tokens, wide, model_width),
            forward,
            unpack,
            backward,
            send_order,
        ),
        out_shape=outs,
        in_specs=specs,
        out_specs=[VMEM] * len(outs),
        compiler_params=pltpu.CompilerParams(vmem_limit_bytes=VMEM_LIMIT),
        cost_estimate=pl.CostEstimate(
            flops=flops, bytes_accessed=2 * rows * model_width, transcendentals=tokens * rows
        ),
    )(*operands)


def last_kernel(offsets, places, dims, part_count, *refs):
    tokens, wide, model_width, first_size = dims
    scalars, weights, pieces, stat, z_ref, dy_ref = refs[:6]
    refs = refs[6:]
    if part_count:
        parts, (block_ref, next_stat, next_gain), refs = (
            refs[:part_count],
            refs[part_count : part_count + 3],
            refs[part_count + 3 :],
        )
        next_gain_out = refs[-1]
    dz_out, gain_out = refs[0], refs[1 : 1 + first_size]
    me, windex = scalars[0], scalars[1]
    held = weights.at[0, windex]
    dy = dy_ref[...]
    if part_count:
        total = parts[0][...]
        for part in parts[1:]:
            total = total + part[...].astype(F32)
        du, first, second = split_packed(total, tokens, wide)
        dy, gain_grad = input_gradient(
            du,
            first,
            second,
            dy,
            block_ref[...],
            next_stat[:, 0:1],
            next_stat[:, 1:2],
            next_gain[...],
            model_width,
        )
        next_gain_out[...] = gain_grad
    slope = gelu_and_slope(z_ref[...])[1]
    dz = (dy.astype(F32) * slope).astype(BF16)
    dz_out[...] = dz
    mean, scale = stat[:, 0:1], stat[:, 1:2]
    for e, offset in enumerate(offsets):
        column = pl.multiple_of((me ^ offset) * wide, LANES)
        part = jnp.dot(dz, held[:, pl.ds(column, wide)], preferred_element_type=F32)
        hat = (pieces[e, 0:tokens, :].astype(F32) - mean) * scale
        a, b = places[e]
        gain_out[a][b : b + 1, :] = jnp.sum(part * hat, axis=0, keepdims=True)


def last_call(scalars, weights, pieces, stat, z, dy, finish, offsets, send_order, wide, first_size):
    rows, model_width = weights.shape[2:]
    tokens = dy.shape[0]
    rest = len(offsets) // first_size
    places = [divmod(send_order.index(o), rest) for o in offsets]
    operands = [scalars, weights, pieces, stat, z, dy]
    outs = [
        jax.ShapeDtypeStruct((tokens, rows), BF16),
    ] + [jax.ShapeDtypeStruct((rest, wide), F32)] * first_size
    part_count = 0
    if finish is not None:
        parts, others = finish
        part_count = len(parts)
        operands += list(parts) + list(others)
        outs.append(jax.ShapeDtypeStruct((1, rows), F32))
    return pl.pallas_call(
        functools.partial(
            last_kernel,
            offsets,
            places,
            (tokens, wide, model_width, first_size),
            part_count,
        ),
        out_shape=outs,
        in_specs=[SMEM] + [VMEM] * (len(operands) - 1),
        out_specs=[VMEM] * len(outs),
        compiler_params=pltpu.CompilerParams(vmem_limit_bytes=VMEM_LIMIT),
        cost_estimate=pl.CostEstimate(
            flops=2 * tokens * rows * model_width,
            bytes_accessed=2 * rows * model_width,
            transcendentals=tokens * rows,
        ),
    )(*operands)


def weight_grad_kernel(take_early, *refs):
    scalars, early, early_other, late, late_other, u_own, u_other, _, out, order, depth = refs
    tokens = early.shape[0]

    @pl.when(pl.program_id(0) == 0)
    def _():
        pick = scalars[1] == (0 if take_early else 1)
        mine = jnp.where(pick, early[...], late[...])
        theirs = jnp.where(pick, early_other[...], late_other[...])
        depth[...] = jnp.concatenate([mine, theirs], axis=0).T
        order[...] = jnp.zeros_like(order)

    both = jnp.concatenate([u_own[...], u_other[...]], axis=0)
    out[...] = jnp.dot(depth[...], both, preferred_element_type=F32)


def weight_grad_call(scalars, first, dz_a, dz_a_other, dz_b, dz_b_other, u_own, u_other, after):
    tokens, rows = dz_a.shape
    columns = u_own.shape[1]
    steps = 4
    tile = columns // steps
    whole = pl.BlockSpec((tokens, rows), lambda i: (0, 0))
    narrow = pl.BlockSpec((tokens, tile), lambda i: (0, i))
    small = pl.BlockSpec(after.shape, lambda i: (0,) * after.ndim)
    return pl.pallas_call(
        functools.partial(weight_grad_kernel, first),
        grid=(steps,),
        out_shape=[
            jax.ShapeDtypeStruct((rows, columns), F32),
            jax.ShapeDtypeStruct(after.shape, F32),
        ],
        in_specs=[SMEM] + [whole] * 4 + [narrow] * 2 + [small],
        out_specs=[pl.BlockSpec((rows, tile), lambda i: (0, i)), small],
        scratch_shapes=[pltpu.VMEM((rows, 2 * tokens), BF16)],
        compiler_params=pltpu.CompilerParams(vmem_limit_bytes=VMEM_LIMIT),
        cost_estimate=pl.CostEstimate(
            flops=4 * tokens * rows * columns, bytes_accessed=4 * rows * columns, transcendentals=0
        ),
    )(scalars, dz_a, dz_a_other, dz_b, dz_b_other, u_own, u_other, after)


def load_kernel(weights, _, held, sems):
    copies = [
        pltpu.make_async_copy(weights.at[0, n], held.at[0, n], sems.at[n]) for n in range(2)
    ]
    for copy in copies:
        copy.start()
    for copy in copies:
        copy.wait()


def load_call(weights, after):
    return pl.pallas_call(
        load_kernel,
        out_shape=jax.ShapeDtypeStruct(weights.shape, weights.dtype),
        in_specs=[ANY, ANY],
        out_specs=VMEM,
        scratch_shapes=[pltpu.SemaphoreType.DMA((2,))],
        compiler_params=pltpu.CompilerParams(vmem_limit_bytes=VMEM_LIMIT),
        cost_estimate=pl.CostEstimate(
            flops=0, bytes_accessed=2 * weights.size, transcendentals=0
        ),
    )(in_hbm(weights), after)


def pack_kernel(scalars, *refs):
    sources, gains_source, (state, cot, payload), gains, sems = (
        refs[:4],
        refs[4],
        refs[5:8],
        refs[8],
        refs[9],
    )
    tokens = state.shape[0]
    gains_copy = pltpu.make_async_copy(gains_source, gains, sems.at[0])
    gains_copy.start()
    for n in range(2):

        @pl.when(scalars[1] == n)
        def _():
            pltpu.make_async_copy(sources[n], state, sems.at[1]).start()
            pltpu.make_async_copy(sources[2 + n], cot, sems.at[2]).start()

    gains_copy.wait()
    row = lax.broadcasted_iota(jnp.int32, (PAD_ROWS, state.shape[1]), 0)
    block = jnp.zeros((PAD_ROWS, state.shape[1]), F32)
    n = 0
    for section in range(2):
        for term in three_terms(gains[section : section + 1, :]):
            block = jnp.where(row == n, term.astype(F32), block)
            n += 1
    payload[tokens:] = block.astype(BF16)
    pltpu.make_async_copy(sources[0], state, sems.at[1]).wait()
    payload[0:tokens] = state[...]
    pltpu.make_async_copy(sources[2], cot, sems.at[2]).wait()


def pack_call(scalars, down_input, up_input, down_cot, up_cot, gains):
    tokens, block = down_input.shape
    return pl.pallas_call(
        pack_kernel,
        out_shape=[
            jax.ShapeDtypeStruct((tokens, block), BF16),
            jax.ShapeDtypeStruct((tokens, block), BF16),
            jax.ShapeDtypeStruct((tokens + PAD_ROWS, block), BF16),
        ],
        in_specs=[SMEM] + [ANY] * 5,
        out_specs=[VMEM] * 3,
        scratch_shapes=[pltpu.VMEM(gains.shape, F32), pltpu.SemaphoreType.DMA((3,))],
        compiler_params=pltpu.CompilerParams(vmem_limit_bytes=VMEM_LIMIT),
    )(scalars, *map(in_hbm, (down_input, up_input, down_cot, up_cot, gains)))


def keep_live(live, record, previous):
    if previous is None or live is None:
        return record
    return jax.tree.map(lambda fresh, older: jnp.where(live, fresh, older), record, previous)


def per_device(down_input, up_input, down_cot, up_cot, section_weights, section_gains):
    sections = lax.axis_size("section")
    middle = sections // 2
    position = lax.axis_index("section")
    seq_size = lax.axis_size("seq")
    seq_index = lax.axis_index("seq")
    lower = position < middle
    tokens, block = down_input.shape
    model_width = section_weights.shape[3]
    half = model_width // 2
    merged = 0
    while (block << merged) % LANES:
        merged += 1
    wide = block << merged
    bit_count = seq_size.bit_length() - 1
    groups = bit_groups(merged, bit_count)
    back_groups = [group[::-1] for group in groups[::-1]]
    offsets = [o >> merged for o in offsets_of(groups)]
    send_order = [o >> merged for o in offsets_of(back_groups[::-1])]
    me = (seq_index >> merged).astype(jnp.int32)
    first_index = jnp.where(lower, 0, 1).astype(jnp.int32)
    turn = jnp.minimum(position, sections - 1 - position)

    def index_at(step):
        return first_index if step < middle else 1 - first_index

    def scalars_at(step):
        return jnp.stack([me, index_at(step)]).astype(jnp.int32)

    def live_at(step):
        if sections == 2:
            return None
        return turn == min(step, sections - 1 - step)

    def joined_halves(value, axis):
        for bit in range(merged):
            other = from_xor(value, 1 << bit)
            upper = (seq_index >> bit) & 1
            value = jnp.where(
                upper == 1,
                jnp.concatenate([other, value], axis=axis),
                jnp.concatenate([value, other], axis=axis),
            )
        return value

    def own_part(value, width, bit):
        start = ((seq_index >> bit) & 1) * width
        return (
            lax.dynamic_slice_in_dim(value, start, width, axis=1),
            lax.dynamic_slice_in_dim(value, width - start, width, axis=1),
        )

    def gathered(value):
        return gather_xor(joined_halves(value, 1), groups)

    def moved(value, step, later):
        low = min(step, sections - 1 - step)
        new = min(later, sections - 1 - later)
        if low == new:
            return value
        route = [(low, new), (sections - 1 - low, sections - 1 - new)]
        return lax.ppermute(value, "section", route)

    def reduced(sent):
        parts = None
        for n, group in enumerate(back_groups):
            sent = sent.reshape((len(group) + 1, -1) + sent.shape[1:])
            parts = reduce_round(sent, group)
            if n + 1 < len(back_groups):
                total = functools.reduce(jnp.add, [p.astype(F32) for p in parts])
                sent = total.astype(BF16)
                kept = total[0]
        parts = [kept if len(back_groups) > 1 else parts[0][0].astype(F32)] + [
            p[0] for p in parts[1:]
        ]
        return parts

    def finished(parts):
        total = functools.reduce(jnp.add, [p.astype(F32) for p in parts])
        du, first, second = split_packed(total, tokens, wide)
        for bit in reversed(range(merged)):
            width = du.shape[1] // 2
            mine, theirs = own_part(du, width, bit)
            tail = jnp.concatenate(two_terms(first) + two_terms(second), axis=1)
            message = jnp.concatenate([theirs.astype(BF16), tail], axis=1)
            message = from_xor(message, 1 << bit).astype(F32)
            du = mine + message[:, :width]
            first = first + message[:, width : width + 1] + message[:, width + 1 : width + 2]
            second = second + message[:, width + 2 : width + 3] + message[:, width + 3 :]
        return du, first, second

    own_gains = section_gains[0]
    state, grad, packed = pack_call(
        scalars_at(0), down_input, up_input, down_cot, up_cot, own_gains
    )
    first_record = second_record = None
    gains = None
    for step in range(sections):
        last = step == sections - 1
        pieces, partly = gathered(packed if step == 0 else state)
        if step == 0:
            weights = load_call(section_weights, partly)
        result = section_call(
            scalars_at(step),
            weights,
            pieces,
            state,
            gains,
            grad if last else None,
            None,
            offsets,
            send_order,
            wide,
            step == 0,
        )
        u, stat, z, y = result[:4]
        if step == 0:
            gains = result[4]
        record = (state, pieces[:, :tokens] if sections > 2 else pieces, u, stat, z, y)
        if step < middle:
            first_record = keep_live(live_at(step), record, first_record)
        else:
            second_record = keep_live(live_at(step), record, second_record)
        if last:
            dz, sent = result[-2:]
        else:
            state = moved(y, step, step + 1)
    u_a, y_a = first_record[2], first_record[5]
    u_b, y_b = second_record[2], second_record[5]
    y_other = swapped(y_b)
    down_out = jnp.where(lower, y_a, y_other)
    up_out = jnp.where(lower, y_other, y_a)
    u_first = jnp.where(lower, u_a[:, :half], u_b[:, :half])
    u_second = jnp.where(lower, u_b[:, half:], u_a[:, half:])
    other_first = swapped(jnp.where(lower, u_b[:, :half], u_a[:, :half]))
    other_second = swapped(jnp.where(lower, u_a[:, half:], u_b[:, half:]))
    dz_a = dz_b = gain_b = gain_a = None
    for step in reversed(range(1, sections)):
        source, _, _, stat, z, _ = second_record if step >= middle else first_record
        if step < sections - 1:
            dz, sent = section_call(
                scalars_at(step),
                weights,
                None,
                None,
                gains,
                grad,
                z,
                offsets,
                send_order,
                wide,
                False,
            )
        parts = reduced(sent)
        gain_row = lax.dynamic_slice_in_dim(own_gains, index_at(step), 1, axis=0)
        if step >= middle:
            dz_b = keep_live(live_at(step), dz, dz_b)
        else:
            dz_a = keep_live(live_at(step), dz, dz_a)
        finish = None
        if sections == 2 and not merged:
            finish = (parts, (source, stat, gain_row))
        else:
            du, first, second = finished(parts)
            new_grad, gain_grad = input_gradient(
                du,
                first,
                second,
                grad,
                source,
                stat[:, 0:1],
                stat[:, 1:2],
                gain_row,
                model_width,
            )
            if step >= middle:
                gain_b = keep_live(live_at(step), gain_grad, gain_b)
            else:
                gain_a = keep_live(live_at(step), gain_grad, gain_a)
            grad = moved(new_grad, step, step - 1)
    _, pieces, _, stat, z, _ = first_record
    first_size = len(back_groups[0]) + 1
    result = last_call(
        scalars_at(0),
        weights,
        pieces,
        stat,
        z,
        grad,
        finish,
        offsets,
        send_order,
        wide,
        first_size,
    )
    dz, gain_parts = result[0], result[1 : 1 + first_size]
    if finish is not None:
        gain_b = result[-1]
    dz_a = keep_live(live_at(0), dz, dz_a)
    dz_a_other = swapped(dz_a)
    dz_b_other = swapped(dz_b)
    dz_all = (dz_a, dz_a_other, dz_b, dz_b_other)
    grads = []
    halves = [(True, u_first, other_first), (False, u_second, other_second)]
    for n, group in enumerate(back_groups):
        if n:
            gain_parts = gain_parts.reshape((len(group) + 1, -1) + gain_parts.shape[1:])
        parts = reduce_round(gain_parts, group)
        if halves:
            first, mine, theirs = halves.pop(0)
            grad_half, token = weight_grad_call(
                scalars_at(0), first, *dz_all, mine, theirs, parts[0]
            )
            grads.append(grad_half)
            parts.append(token)
        gain_parts = functools.reduce(jnp.add, parts)
    for first, mine, theirs in halves:
        grads.append(weight_grad_call(scalars_at(0), first, *dz_all, mine, theirs, token)[0])
    grad_first, grad_second = grads
    gain = gain_parts.reshape(1, wide)
    for bit in reversed(range(merged)):
        mine, theirs = own_part(gain, gain.shape[1] // 2, bit)
        gain = mine + from_xor(theirs, 1 << bit)
    gain_a = keep_live(live_at(0), gain, gain_a)
    gain_other = swapped(jnp.where(lower, gain_b, gain_a))
    gain_total = jnp.where(lower, gain_a, gain_b) + gain_other
    return (
        down_out[None],
        up_out[None],
        grad_first[None],
        grad_second[None],
        gain_total,
    )


def solution(mesh):
    in_specs = (
        P(None, "seq"),
        P(None, "seq"),
        P(None, "seq"),
        P(None, "seq"),
        P("section", None, "seq", None),
        P("section", None, "seq"),
    )
    out_specs = (
        P("section", None, "seq"),
        P("section", None, "seq"),
        P("section", "seq", None),
        P("section", "seq", None),
        P("section", "seq"),
    )
    return jax.shard_map(
        per_device, mesh=mesh, in_specs=in_specs, out_specs=out_specs, check_vma=False
    )
```

```python
import functools
import math

import jax
import jax.numpy as jnp
from jax import lax
from jax.experimental import pallas as pl
from jax.experimental.pallas import tpu as pltpu
from jax.sharding import PartitionSpec as P

EPS = 1e-05
F32 = jnp.float32
BF16 = jnp.bfloat16
LANES = 128
PAD_ROWS = 8
SQRT_HALF = math.sqrt(0.5)
INV_SQRT_2PI = 1.0 / math.sqrt(2.0 * math.pi)
VMEM_LIMIT = 32 * 1024 * 1024

VMEM = pl.BlockSpec(memory_space=pltpu.VMEM)
HBM = pl.BlockSpec(memory_space=pltpu.HBM)
ANY = pl.BlockSpec(memory_space=pl.ANY)
SMEM = pl.BlockSpec(memory_space=pltpu.SMEM)


def from_xor(value, distance):
    size = lax.axis_size("seq")
    return lax.ppermute(value, "seq", [(i, i ^ distance) for i in range(size)])


def swapped(value):
    size = lax.axis_size("section")
    return lax.ppermute(value, "section", [(i, size - 1 - i) for i in range(size)])


def bit_groups(low, count):
    bits = [1 << b for b in range(low, count)][::-1]
    groups = []
    while bits:
        pair, bits = bits[:2], bits[2:]
        groups.append(tuple(pair) if len(pair) == 1 else (pair[0], pair[1], pair[0] ^ pair[1]))
    return groups


def offsets_of(groups):
    offsets = [0]
    for group in groups:
        offsets = [o ^ d for d in (0,) + group for o in offsets]
    return offsets


def gather_xor(block, groups):
    held = block[None]
    for n, group in enumerate(groups):
        if n <= 1:
            early = held
        held = jnp.concatenate([held] + [from_xor(held, d) for d in group], axis=0)
    return held, early


def reduce_round(held, group):
    sent = [from_xor(held[n + 1], d) for n, d in enumerate(group)]
    return [held[0]] + sent


def in_hbm(value):
    return pltpu.with_memory_space_constraint(value, pltpu.HBM)


def gelu_and_slope(z):
    cdf = 0.5 * (1.0 + lax.erf(z * SQRT_HALF))
    slope = cdf + z * (jnp.exp(-0.5 * z * z) * INV_SQRT_2PI)
    return z * cdf, slope


def column_to_row(column):
    tokens = column.shape[0]
    rows = lax.broadcasted_iota(jnp.int32, (tokens, LANES), 0)
    lanes = lax.broadcasted_iota(jnp.int32, (tokens, LANES), 1)
    return jnp.sum(jnp.where(rows == lanes, column, 0.0), axis=0, keepdims=True)


def row_to_column(row, tokens):
    rows = lax.broadcasted_iota(jnp.int32, (tokens, LANES), 0)
    lanes = lax.broadcasted_iota(jnp.int32, (tokens, LANES), 1)
    return jnp.sum(jnp.where(rows == lanes, row, 0.0), axis=1, keepdims=True)


def two_terms(value):
    high = value.astype(BF16)
    return high, (value - high.astype(F32)).astype(BF16)


def three_terms(value):
    high, rest = value.astype(BF16), None
    rest = value - high.astype(F32)
    middle = rest.astype(BF16)
    return high, middle, (rest - middle.astype(F32)).astype(BF16)


def sums_block(first_sum, second_sum):
    row = lax.broadcasted_iota(jnp.int32, (PAD_ROWS, LANES), 0)
    block = jnp.zeros((PAD_ROWS, LANES), F32)
    n = 0
    for column in (first_sum, second_sum):
        for term in two_terms(column_to_row(column)):
            block = jnp.where(row == n, term.astype(F32), block)
            n += 1
    return block.astype(BF16)


def split_packed(total, tokens, width):
    chunks = width // LANES
    du = jnp.concatenate([total[c * tokens : (c + 1) * tokens] for c in range(chunks)], axis=1)
    tail = total[chunks * tokens : chunks * tokens + PAD_ROWS]
    first = row_to_column(tail[0:1] + tail[1:2], tokens)
    second = row_to_column(tail[2:3] + tail[3:4], tokens)
    return du, first, second


def input_gradient(du, first_sum, second_sum, dy, block, mean, scale, gain, model_width):
    hat = (block.astype(F32) - mean) * scale
    gained = du * gain
    dx = dy.astype(F32) + scale * (
        gained - first_sum / model_width - hat * (second_sum / model_width)
    )
    return dx.astype(BF16), jnp.sum(du * hat, axis=0, keepdims=True)


def section_kernel(offsets, dims, forward, unpack, backward, send_order, *refs):
    tokens, block, model_width = dims
    refs = list(refs)
    take = refs.pop
    scalars = take(0)
    weights = take(0)
    pieces = take(0) if forward else None
    own = take(0) if forward else None
    gains = None if unpack else take(0)
    dy_ref = take(0) if backward else None
    z_ref = None if forward else take(0)
    if forward:
        u_out, stat_out, z_out, y_out = take(0), take(0), take(0), take(0)
    if unpack:
        gains = take(0)
    if backward:
        dz_out, sent_out = take(0), take(0)
    me, windex = scalars[0], scalars[1]
    held = weights.at[0, windex]
    wide = block
    if forward:
        total = jnp.zeros((tokens, LANES), F32)
        squares = jnp.zeros((tokens, LANES), F32)
        for e in range(len(offsets)):
            for c in range(wide // LANES):
                part = pieces[e, 0:tokens, c * LANES : (c + 1) * LANES].astype(F32)
                total = total + part
                squares = squares + part * part
        mean = jnp.sum(total, axis=1, keepdims=True) / model_width
        var = jnp.sum(squares, axis=1, keepdims=True) / model_width - mean * mean
        scale = lax.rsqrt(var + EPS)
        lane = lax.broadcasted_iota(jnp.int32, (tokens, LANES), 1)
        stat_out[...] = jnp.where(lane == 0, mean, scale)
        for e, offset in enumerate(offsets):
            column = pl.multiple_of((me ^ offset) * wide, LANES)
            if unpack:
                terms = pieces[e, tokens : tokens + PAD_ROWS, :].astype(F32)
                gains[0:1, pl.ds(column, wide)] = terms[0:1] + terms[1:2] + terms[2:3]
                gains[1:2, pl.ds(column, wide)] = terms[3:4] + terms[4:5] + terms[5:6]
            gain = gains[pl.ds(windex, 1), pl.ds(column, wide)]
            hat = (pieces[e, 0:tokens, :].astype(F32) - mean) * scale
            u_out[:, pl.ds(column, wide)] = (hat * gain).astype(BF16)
        contract = (((1,), (1,)), ((), ()))
        if backward:
            z = lax.dot_general(u_out[...], held[...], contract, preferred_element_type=F32)
        else:
            z = lax.dot_general(held[...], u_out[...], contract, preferred_element_type=F32).T
        gelu, slope = gelu_and_slope(z)
        z_out[...] = z
        y_out[...] = (own[...].astype(F32) + gelu).astype(BF16)
    if backward:
        if not forward:
            z = z_ref[...]
            gelu, slope = gelu_and_slope(z)
        dz = (dy_ref[...].astype(F32) * slope).astype(BF16)
        dz_out[...] = dz
        second = jnp.sum(dz.astype(F32) * z, axis=1, keepdims=True)
        first = jnp.zeros((tokens, LANES), F32)
        for n, offset in enumerate(send_order):
            column = pl.multiple_of((me ^ offset) * wide, LANES)
            part = jnp.dot(dz, held[:, pl.ds(column, wide)], preferred_element_type=F32)
            gained = part * gains[pl.ds(windex, 1), pl.ds(column, wide)]
            for c in range(wide // LANES):
                first = first + gained[:, c * LANES : (c + 1) * LANES]
                sent_out[n, c * tokens : (c + 1) * tokens, :] = part[
                    :, c * LANES : (c + 1) * LANES
                ].astype(BF16)
        tail = sums_block(jnp.sum(first, axis=1, keepdims=True), second)
        rows = tokens * (wide // LANES)
        for n in range(len(send_order)):
            sent_out[n, rows : rows + PAD_ROWS, :] = tail


def section_call(scalars, weights, pieces, own, gains, dy, z, offsets, send_order, wide, unpack):
    forward, backward = pieces is not None, dy is not None
    rows, model_width = weights.shape[2:]
    tokens = (own if forward else dy).shape[0]
    operands, specs = [scalars, weights], [SMEM, VMEM]
    for value in (pieces, own, gains, dy, z):
        if value is not None:
            operands.append(value)
            specs.append(VMEM)
    outs = []
    if forward:
        outs += [
            jax.ShapeDtypeStruct((tokens, model_width), BF16),
            jax.ShapeDtypeStruct((tokens, LANES), F32),
            jax.ShapeDtypeStruct((tokens, rows), F32),
            jax.ShapeDtypeStruct((tokens, rows), BF16),
        ]
    if unpack:
        outs.append(jax.ShapeDtypeStruct((2, model_width), F32))
    if backward:
        outs += [
            jax.ShapeDtypeStruct((tokens, rows), BF16),
            jax.ShapeDtypeStruct(
                (len(send_order), tokens * (wide // LANES) + PAD_ROWS, LANES), BF16
            ),
        ]
    flops = 2 * tokens * rows * model_width * (int(forward) + int(backward))
    return pl.pallas_call(
        functools.partial(
            section_kernel,
            offsets,
            (tokens, wide, model_width),
            forward,
            unpack,
            backward,
            send_order,
        ),
        out_shape=outs,
        in_specs=specs,
        out_specs=[VMEM] * len(outs),
        compiler_params=pltpu.CompilerParams(vmem_limit_bytes=VMEM_LIMIT),
        cost_estimate=pl.CostEstimate(
            flops=flops, bytes_accessed=2 * rows * model_width, transcendentals=tokens * rows
        ),
    )(*operands)


def last_kernel(offsets, places, dims, part_count, *refs):
    tokens, wide, model_width, first_size = dims
    scalars, weights, pieces, stat, z_ref, dy_ref = refs[:6]
    refs = refs[6:]
    if part_count:
        parts, (block_ref, next_stat, next_gain), refs = (
            refs[:part_count],
            refs[part_count : part_count + 3],
            refs[part_count + 3 :],
        )
        next_gain_out = refs[-1]
    dz_out, gain_out = refs[0], refs[1 : 1 + first_size]
    me, windex = scalars[0], scalars[1]
    held = weights.at[0, windex]
    dy = dy_ref[...]
    if part_count:
        total = parts[0][...]
        for part in parts[1:]:
            total = total + part[...].astype(F32)
        du, first, second = split_packed(total, tokens, wide)
        dy, gain_grad = input_gradient(
            du,
            first,
            second,
            dy,
            block_ref[...],
            next_stat[:, 0:1],
            next_stat[:, 1:2],
            next_gain[...],
            model_width,
        )
        next_gain_out[...] = gain_grad
    slope = gelu_and_slope(z_ref[...])[1]
    dz = (dy.astype(F32) * slope).astype(BF16)
    dz_out[...] = dz
    mean, scale = stat[:, 0:1], stat[:, 1:2]
    for e, offset in enumerate(offsets):
        column = pl.multiple_of((me ^ offset) * wide, LANES)
        part = jnp.dot(dz, held[:, pl.ds(column, wide)], preferred_element_type=F32)
        hat = (pieces[e, 0:tokens, :].astype(F32) - mean) * scale
        a, b = places[e]
        gain_out[a][b : b + 1, :] = jnp.sum(part * hat, axis=0, keepdims=True)


def last_call(scalars, weights, pieces, stat, z, dy, finish, offsets, send_order, wide, first_size):
    rows, model_width = weights.shape[2:]
    tokens = dy.shape[0]
    rest = len(offsets) // first_size
    places = [divmod(send_order.index(o), rest) for o in offsets]
    operands = [scalars, weights, pieces, stat, z, dy]
    outs = [
        jax.ShapeDtypeStruct((tokens, rows), BF16),
    ] + [jax.ShapeDtypeStruct((rest, wide), F32)] * first_size
    part_count = 0
    if finish is not None:
        parts, others = finish
        part_count = len(parts)
        operands += list(parts) + list(others)
        outs.append(jax.ShapeDtypeStruct((1, rows), F32))
    return pl.pallas_call(
        functools.partial(
            last_kernel,
            offsets,
            places,
            (tokens, wide, model_width, first_size),
            part_count,
        ),
        out_shape=outs,
        in_specs=[SMEM] + [VMEM] * (len(operands) - 1),
        out_specs=[VMEM] * len(outs),
        compiler_params=pltpu.CompilerParams(vmem_limit_bytes=VMEM_LIMIT),
        cost_estimate=pl.CostEstimate(
            flops=2 * tokens * rows * model_width,
            bytes_accessed=2 * rows * model_width,
            transcendentals=tokens * rows,
        ),
    )(*operands)


def weight_grad_kernel(take_early, tiles, *refs):
    scalars, early, early_other, late, late_other, u_own, u_other, _ = refs[:8]
    out, order, result, sems = refs[8:]
    pick = scalars[1] == (0 if take_early else 1)
    mine = jnp.where(pick, early[...], late[...])
    theirs = jnp.where(pick, early_other[...], late_other[...])
    depth = jnp.concatenate([mine, theirs], axis=0).T
    order[...] = jnp.zeros_like(order)
    tile = u_own.shape[1] // tiles
    copies = []
    for n in range(tiles):
        columns = slice(n * tile, (n + 1) * tile)
        both = jnp.concatenate([u_own[:, columns], u_other[:, columns]], axis=0)
        result[:, columns] = jnp.dot(depth, both, preferred_element_type=F32)
        where = pl.ds(n * tile, tile)
        copies.append(pltpu.make_async_copy(result.at[:, where], out.at[:, where], sems.at[n]))
        copies[n].start()
    for copy in copies:
        copy.wait()


def weight_grad_call(scalars, first, dz_a, dz_a_other, dz_b, dz_b_other, u_own, u_other, after):
    tokens, rows = dz_a.shape
    columns = u_own.shape[1]
    tiles = 6
    return pl.pallas_call(
        functools.partial(weight_grad_kernel, first, tiles),
        out_shape=[
            jax.ShapeDtypeStruct((rows, columns), F32),
            jax.ShapeDtypeStruct(after.shape, F32),
        ],
        in_specs=[SMEM] + [VMEM] * 7,
        out_specs=[HBM, VMEM],
        scratch_shapes=[pltpu.VMEM((rows, columns), F32), pltpu.SemaphoreType.DMA((tiles,))],
        compiler_params=pltpu.CompilerParams(vmem_limit_bytes=VMEM_LIMIT),
        cost_estimate=pl.CostEstimate(
            flops=4 * tokens * rows * columns, bytes_accessed=4 * rows * columns, transcendentals=0
        ),
    )(scalars, dz_a, dz_a_other, dz_b, dz_b_other, u_own, u_other, after)


def load_kernel(weights, _, held, sems):
    copies = [
        pltpu.make_async_copy(weights.at[0, n], held.at[0, n], sems.at[n]) for n in range(2)
    ]
    for copy in copies:
        copy.start()
    for copy in copies:
        copy.wait()


def load_call(weights, after):
    return pl.pallas_call(
        load_kernel,
        out_shape=jax.ShapeDtypeStruct(weights.shape, weights.dtype),
        in_specs=[ANY, ANY],
        out_specs=VMEM,
        scratch_shapes=[pltpu.SemaphoreType.DMA((2,))],
        compiler_params=pltpu.CompilerParams(vmem_limit_bytes=VMEM_LIMIT),
        cost_estimate=pl.CostEstimate(
            flops=0, bytes_accessed=2 * weights.size, transcendentals=0
        ),
    )(in_hbm(weights), after)


def pack_kernel(scalars, *refs):
    sources, gains_source, (state, cot, payload), gains, sems = (
        refs[:4],
        refs[4],
        refs[5:8],
        refs[8],
        refs[9],
    )
    tokens = state.shape[0]
    gains_copy = pltpu.make_async_copy(gains_source, gains, sems.at[0])
    gains_copy.start()
    for n in range(2):

        @pl.when(scalars[1] == n)
        def _():
            pltpu.make_async_copy(sources[n], state, sems.at[1]).start()
            pltpu.make_async_copy(sources[2 + n], cot, sems.at[2]).start()

    gains_copy.wait()
    row = lax.broadcasted_iota(jnp.int32, (PAD_ROWS, state.shape[1]), 0)
    block = jnp.zeros((PAD_ROWS, state.shape[1]), F32)
    n = 0
    for section in range(2):
        for term in three_terms(gains[section : section + 1, :]):
            block = jnp.where(row == n, term.astype(F32), block)
            n += 1
    payload[tokens:] = block.astype(BF16)
    pltpu.make_async_copy(sources[0], state, sems.at[1]).wait()
    payload[0:tokens] = state[...]
    pltpu.make_async_copy(sources[2], cot, sems.at[2]).wait()


def pack_call(scalars, down_input, up_input, down_cot, up_cot, gains):
    tokens, block = down_input.shape
    return pl.pallas_call(
        pack_kernel,
        out_shape=[
            jax.ShapeDtypeStruct((tokens, block), BF16),
            jax.ShapeDtypeStruct((tokens, block), BF16),
            jax.ShapeDtypeStruct((tokens + PAD_ROWS, block), BF16),
        ],
        in_specs=[SMEM] + [ANY] * 5,
        out_specs=[VMEM] * 3,
        scratch_shapes=[pltpu.VMEM(gains.shape, F32), pltpu.SemaphoreType.DMA((3,))],
        compiler_params=pltpu.CompilerParams(vmem_limit_bytes=VMEM_LIMIT),
    )(scalars, *map(in_hbm, (down_input, up_input, down_cot, up_cot, gains)))


def keep_live(live, record, previous):
    if previous is None or live is None:
        return record
    return jax.tree.map(lambda fresh, older: jnp.where(live, fresh, older), record, previous)


def per_device(down_input, up_input, down_cot, up_cot, section_weights, section_gains):
    sections = lax.axis_size("section")
    middle = sections // 2
    position = lax.axis_index("section")
    seq_size = lax.axis_size("seq")
    seq_index = lax.axis_index("seq")
    lower = position < middle
    tokens, block = down_input.shape
    model_width = section_weights.shape[3]
    half = model_width // 2
    merged = 0
    while (block << merged) % LANES:
        merged += 1
    wide = block << merged
    bit_count = seq_size.bit_length() - 1
    groups = bit_groups(merged, bit_count)
    back_groups = [group[::-1] for group in groups[::-1]]
    later_groups = groups if sections > 2 else [groups[0][::-1]] + groups[1:]
    offsets = [o >> merged for o in offsets_of(groups)]
    later_offsets = [o >> merged for o in offsets_of(later_groups)]
    send_order = [o >> merged for o in offsets_of(back_groups[::-1])]
    me = (seq_index >> merged).astype(jnp.int32)
    first_index = jnp.where(lower, 0, 1).astype(jnp.int32)
    turn = jnp.minimum(position, sections - 1 - position)

    def index_at(step):
        return first_index if step < middle else 1 - first_index

    def scalars_at(step):
        return jnp.stack([me, index_at(step)]).astype(jnp.int32)

    def live_at(step):
        if sections == 2:
            return None
        return turn == min(step, sections - 1 - step)

    def joined_halves(value, axis):
        for bit in range(merged):
            other = from_xor(value, 1 << bit)
            upper = (seq_index >> bit) & 1
            value = jnp.where(
                upper == 1,
                jnp.concatenate([other, value], axis=axis),
                jnp.concatenate([value, other], axis=axis),
            )
        return value

    def own_part(value, width, bit):
        start = ((seq_index >> bit) & 1) * width
        return (
            lax.dynamic_slice_in_dim(value, start, width, axis=1),
            lax.dynamic_slice_in_dim(value, width - start, width, axis=1),
        )

    def gathered(value, step):
        return gather_xor(joined_halves(value, 1), groups if step == 0 else later_groups)

    def moved(value, step, later):
        low = min(step, sections - 1 - step)
        new = min(later, sections - 1 - later)
        if low == new:
            return value
        route = [(low, new), (sections - 1 - low, sections - 1 - new)]
        return lax.ppermute(value, "section", route)

    def reduced(sent):
        parts = None
        for n, group in enumerate(back_groups):
            sent = sent.reshape((len(group) + 1, -1) + sent.shape[1:])
            parts = reduce_round(sent, group)
            if n + 1 < len(back_groups):
                total = functools.reduce(jnp.add, [p.astype(F32) for p in parts])
                sent = total.astype(BF16)
                kept = total[0]
        parts = [kept if len(back_groups) > 1 else parts[0][0].astype(F32)] + [
            p[0] for p in parts[1:]
        ]
        return parts

    def finished(parts):
        total = functools.reduce(jnp.add, [p.astype(F32) for p in parts])
        du, first, second = split_packed(total, tokens, wide)
        for bit in reversed(range(merged)):
            width = du.shape[1] // 2
            mine, theirs = own_part(du, width, bit)
            tail = jnp.concatenate(two_terms(first) + two_terms(second), axis=1)
            message = jnp.concatenate([theirs.astype(BF16), tail], axis=1)
            message = from_xor(message, 1 << bit).astype(F32)
            du = mine + message[:, :width]
            first = first + message[:, width : width + 1] + message[:, width + 1 : width + 2]
            second = second + message[:, width + 2 : width + 3] + message[:, width + 3 :]
        return du, first, second

    own_gains = section_gains[0]
    state, grad, packed = pack_call(
        scalars_at(0), down_input, up_input, down_cot, up_cot, own_gains
    )
    first_record = second_record = None
    gains = None
    for step in range(sections):
        last = step == sections - 1
        pieces, partly = gathered(packed if step == 0 else state, step)
        if step == 0:
            weights = load_call(section_weights, partly)
        result = section_call(
            scalars_at(step),
            weights,
            pieces,
            state,
            gains,
            grad if last else None,
            None,
            offsets if step == 0 else later_offsets,
            send_order,
            wide,
            step == 0,
        )
        u, stat, z, y = result[:4]
        if step == 0:
            gains = result[4]
        record = (state, pieces[:, :tokens] if sections > 2 else pieces, u, stat, z, y)
        if step < middle:
            first_record = keep_live(live_at(step), record, first_record)
        else:
            second_record = keep_live(live_at(step), record, second_record)
        if last:
            dz, sent = result[-2:]
        else:
            state = moved(y, step, step + 1)
    u_a, y_a = first_record[2], first_record[5]
    u_b, y_b = second_record[2], second_record[5]
    y_other = swapped(y_b)
    down_out = jnp.where(lower, y_a, y_other)
    up_out = jnp.where(lower, y_other, y_a)
    u_first = jnp.where(lower, u_a[:, :half], u_b[:, :half])
    u_second = jnp.where(lower, u_b[:, half:], u_a[:, half:])
    other_first = swapped(jnp.where(lower, u_b[:, :half], u_a[:, :half]))
    other_second = swapped(jnp.where(lower, u_a[:, half:], u_b[:, half:]))
    dz_a = dz_b = gain_b = gain_a = None
    for step in reversed(range(1, sections)):
        source, _, _, stat, z, _ = second_record if step >= middle else first_record
        if step < sections - 1:
            dz, sent = section_call(
                scalars_at(step),
                weights,
                None,
                None,
                gains,
                grad,
                z,
                offsets,
                send_order,
                wide,
                False,
            )
        parts = reduced(sent)
        gain_row = lax.dynamic_slice_in_dim(own_gains, index_at(step), 1, axis=0)
        if step >= middle:
            dz_b = keep_live(live_at(step), dz, dz_b)
        else:
            dz_a = keep_live(live_at(step), dz, dz_a)
        finish = None
        if sections == 2 and not merged:
            finish = (parts, (source, stat, gain_row))
        else:
            du, first, second = finished(parts)
            new_grad, gain_grad = input_gradient(
                du,
                first,
                second,
                grad,
                source,
                stat[:, 0:1],
                stat[:, 1:2],
                gain_row,
                model_width,
            )
            if step >= middle:
                gain_b = keep_live(live_at(step), gain_grad, gain_b)
            else:
                gain_a = keep_live(live_at(step), gain_grad, gain_a)
            grad = moved(new_grad, step, step - 1)
    _, pieces, _, stat, z, _ = first_record
    first_size = len(back_groups[0]) + 1
    result = last_call(
        scalars_at(0),
        weights,
        pieces,
        stat,
        z,
        grad,
        finish,
        offsets,
        send_order,
        wide,
        first_size,
    )
    dz, gain_parts = result[0], result[1 : 1 + first_size]
    if finish is not None:
        gain_b = result[-1]
    dz_a = keep_live(live_at(0), dz, dz_a)
    dz_a_other = swapped(dz_a)
    dz_b_other = swapped(dz_b)
    dz_all = (dz_a, dz_a_other, dz_b, dz_b_other)
    grads = []
    halves = [(True, u_first, other_first), (False, u_second, other_second)]
    for n, group in enumerate(back_groups):
        if n:
            gain_parts = gain_parts.reshape((len(group) + 1, -1) + gain_parts.shape[1:])
        parts = reduce_round(gain_parts, group)
        if halves:
            first, mine, theirs = halves.pop(0)
            grad_half, token = weight_grad_call(
                scalars_at(0), first, *dz_all, mine, theirs, parts[0]
            )
            grads.append(grad_half)
            parts.append(token)
        gain_parts = functools.reduce(jnp.add, parts)
    for first, mine, theirs in halves:
        grads.append(weight_grad_call(scalars_at(0), first, *dz_all, mine, theirs, token)[0])
    grad_first, grad_second = grads
    gain = gain_parts.reshape(1, wide)
    for bit in reversed(range(merged)):
        mine, theirs = own_part(gain, gain.shape[1] // 2, bit)
        gain = mine + from_xor(theirs, 1 << bit)
    gain_a = keep_live(live_at(0), gain, gain_a)
    gain_other = swapped(jnp.where(lower, gain_b, gain_a))
    gain_total = jnp.where(lower, gain_a, gain_b) + gain_other
    return (
        down_out[None],
        up_out[None],
        grad_first[None],
        grad_second[None],
        gain_total,
    )


def solution(mesh):
    in_specs = (
        P(None, "seq"),
        P(None, "seq"),
        P(None, "seq"),
        P(None, "seq"),
        P("section", None, "seq", None),
        P("section", None, "seq"),
    )
    out_specs = (
        P("section", None, "seq"),
        P("section", None, "seq"),
        P("section", "seq", None),
        P("section", "seq", None),
        P("section", "seq"),
    )
    return jax.shard_map(
        per_device, mesh=mesh, in_specs=in_specs, out_specs=out_specs, check_vma=False
    )
```

```python
import functools
import math

import jax
import jax.numpy as jnp
from jax import lax
from jax.experimental import pallas as pl
from jax.experimental.pallas import tpu as pltpu
from jax.sharding import PartitionSpec as P

EPS = 1e-05
F32 = jnp.float32
BF16 = jnp.bfloat16
LANES = 128
PAD_ROWS = 8
SQRT_HALF = math.sqrt(0.5)
INV_SQRT_2PI = 1.0 / math.sqrt(2.0 * math.pi)
VMEM_LIMIT = 32 * 1024 * 1024

VMEM = pl.BlockSpec(memory_space=pltpu.VMEM)
HBM = pl.BlockSpec(memory_space=pltpu.HBM)
ANY = pl.BlockSpec(memory_space=pl.ANY)
SMEM = pl.BlockSpec(memory_space=pltpu.SMEM)


def from_xor(value, distance):
    size = lax.axis_size("seq")
    return lax.ppermute(value, "seq", [(i, i ^ distance) for i in range(size)])


def swapped(value):
    size = lax.axis_size("section")
    return lax.ppermute(value, "section", [(i, size - 1 - i) for i in range(size)])


def bit_groups(low, count):
    bits = [1 << b for b in range(low, count)][::-1]
    groups = []
    while bits:
        pair, bits = bits[:2], bits[2:]
        groups.append(tuple(pair) if len(pair) == 1 else (pair[0], pair[1], pair[0] ^ pair[1]))
    return groups


def offsets_of(groups):
    offsets = [0]
    for group in groups:
        offsets = [o ^ d for d in (0,) + group for o in offsets]
    return offsets


def gather_xor(block, groups):
    held = block[None]
    for n, group in enumerate(groups):
        if n <= 1:
            early = held
        held = jnp.concatenate([held] + [from_xor(held, d) for d in group], axis=0)
    return held, early


def reduce_round(held, group):
    sent = [from_xor(held[n + 1], d) for n, d in enumerate(group)]
    return [held[0]] + sent


def in_hbm(value):
    return pltpu.with_memory_space_constraint(value, pltpu.HBM)


def gelu_and_slope(z):
    cdf = 0.5 * (1.0 + lax.erf(z * SQRT_HALF))
    slope = cdf + z * (jnp.exp(-0.5 * z * z) * INV_SQRT_2PI)
    return z * cdf, slope


def column_to_row(column):
    tokens = column.shape[0]
    rows = lax.broadcasted_iota(jnp.int32, (tokens, LANES), 0)
    lanes = lax.broadcasted_iota(jnp.int32, (tokens, LANES), 1)
    return jnp.sum(jnp.where(rows == lanes, column, 0.0), axis=0, keepdims=True)


def row_to_column(row, tokens):
    rows = lax.broadcasted_iota(jnp.int32, (tokens, LANES), 0)
    lanes = lax.broadcasted_iota(jnp.int32, (tokens, LANES), 1)
    return jnp.sum(jnp.where(rows == lanes, row, 0.0), axis=1, keepdims=True)


def two_terms(value):
    high = value.astype(BF16)
    return high, (value - high.astype(F32)).astype(BF16)


def three_terms(value):
    high, rest = value.astype(BF16), None
    rest = value - high.astype(F32)
    middle = rest.astype(BF16)
    return high, middle, (rest - middle.astype(F32)).astype(BF16)


def sums_block(first_sum, second_sum):
    row = lax.broadcasted_iota(jnp.int32, (PAD_ROWS, LANES), 0)
    block = jnp.zeros((PAD_ROWS, LANES), F32)
    n = 0
    for column in (first_sum, second_sum):
        for term in two_terms(column_to_row(column)):
            block = jnp.where(row == n, term.astype(F32), block)
            n += 1
    return block.astype(BF16)


def split_packed(total, tokens, width):
    chunks = width // LANES
    du = jnp.concatenate([total[c * tokens : (c + 1) * tokens] for c in range(chunks)], axis=1)
    tail = total[chunks * tokens : chunks * tokens + PAD_ROWS]
    first = row_to_column(tail[0:1] + tail[1:2], tokens)
    second = row_to_column(tail[2:3] + tail[3:4], tokens)
    return du, first, second


def input_gradient(du, first_sum, second_sum, dy, block, mean, scale, gain, model_width):
    hat = (block.astype(F32) - mean) * scale
    gained = du * gain
    dx = dy.astype(F32) + scale * (
        gained - first_sum / model_width - hat * (second_sum / model_width)
    )
    return dx.astype(BF16), jnp.sum(du * hat, axis=0, keepdims=True)


def section_kernel(offsets, dims, forward, unpack, backward, send_order, *refs):
    tokens, block, model_width = dims
    refs = list(refs)
    take = refs.pop
    scalars = take(0)
    weights = take(0)
    pieces = take(0) if forward else None
    own = take(0) if forward else None
    gains = None if unpack else take(0)
    dy_ref = take(0) if backward else None
    z_ref = None if forward else take(0)
    if forward:
        u_out, stat_out, z_out, y_out = take(0), take(0), take(0), take(0)
    if unpack:
        gains = take(0)
    if backward:
        dz_out, sent_out = take(0), take(0)
    me, windex = scalars[0], scalars[1]
    held = weights.at[0, windex]
    wide = block
    if forward:
        total = jnp.zeros((tokens, LANES), F32)
        squares = jnp.zeros((tokens, LANES), F32)
        for e in range(len(offsets)):
            for c in range(wide // LANES):
                part = pieces[e, 0:tokens, c * LANES : (c + 1) * LANES].astype(F32)
                total = total + part
                squares = squares + part * part
        mean = jnp.sum(total, axis=1, keepdims=True) / model_width
        var = jnp.sum(squares, axis=1, keepdims=True) / model_width - mean * mean
        scale = lax.rsqrt(var + EPS)
        lane = lax.broadcasted_iota(jnp.int32, (tokens, LANES), 1)
        stat_out[...] = jnp.where(lane == 0, mean, scale)
        for e, offset in enumerate(offsets):
            column = pl.multiple_of((me ^ offset) * wide, LANES)
            if unpack:
                terms = pieces[e, tokens : tokens + PAD_ROWS, :].astype(F32)
                gains[0:1, pl.ds(column, wide)] = terms[0:1] + terms[1:2] + terms[2:3]
                gains[1:2, pl.ds(column, wide)] = terms[3:4] + terms[4:5] + terms[5:6]
            gain = gains[pl.ds(windex, 1), pl.ds(column, wide)]
            hat = (pieces[e, 0:tokens, :].astype(F32) - mean) * scale
            u_out[:, pl.ds(column, wide)] = (hat * gain).astype(BF16)
        contract = (((1,), (1,)), ((), ()))
        if backward:
            z = lax.dot_general(u_out[...], held[...], contract, preferred_element_type=F32)
        else:
            z = lax.dot_general(held[...], u_out[...], contract, preferred_element_type=F32).T
        gelu, slope = gelu_and_slope(z)
        z_out[...] = z
        y_out[...] = (own[...].astype(F32) + gelu).astype(BF16)
    if backward:
        if not forward:
            z = z_ref[...]
            gelu, slope = gelu_and_slope(z)
        dz = (dy_ref[...].astype(F32) * slope).astype(BF16)
        dz_out[...] = dz
        second = jnp.sum(dz.astype(F32) * z, axis=1, keepdims=True)
        first = jnp.zeros((tokens, LANES), F32)
        for n, offset in enumerate(send_order):
            column = pl.multiple_of((me ^ offset) * wide, LANES)
            part = jnp.dot(dz, held[:, pl.ds(column, wide)], preferred_element_type=F32)
            gained = part * gains[pl.ds(windex, 1), pl.ds(column, wide)]
            for c in range(wide // LANES):
                first = first + gained[:, c * LANES : (c + 1) * LANES]
                sent_out[n, c * tokens : (c + 1) * tokens, :] = part[
                    :, c * LANES : (c + 1) * LANES
                ].astype(BF16)
        tail = sums_block(jnp.sum(first, axis=1, keepdims=True), second)
        rows = tokens * (wide // LANES)
        for n in range(len(send_order)):
            sent_out[n, rows : rows + PAD_ROWS, :] = tail


def section_call(scalars, weights, pieces, own, gains, dy, z, offsets, send_order, wide, unpack):
    forward, backward = pieces is not None, dy is not None
    rows, model_width = weights.shape[2:]
    tokens = (own if forward else dy).shape[0]
    operands, specs = [scalars, weights], [SMEM, VMEM]
    for value in (pieces, own, gains, dy, z):
        if value is not None:
            operands.append(value)
            specs.append(VMEM)
    outs = []
    if forward:
        outs += [
            jax.ShapeDtypeStruct((tokens, model_width), BF16),
            jax.ShapeDtypeStruct((tokens, LANES), F32),
            jax.ShapeDtypeStruct((tokens, rows), F32),
            jax.ShapeDtypeStruct((tokens, rows), BF16),
        ]
    if unpack:
        outs.append(jax.ShapeDtypeStruct((2, model_width), F32))
    if backward:
        outs += [
            jax.ShapeDtypeStruct((tokens, rows), BF16),
            jax.ShapeDtypeStruct(
                (len(send_order), tokens * (wide // LANES) + PAD_ROWS, LANES), BF16
            ),
        ]
    flops = 2 * tokens * rows * model_width * (int(forward) + int(backward))
    return pl.pallas_call(
        functools.partial(
            section_kernel,
            offsets,
            (tokens, wide, model_width),
            forward,
            unpack,
            backward,
            send_order,
        ),
        out_shape=outs,
        in_specs=specs,
        out_specs=[VMEM] * len(outs),
        compiler_params=pltpu.CompilerParams(vmem_limit_bytes=VMEM_LIMIT),
        cost_estimate=pl.CostEstimate(
            flops=flops, bytes_accessed=2 * rows * model_width, transcendentals=tokens * rows
        ),
    )(*operands)


def last_kernel(offsets, places, dims, part_count, *refs):
    tokens, wide, model_width, first_size = dims
    scalars, weights, pieces, stat, z_ref, dy_ref = refs[:6]
    refs = refs[7:]
    if part_count:
        parts, (block_ref, next_stat, next_gain), refs = (
            refs[:part_count],
            refs[part_count : part_count + 3],
            refs[part_count + 3 :],
        )
        next_gain_out = refs[-1]
    dz_out, gain_out = refs[0], refs[1 : 1 + first_size]
    me, windex = scalars[0], scalars[1]
    held = weights.at[0, windex]
    dy = dy_ref[...]
    if part_count:
        total = parts[0][...]
        for part in parts[1:]:
            total = total + part[...].astype(F32)
        du, first, second = split_packed(total, tokens, wide)
        dy, gain_grad = input_gradient(
            du,
            first,
            second,
            dy,
            block_ref[...],
            next_stat[:, 0:1],
            next_stat[:, 1:2],
            next_gain[...],
            model_width,
        )
        next_gain_out[...] = gain_grad
    slope = gelu_and_slope(z_ref[...])[1]
    dz = (dy.astype(F32) * slope).astype(BF16)
    dz_out[...] = dz
    mean, scale = stat[:, 0:1], stat[:, 1:2]
    for e, offset in enumerate(offsets):
        column = pl.multiple_of((me ^ offset) * wide, LANES)
        part = jnp.dot(dz, held[:, pl.ds(column, wide)], preferred_element_type=F32)
        hat = (pieces[e, 0:tokens, :].astype(F32) - mean) * scale
        a, b = places[e]
        gain_out[a][b : b + 1, :] = jnp.sum(part * hat, axis=0, keepdims=True)


def last_call(scalars, weights, pieces, stat, z, dy, after, finish, offsets, send_order, wide, first_size):
    rows, model_width = weights.shape[2:]
    tokens = dy.shape[0]
    rest = len(offsets) // first_size
    places = [divmod(send_order.index(o), rest) for o in offsets]
    operands = [scalars, weights, pieces, stat, z, dy, after]
    outs = [
        jax.ShapeDtypeStruct((tokens, rows), BF16),
    ] + [jax.ShapeDtypeStruct((rest, wide), F32)] * first_size
    part_count = 0
    if finish is not None:
        parts, others = finish
        part_count = len(parts)
        operands += list(parts) + list(others)
        outs.append(jax.ShapeDtypeStruct((1, rows), F32))
    return pl.pallas_call(
        functools.partial(
            last_kernel,
            offsets,
            places,
            (tokens, wide, model_width, first_size),
            part_count,
        ),
        out_shape=outs,
        in_specs=[SMEM] + [VMEM] * (len(operands) - 1),
        out_specs=[VMEM] * len(outs),
        compiler_params=pltpu.CompilerParams(vmem_limit_bytes=VMEM_LIMIT),
        cost_estimate=pl.CostEstimate(
            flops=2 * tokens * rows * model_width,
            bytes_accessed=2 * rows * model_width,
            transcendentals=tokens * rows,
        ),
    )(*operands)


def weight_grad_kernel(first_at, tiles, kept, *refs):
    scalars, dz_own, dz_other, u_own, u_other, _ = refs[:6]
    first, second, order, result, sems = refs[6 + kept :]
    tile = u_own.shape[1] // tiles
    depth = jnp.concatenate([dz_own[...], dz_other[...]], axis=0).T
    order[...] = jnp.zeros_like(order)

    def copy(n, target):
        columns = pl.ds(n * tile, tile)
        return pltpu.make_async_copy(result.at[:, columns], target.at[:, columns], sems.at[n])

    for n in range(tiles):
        columns = slice(n * tile, (n + 1) * tile)
        both = jnp.concatenate([u_own[:, columns], u_other[:, columns]], axis=0)
        result[:, columns] = jnp.dot(depth, both, preferred_element_type=F32)

        @pl.when(scalars[1] == first_at)
        def _():
            copy(n, first).start()

        @pl.when(scalars[1] != first_at)
        def _():
            copy(n, second).start()

    for n in range(tiles):
        copy(n, first).wait()


def weight_grad_call(scalars, first_at, dz_own, dz_other, u_own, u_other, after, kept):
    tokens, rows = dz_own.shape
    columns = u_own.shape[1]
    tiles = 4
    return pl.pallas_call(
        functools.partial(weight_grad_kernel, first_at, tiles, len(kept)),
        out_shape=[
            jax.ShapeDtypeStruct((rows, columns), F32),
            jax.ShapeDtypeStruct((rows, columns), F32),
            jax.ShapeDtypeStruct(after.shape, F32),
        ],
        in_specs=[SMEM] + [VMEM] * 5 + [HBM] * len(kept),
        out_specs=[HBM, HBM, VMEM],
        input_output_aliases={6 + n: n for n in range(len(kept))},
        scratch_shapes=[pltpu.VMEM((rows, columns), F32), pltpu.SemaphoreType.DMA((tiles,))],
        compiler_params=pltpu.CompilerParams(vmem_limit_bytes=VMEM_LIMIT),
        cost_estimate=pl.CostEstimate(
            flops=4 * tokens * rows * columns, bytes_accessed=4 * rows * columns, transcendentals=0
        ),
    )(scalars, dz_own, dz_other, u_own, u_other, after, *kept)


def load_kernel(weights, _, held, sems):
    copies = [
        pltpu.make_async_copy(weights.at[0, n], held.at[0, n], sems.at[n]) for n in range(2)
    ]
    for copy in copies:
        copy.start()
    for copy in copies:
        copy.wait()


def load_call(weights, after):
    return pl.pallas_call(
        load_kernel,
        out_shape=jax.ShapeDtypeStruct(weights.shape, weights.dtype),
        in_specs=[ANY, ANY],
        out_specs=VMEM,
        scratch_shapes=[pltpu.SemaphoreType.DMA((2,))],
        compiler_params=pltpu.CompilerParams(vmem_limit_bytes=VMEM_LIMIT),
        cost_estimate=pl.CostEstimate(
            flops=0, bytes_accessed=2 * weights.size, transcendentals=0
        ),
    )(in_hbm(weights), after)


def pack_kernel(scalars, *refs):
    sources, gains_source, (state, cot, payload), gains, sems = (
        refs[:4],
        refs[4],
        refs[5:8],
        refs[8],
        refs[9],
    )
    tokens = state.shape[0]
    gains_copy = pltpu.make_async_copy(gains_source, gains, sems.at[0])
    gains_copy.start()
    for n in range(2):

        @pl.when(scalars[1] == n)
        def _():
            pltpu.make_async_copy(sources[n], state, sems.at[1]).start()
            pltpu.make_async_copy(sources[2 + n], cot, sems.at[2]).start()

    gains_copy.wait()
    row = lax.broadcasted_iota(jnp.int32, (PAD_ROWS, state.shape[1]), 0)
    block = jnp.zeros((PAD_ROWS, state.shape[1]), F32)
    n = 0
    for section in range(2):
        for term in three_terms(gains[section : section + 1, :]):
            block = jnp.where(row == n, term.astype(F32), block)
            n += 1
    payload[tokens:] = block.astype(BF16)
    pltpu.make_async_copy(sources[0], state, sems.at[1]).wait()
    payload[0:tokens] = state[...]
    pltpu.make_async_copy(sources[2], cot, sems.at[2]).wait()


def pack_call(scalars, down_input, up_input, down_cot, up_cot, gains):
    tokens, block = down_input.shape
    return pl.pallas_call(
        pack_kernel,
        out_shape=[
            jax.ShapeDtypeStruct((tokens, block), BF16),
            jax.ShapeDtypeStruct((tokens, block), BF16),
            jax.ShapeDtypeStruct((tokens + PAD_ROWS, block), BF16),
        ],
        in_specs=[SMEM] + [ANY] * 5,
        out_specs=[VMEM] * 3,
        scratch_shapes=[pltpu.VMEM(gains.shape, F32), pltpu.SemaphoreType.DMA((3,))],
        compiler_params=pltpu.CompilerParams(vmem_limit_bytes=VMEM_LIMIT),
    )(scalars, *map(in_hbm, (down_input, up_input, down_cot, up_cot, gains)))


def keep_live(live, record, previous):
    if previous is None or live is None:
        return record
    return jax.tree.map(lambda fresh, older: jnp.where(live, fresh, older), record, previous)


def per_device(down_input, up_input, down_cot, up_cot, section_weights, section_gains):
    sections = lax.axis_size("section")
    middle = sections // 2
    position = lax.axis_index("section")
    seq_size = lax.axis_size("seq")
    seq_index = lax.axis_index("seq")
    lower = position < middle
    tokens, block = down_input.shape
    model_width = section_weights.shape[3]
    half = model_width // 2
    merged = 0
    while (block << merged) % LANES:
        merged += 1
    wide = block << merged
    bit_count = seq_size.bit_length() - 1
    groups = bit_groups(merged, bit_count)
    back_groups = [group[::-1] for group in groups[::-1]]
    later_groups = groups if sections > 2 else [groups[0][::-1]] + groups[1:]
    offsets = [o >> merged for o in offsets_of(groups)]
    later_offsets = [o >> merged for o in offsets_of(later_groups)]
    send_order = [o >> merged for o in offsets_of(back_groups[::-1])]
    me = (seq_index >> merged).astype(jnp.int32)
    first_index = jnp.where(lower, 0, 1).astype(jnp.int32)
    turn = jnp.minimum(position, sections - 1 - position)

    def index_at(step):
        return first_index if step < middle else 1 - first_index

    def scalars_at(step):
        return jnp.stack([me, index_at(step)]).astype(jnp.int32)

    def live_at(step):
        if sections == 2:
            return None
        return turn == min(step, sections - 1 - step)

    def joined_halves(value, axis):
        for bit in range(merged):
            other = from_xor(value, 1 << bit)
            upper = (seq_index >> bit) & 1
            value = jnp.where(
                upper == 1,
                jnp.concatenate([other, value], axis=axis),
                jnp.concatenate([value, other], axis=axis),
            )
        return value

    def own_part(value, width, bit):
        start = ((seq_index >> bit) & 1) * width
        return (
            lax.dynamic_slice_in_dim(value, start, width, axis=1),
            lax.dynamic_slice_in_dim(value, width - start, width, axis=1),
        )

    def gathered(value, step):
        return gather_xor(joined_halves(value, 1), groups if step == 0 else later_groups)

    def moved(value, step, later):
        low = min(step, sections - 1 - step)
        new = min(later, sections - 1 - later)
        if low == new:
            return value
        route = [(low, new), (sections - 1 - low, sections - 1 - new)]
        return lax.ppermute(value, "section", route)

    def reduced(sent):
        parts = None
        for n, group in enumerate(back_groups):
            sent = sent.reshape((len(group) + 1, -1) + sent.shape[1:])
            parts = reduce_round(sent, group)
            if n + 1 < len(back_groups):
                total = functools.reduce(jnp.add, [p.astype(F32) for p in parts])
                sent = total.astype(BF16)
                kept = total[0]
        parts = [kept if len(back_groups) > 1 else parts[0][0].astype(F32)] + [
            p[0] for p in parts[1:]
        ]
        return parts

    def finished(parts):
        total = functools.reduce(jnp.add, [p.astype(F32) for p in parts])
        du, first, second = split_packed(total, tokens, wide)
        for bit in reversed(range(merged)):
            width = du.shape[1] // 2
            mine, theirs = own_part(du, width, bit)
            tail = jnp.concatenate(two_terms(first) + two_terms(second), axis=1)
            message = jnp.concatenate([theirs.astype(BF16), tail], axis=1)
            message = from_xor(message, 1 << bit).astype(F32)
            du = mine + message[:, :width]
            first = first + message[:, width : width + 1] + message[:, width + 1 : width + 2]
            second = second + message[:, width + 2 : width + 3] + message[:, width + 3 :]
        return du, first, second

    own_gains = section_gains[0]
    state, grad, packed = pack_call(
        scalars_at(0), down_input, up_input, down_cot, up_cot, own_gains
    )
    first_record = second_record = None
    gains = None
    for step in range(sections):
        last = step == sections - 1
        pieces, partly = gathered(packed if step == 0 else state, step)
        if step == 0:
            weights = load_call(section_weights, partly)
        result = section_call(
            scalars_at(step),
            weights,
            pieces,
            state,
            gains,
            grad if last else None,
            None,
            offsets if step == 0 else later_offsets,
            send_order,
            wide,
            step == 0,
        )
        u, stat, z, y = result[:4]
        if step == 0:
            gains = result[4]
        record = (state, pieces[:, :tokens] if sections > 2 else pieces, u, stat, z, y)
        if step < middle:
            first_record = keep_live(live_at(step), record, first_record)
        else:
            second_record = keep_live(live_at(step), record, second_record)
        if last:
            dz, sent = result[-2:]
        else:
            state = moved(y, step, step + 1)
    u_a, y_a = first_record[2], first_record[5]
    u_b, y_b = second_record[2], second_record[5]
    y_other = swapped(y_b)
    down_out = jnp.where(lower, y_a, y_other)
    up_out = jnp.where(lower, y_other, y_a)
    needed_a = jnp.where(lower, u_a[:, :half], u_a[:, half:])
    needed_b = jnp.where(lower, u_b[:, half:], u_b[:, :half])
    sent_a = jnp.where(lower, u_a[:, half:], u_a[:, :half])
    other_b = swapped(jnp.where(lower, u_b[:, :half], u_b[:, half:]))

    dz_a = dz_b = gain_b = gain_a = None
    for step in reversed(range(1, sections)):
        source, _, _, stat, z, _ = second_record if step >= middle else first_record
        if step < sections - 1:
            dz, sent = section_call(
                scalars_at(step),
                weights,
                None,
                None,
                gains,
                grad,
                z,
                offsets,
                send_order,
                wide,
                False,
            )
        parts = reduced(sent)
        gain_row = lax.dynamic_slice_in_dim(own_gains, index_at(step), 1, axis=0)
        if step >= middle:
            dz_b = keep_live(live_at(step), dz, dz_b)
        else:
            dz_a = keep_live(live_at(step), dz, dz_a)
        finish = None
        if sections == 2 and not merged:
            finish = (parts, (source, stat, gain_row))
        else:
            du, first, second = finished(parts)
            new_grad, gain_grad = input_gradient(
                du,
                first,
                second,
                grad,
                source,
                stat[:, 0:1],
                stat[:, 1:2],
                gain_row,
                model_width,
            )
            if step >= middle:
                gain_b = keep_live(live_at(step), gain_grad, gain_b)
            else:
                gain_a = keep_live(live_at(step), gain_grad, gain_a)
            grad = moved(new_grad, step, step - 1)
    *early, token = weight_grad_call(
        scalars_at(0), 1, dz_b, swapped(dz_b), needed_b, other_b, jnp.zeros((8, LANES), F32), ()
    )
    _, pieces, _, stat, z, _ = first_record
    first_size = len(back_groups[0]) + 1
    result = last_call(
        scalars_at(0),
        weights,
        pieces,
        stat,
        z,
        grad,
        token,
        finish,
        offsets,
        send_order,
        wide,
        first_size,
    )
    dz, gain_parts = result[0], result[1 : 1 + first_size]
    if finish is not None:
        gain_b = result[-1]
    dz_a = keep_live(live_at(0), dz, dz_a)
    sent_a, dz_a = lax.optimization_barrier((sent_a, dz_a))
    other_a = swapped(sent_a)
    dz_a_other = swapped(dz_a)
    for n, group in enumerate(back_groups):
        if n:
            gain_parts = gain_parts.reshape((len(group) + 1, -1) + gain_parts.shape[1:])
        parts = reduce_round(gain_parts, group)
        if n == 0:
            grad_first, grad_second, token = weight_grad_call(
                scalars_at(0), 0, dz_a, dz_a_other, needed_a, other_a, parts[0], early
            )
            parts.append(token)
        gain_parts = functools.reduce(jnp.add, parts)
    gain = gain_parts.reshape(1, wide)
    for bit in reversed(range(merged)):
        mine, theirs = own_part(gain, gain.shape[1] // 2, bit)
        gain = mine + from_xor(theirs, 1 << bit)
    gain_a = keep_live(live_at(0), gain, gain_a)
    gain_other = swapped(jnp.where(lower, gain_b, gain_a))
    gain_total = jnp.where(lower, gain_a, gain_b) + gain_other
    return (
        down_out[None],
        up_out[None],
        grad_first[None],
        grad_second[None],
        gain_total,
    )


def solution(mesh):
    in_specs = (
        P(None, "seq"),
        P(None, "seq"),
        P(None, "seq"),
        P(None, "seq"),
        P("section", None, "seq", None),
        P("section", None, "seq"),
    )
    out_specs = (
        P("section", None, "seq"),
        P("section", None, "seq"),
        P("section", "seq", None),
        P("section", "seq", None),
        P("section", "seq"),
    )
    return jax.shard_map(
        per_device, mesh=mesh, in_specs=in_specs, out_specs=out_specs, check_vma=False
    )
```

```python
import functools
import math

import jax
import jax.numpy as jnp
from jax import lax
from jax.experimental import pallas as pl
from jax.experimental.pallas import tpu as pltpu
from jax.sharding import PartitionSpec as P

EPS = 1e-05
F32 = jnp.float32
BF16 = jnp.bfloat16
LANES = 128
PAD_ROWS = 8
SQRT_HALF = math.sqrt(0.5)
INV_SQRT_2PI = 1.0 / math.sqrt(2.0 * math.pi)
VMEM_LIMIT = 32 * 1024 * 1024

VMEM = pl.BlockSpec(memory_space=pltpu.VMEM)
HBM = pl.BlockSpec(memory_space=pltpu.HBM)
ANY = pl.BlockSpec(memory_space=pl.ANY)
SMEM = pl.BlockSpec(memory_space=pltpu.SMEM)


def from_xor(value, distance):
    size = lax.axis_size("seq")
    return lax.ppermute(value, "seq", [(i, i ^ distance) for i in range(size)])


def swapped(value):
    size = lax.axis_size("section")
    return lax.ppermute(value, "section", [(i, size - 1 - i) for i in range(size)])


def bit_groups(low, count):
    bits = [1 << b for b in range(low, count)][::-1]
    groups = []
    while bits:
        pair, bits = bits[:2], bits[2:]
        groups.append(tuple(pair) if len(pair) == 1 else (pair[0], pair[1], pair[0] ^ pair[1]))
    return groups


def offsets_of(groups):
    offsets = [0]
    for group in groups:
        offsets = [o ^ d for d in (0,) + group for o in offsets]
    return offsets


def gather_xor(block, groups):
    held = block[None]
    for n, group in enumerate(groups):
        if n <= 1:
            early = held
        held = jnp.concatenate([held] + [from_xor(held, d) for d in group], axis=0)
    return held, early


def reduce_round(held, group):
    sent = [from_xor(held[n + 1], d) for n, d in enumerate(group)]
    return [held[0]] + sent


def in_hbm(value):
    return pltpu.with_memory_space_constraint(value, pltpu.HBM)


def gelu_and_slope(z):
    cdf = 0.5 * (1.0 + lax.erf(z * SQRT_HALF))
    slope = cdf + z * (jnp.exp(-0.5 * z * z) * INV_SQRT_2PI)
    return z * cdf, slope


def column_to_row(column):
    tokens = column.shape[0]
    rows = lax.broadcasted_iota(jnp.int32, (tokens, LANES), 0)
    lanes = lax.broadcasted_iota(jnp.int32, (tokens, LANES), 1)
    return jnp.sum(jnp.where(rows == lanes, column, 0.0), axis=0, keepdims=True)


def row_to_column(row, tokens):
    rows = lax.broadcasted_iota(jnp.int32, (tokens, LANES), 0)
    lanes = lax.broadcasted_iota(jnp.int32, (tokens, LANES), 1)
    return jnp.sum(jnp.where(rows == lanes, row, 0.0), axis=1, keepdims=True)


def two_terms(value):
    high = value.astype(BF16)
    return high, (value - high.astype(F32)).astype(BF16)


def three_terms(value):
    high, rest = value.astype(BF16), None
    rest = value - high.astype(F32)
    middle = rest.astype(BF16)
    return high, middle, (rest - middle.astype(F32)).astype(BF16)


def sums_block(first_sum, second_sum):
    row = lax.broadcasted_iota(jnp.int32, (PAD_ROWS, LANES), 0)
    block = jnp.zeros((PAD_ROWS, LANES), F32)
    n = 0
    for column in (first_sum, second_sum):
        for term in two_terms(column_to_row(column)):
            block = jnp.where(row == n, term.astype(F32), block)
            n += 1
    return block.astype(BF16)


def split_packed(total, tokens, width):
    chunks = width // LANES
    du = jnp.concatenate([total[c * tokens : (c + 1) * tokens] for c in range(chunks)], axis=1)
    tail = total[chunks * tokens : chunks * tokens + PAD_ROWS]
    first = row_to_column(tail[0:1] + tail[1:2], tokens)
    second = row_to_column(tail[2:3] + tail[3:4], tokens)
    return du, first, second


def input_gradient(du, first_sum, second_sum, dy, block, mean, scale, gain, model_width):
    hat = (block.astype(F32) - mean) * scale
    gained = du * gain
    dx = dy.astype(F32) + scale * (
        gained - first_sum / model_width - hat * (second_sum / model_width)
    )
    return dx.astype(BF16), jnp.sum(du * hat, axis=0, keepdims=True)


def section_kernel(offsets, dims, forward, unpack, backward, send_order, *refs):
    tokens, block, model_width = dims
    refs = list(refs)
    take = refs.pop
    scalars = take(0)
    weights = take(0)
    pieces = take(0) if forward else None
    own = take(0) if forward else None
    gains = None if unpack else take(0)
    dy_ref = take(0) if backward else None
    z_ref = None if forward else take(0)
    if forward:
        u_out, stat_out, z_out, y_out = take(0), take(0), take(0), take(0)
    if unpack:
        gains = take(0)
    if backward:
        dz_out, sent_out = take(0), take(0)
    me, windex = scalars[0], scalars[1]
    held = weights.at[0, windex]
    wide = block
    if forward:
        total = jnp.zeros((tokens, LANES), F32)
        squares = jnp.zeros((tokens, LANES), F32)
        for e in range(len(offsets)):
            for c in range(wide // LANES):
                part = pieces[e, 0:tokens, c * LANES : (c + 1) * LANES].astype(F32)
                total = total + part
                squares = squares + part * part
        mean = jnp.sum(total, axis=1, keepdims=True) / model_width
        var = jnp.sum(squares, axis=1, keepdims=True) / model_width - mean * mean
        scale = lax.rsqrt(var + EPS)
        lane = lax.broadcasted_iota(jnp.int32, (tokens, LANES), 1)
        stat_out[...] = jnp.where(lane == 0, mean, scale)
        for e, offset in enumerate(offsets):
            column = pl.multiple_of((me ^ offset) * wide, LANES)
            if unpack:
                terms = pieces[e, tokens : tokens + PAD_ROWS, :].astype(F32)
                gains[0:1, pl.ds(column, wide)] = terms[0:1] + terms[1:2] + terms[2:3]
                gains[1:2, pl.ds(column, wide)] = terms[3:4] + terms[4:5] + terms[5:6]
            gain = gains[pl.ds(windex, 1), pl.ds(column, wide)]
            hat = (pieces[e, 0:tokens, :].astype(F32) - mean) * scale
            u_out[:, pl.ds(column, wide)] = (hat * gain).astype(BF16)
        contract = (((1,), (1,)), ((), ()))
        if backward:
            z = lax.dot_general(u_out[...], held[...], contract, preferred_element_type=F32)
        else:
            z = lax.dot_general(held[...], u_out[...], contract, preferred_element_type=F32).T
        gelu, slope = gelu_and_slope(z)
        z_out[...] = z
        y_out[...] = (own[...].astype(F32) + gelu).astype(BF16)
    if backward:
        if not forward:
            z = z_ref[...]
            gelu, slope = gelu_and_slope(z)
        dz = (dy_ref[...].astype(F32) * slope).astype(BF16)
        dz_out[...] = dz
        second = jnp.sum(dz.astype(F32) * z, axis=1, keepdims=True)
        first = jnp.zeros((tokens, LANES), F32)
        for n, offset in enumerate(send_order):
            column = pl.multiple_of((me ^ offset) * wide, LANES)
            part = jnp.dot(dz, held[:, pl.ds(column, wide)], preferred_element_type=F32)
            gained = part * gains[pl.ds(windex, 1), pl.ds(column, wide)]
            for c in range(wide // LANES):
                first = first + gained[:, c * LANES : (c + 1) * LANES]
                sent_out[n, c * tokens : (c + 1) * tokens, :] = part[
                    :, c * LANES : (c + 1) * LANES
                ].astype(BF16)
        tail = sums_block(jnp.sum(first, axis=1, keepdims=True), second)
        rows = tokens * (wide // LANES)
        for n in range(len(send_order)):
            sent_out[n, rows : rows + PAD_ROWS, :] = tail


def section_call(scalars, weights, pieces, own, gains, dy, z, offsets, send_order, wide, unpack):
    forward, backward = pieces is not None, dy is not None
    rows, model_width = weights.shape[2:]
    tokens = (own if forward else dy).shape[0]
    operands, specs = [scalars, weights], [SMEM, VMEM]
    for value in (pieces, own, gains, dy, z):
        if value is not None:
            operands.append(value)
            specs.append(VMEM)
    outs = []
    if forward:
        outs += [
            jax.ShapeDtypeStruct((tokens, model_width), BF16),
            jax.ShapeDtypeStruct((tokens, LANES), F32),
            jax.ShapeDtypeStruct((tokens, rows), F32),
            jax.ShapeDtypeStruct((tokens, rows), BF16),
        ]
    if unpack:
        outs.append(jax.ShapeDtypeStruct((2, model_width), F32))
    if backward:
        outs += [
            jax.ShapeDtypeStruct((tokens, rows), BF16),
            jax.ShapeDtypeStruct(
                (len(send_order), tokens * (wide // LANES) + PAD_ROWS, LANES), BF16
            ),
        ]
    flops = 2 * tokens * rows * model_width * (int(forward) + int(backward))
    return pl.pallas_call(
        functools.partial(
            section_kernel,
            offsets,
            (tokens, wide, model_width),
            forward,
            unpack,
            backward,
            send_order,
        ),
        out_shape=outs,
        in_specs=specs,
        out_specs=[VMEM] * len(outs),
        compiler_params=pltpu.CompilerParams(vmem_limit_bytes=VMEM_LIMIT),
        cost_estimate=pl.CostEstimate(
            flops=flops, bytes_accessed=2 * rows * model_width, transcendentals=tokens * rows
        ),
    )(*operands)


def last_kernel(offsets, places, dims, part_count, *refs):
    tokens, wide, model_width, first_size = dims
    scalars, weights, pieces, stat, z_ref, dy_ref = refs[:6]
    refs = refs[7:]
    if part_count:
        parts, (block_ref, next_stat, next_gain), refs = (
            refs[:part_count],
            refs[part_count : part_count + 3],
            refs[part_count + 3 :],
        )
        next_gain_out = refs[-1]
    dz_out, gain_out = refs[0], refs[1 : 1 + first_size]
    me, windex = scalars[0], scalars[1]
    held = weights.at[0, windex]
    dy = dy_ref[...]
    if part_count:
        total = parts[0][...]
        for part in parts[1:]:
            total = total + part[...].astype(F32)
        du, first, second = split_packed(total, tokens, wide)
        dy, gain_grad = input_gradient(
            du,
            first,
            second,
            dy,
            block_ref[...],
            next_stat[:, 0:1],
            next_stat[:, 1:2],
            next_gain[...],
            model_width,
        )
        next_gain_out[...] = gain_grad
    slope = gelu_and_slope(z_ref[...])[1]
    dz = (dy.astype(F32) * slope).astype(BF16)
    dz_out[...] = dz
    mean, scale = stat[:, 0:1], stat[:, 1:2]
    for e, offset in enumerate(offsets):
        column = pl.multiple_of((me ^ offset) * wide, LANES)
        part = jnp.dot(dz, held[:, pl.ds(column, wide)], preferred_element_type=F32)
        hat = (pieces[e, 0:tokens, :].astype(F32) - mean) * scale
        a, b = places[e]
        gain_out[a][b : b + 1, :] = jnp.sum(part * hat, axis=0, keepdims=True)


def last_call(scalars, weights, pieces, stat, z, dy, after, finish, offsets, send_order, wide, first_size):
    rows, model_width = weights.shape[2:]
    tokens = dy.shape[0]
    rest = len(offsets) // first_size
    places = [divmod(send_order.index(o), rest) for o in offsets]
    operands = [scalars, weights, pieces, stat, z, dy, after]
    outs = [
        jax.ShapeDtypeStruct((tokens, rows), BF16),
    ] + [jax.ShapeDtypeStruct((rest, wide), F32)] * first_size
    part_count = 0
    if finish is not None:
        parts, others = finish
        part_count = len(parts)
        operands += list(parts) + list(others)
        outs.append(jax.ShapeDtypeStruct((1, rows), F32))
    return pl.pallas_call(
        functools.partial(
            last_kernel,
            offsets,
            places,
            (tokens, wide, model_width, first_size),
            part_count,
        ),
        out_shape=outs,
        in_specs=[SMEM] + [VMEM] * (len(operands) - 1),
        out_specs=[VMEM] * len(outs),
        compiler_params=pltpu.CompilerParams(vmem_limit_bytes=VMEM_LIMIT),
        cost_estimate=pl.CostEstimate(
            flops=2 * tokens * rows * model_width,
            bytes_accessed=2 * rows * model_width,
            transcendentals=tokens * rows,
        ),
    )(*operands)


def weight_grad_kernel(first_at, tiles, kept, *refs):
    scalars, dz_own, dz_other, u_own, u_other, _ = refs[:6]
    first, second, order, result, sems = refs[6 + kept :]
    tile = u_own.shape[1] // tiles
    depth = jnp.concatenate([dz_own[...], dz_other[...]], axis=0).T
    order[...] = jnp.zeros_like(order)

    def copy(n, target):
        columns = pl.ds(n * tile, tile)
        return pltpu.make_async_copy(result.at[:, columns], target.at[:, columns], sems.at[n])

    for n in range(tiles):
        columns = slice(n * tile, (n + 1) * tile)
        both = jnp.concatenate([u_own[:, columns], u_other[:, columns]], axis=0)
        result[:, columns] = jnp.dot(depth, both, preferred_element_type=F32)

        @pl.when(scalars[1] == first_at)
        def _():
            copy(n, first).start()

        @pl.when(scalars[1] != first_at)
        def _():
            copy(n, second).start()

    for n in range(tiles):
        copy(n, first).wait()


def weight_grad_call(scalars, first_at, dz_own, dz_other, u_own, u_other, after, kept):
    tokens, rows = dz_own.shape
    columns = u_own.shape[1]
    tiles = 6
    return pl.pallas_call(
        functools.partial(weight_grad_kernel, first_at, tiles, len(kept)),
        out_shape=[
            jax.ShapeDtypeStruct((rows, columns), F32),
            jax.ShapeDtypeStruct((rows, columns), F32),
            jax.ShapeDtypeStruct(after.shape, F32),
        ],
        in_specs=[SMEM] + [VMEM] * 5 + [HBM] * len(kept),
        out_specs=[HBM, HBM, VMEM],
        input_output_aliases={6 + n: n for n in range(len(kept))},
        scratch_shapes=[pltpu.VMEM((rows, columns), F32), pltpu.SemaphoreType.DMA((tiles,))],
        compiler_params=pltpu.CompilerParams(vmem_limit_bytes=VMEM_LIMIT),
        cost_estimate=pl.CostEstimate(
            flops=4 * tokens * rows * columns, bytes_accessed=4 * rows * columns, transcendentals=0
        ),
    )(scalars, dz_own, dz_other, u_own, u_other, after, *kept)


def load_kernel(weights, _, held, sems):
    copies = [
        pltpu.make_async_copy(weights.at[0, n], held.at[0, n], sems.at[n]) for n in range(2)
    ]
    for copy in copies:
        copy.start()
    for copy in copies:
        copy.wait()


def load_call(weights, after):
    return pl.pallas_call(
        load_kernel,
        out_shape=jax.ShapeDtypeStruct(weights.shape, weights.dtype),
        in_specs=[ANY, ANY],
        out_specs=VMEM,
        scratch_shapes=[pltpu.SemaphoreType.DMA((2,))],
        compiler_params=pltpu.CompilerParams(vmem_limit_bytes=VMEM_LIMIT),
        cost_estimate=pl.CostEstimate(
            flops=0, bytes_accessed=2 * weights.size, transcendentals=0
        ),
    )(in_hbm(weights), after)


def pack_kernel(scalars, *refs):
    sources, gains_source, (state, cot, payload), gains, sems = (
        refs[:4],
        refs[4],
        refs[5:8],
        refs[8],
        refs[9],
    )
    tokens = state.shape[0]
    gains_copy = pltpu.make_async_copy(gains_source, gains, sems.at[0])
    gains_copy.start()
    for n in range(2):

        @pl.when(scalars[1] == n)
        def _():
            pltpu.make_async_copy(sources[n], state, sems.at[1]).start()
            pltpu.make_async_copy(sources[2 + n], cot, sems.at[2]).start()

    gains_copy.wait()
    row = lax.broadcasted_iota(jnp.int32, (PAD_ROWS, state.shape[1]), 0)
    block = jnp.zeros((PAD_ROWS, state.shape[1]), F32)
    n = 0
    for section in range(2):
        for term in three_terms(gains[section : section + 1, :]):
            block = jnp.where(row == n, term.astype(F32), block)
            n += 1
    payload[tokens:] = block.astype(BF16)
    pltpu.make_async_copy(sources[0], state, sems.at[1]).wait()
    payload[0:tokens] = state[...]
    pltpu.make_async_copy(sources[2], cot, sems.at[2]).wait()


def pack_call(scalars, down_input, up_input, down_cot, up_cot, gains):
    tokens, block = down_input.shape
    return pl.pallas_call(
        pack_kernel,
        out_shape=[
            jax.ShapeDtypeStruct((tokens, block), BF16),
            jax.ShapeDtypeStruct((tokens, block), BF16),
            jax.ShapeDtypeStruct((tokens + PAD_ROWS, block), BF16),
        ],
        in_specs=[SMEM] + [ANY] * 5,
        out_specs=[VMEM] * 3,
        scratch_shapes=[pltpu.VMEM(gains.shape, F32), pltpu.SemaphoreType.DMA((3,))],
        compiler_params=pltpu.CompilerParams(vmem_limit_bytes=VMEM_LIMIT),
    )(scalars, *map(in_hbm, (down_input, up_input, down_cot, up_cot, gains)))


def keep_live(live, record, previous):
    if previous is None or live is None:
        return record
    return jax.tree.map(lambda fresh, older: jnp.where(live, fresh, older), record, previous)


def per_device(down_input, up_input, down_cot, up_cot, section_weights, section_gains):
    sections = lax.axis_size("section")
    middle = sections // 2
    position = lax.axis_index("section")
    seq_size = lax.axis_size("seq")
    seq_index = lax.axis_index("seq")
    lower = position < middle
    tokens, block = down_input.shape
    model_width = section_weights.shape[3]
    half = model_width // 2
    merged = 0
    while (block << merged) % LANES:
        merged += 1
    wide = block << merged
    bit_count = seq_size.bit_length() - 1
    groups = bit_groups(merged, bit_count)
    back_groups = [group[::-1] for group in groups[::-1]]
    first_groups = groups if sections > 2 else [groups[0][::-1]] + groups[1:]
    later_groups = groups if sections > 2 else [groups[0][::-1]] + groups[1:]
    offsets = [o >> merged for o in offsets_of(first_groups)]
    later_offsets = [o >> merged for o in offsets_of(later_groups)]
    send_order = [o >> merged for o in offsets_of(back_groups[::-1])]
    me = (seq_index >> merged).astype(jnp.int32)
    first_index = jnp.where(lower, 0, 1).astype(jnp.int32)
    turn = jnp.minimum(position, sections - 1 - position)

    def index_at(step):
        return first_index if step < middle else 1 - first_index

    def scalars_at(step):
        return jnp.stack([me, index_at(step)]).astype(jnp.int32)

    def live_at(step):
        if sections == 2:
            return None
        return turn == min(step, sections - 1 - step)

    def joined_halves(value, axis):
        for bit in range(merged):
            other = from_xor(value, 1 << bit)
            upper = (seq_index >> bit) & 1
            value = jnp.where(
                upper == 1,
                jnp.concatenate([other, value], axis=axis),
                jnp.concatenate([value, other], axis=axis),
            )
        return value

    def own_part(value, width, bit):
        start = ((seq_index >> bit) & 1) * width
        return (
            lax.dynamic_slice_in_dim(value, start, width, axis=1),
            lax.dynamic_slice_in_dim(value, width - start, width, axis=1),
        )

    def gathered(value, step):
        return gather_xor(joined_halves(value, 1), first_groups if step == 0 else later_groups)

    def moved(value, step, later):
        low = min(step, sections - 1 - step)
        new = min(later, sections - 1 - later)
        if low == new:
            return value
        route = [(low, new), (sections - 1 - low, sections - 1 - new)]
        return lax.ppermute(value, "section", route)

    def reduced(sent):
        parts = None
        for n, group in enumerate(back_groups):
            sent = sent.reshape((len(group) + 1, -1) + sent.shape[1:])
            parts = reduce_round(sent, group)
            if n + 1 < len(back_groups):
                total = functools.reduce(jnp.add, [p.astype(F32) for p in parts])
                sent = total.astype(BF16)
                kept = total[0]
        parts = [kept if len(back_groups) > 1 else parts[0][0].astype(F32)] + [
            p[0] for p in parts[1:]
        ]
        return parts

    def finished(parts):
        total = functools.reduce(jnp.add, [p.astype(F32) for p in parts])
        du, first, second = split_packed(total, tokens, wide)
        for bit in reversed(range(merged)):
            width = du.shape[1] // 2
            mine, theirs = own_part(du, width, bit)
            tail = jnp.concatenate(two_terms(first) + two_terms(second), axis=1)
            message = jnp.concatenate([theirs.astype(BF16), tail], axis=1)
            message = from_xor(message, 1 << bit).astype(F32)
            du = mine + message[:, :width]
            first = first + message[:, width : width + 1] + message[:, width + 1 : width + 2]
            second = second + message[:, width + 2 : width + 3] + message[:, width + 3 :]
        return du, first, second

    own_gains = section_gains[0]
    state, grad, packed = pack_call(
        scalars_at(0), down_input, up_input, down_cot, up_cot, own_gains
    )
    first_record = second_record = None
    gains = None
    for step in range(sections):
        last = step == sections - 1
        pieces, partly = gathered(packed if step == 0 else state, step)
        if step == 0:
            weights = load_call(section_weights, partly)
        result = section_call(
            scalars_at(step),
            weights,
            pieces,
            state,
            gains,
            grad if last else None,
            None,
            offsets if step == 0 else later_offsets,
            send_order,
            wide,
            step == 0,
        )
        u, stat, z, y = result[:4]
        if step == 0:
            gains = result[4]
        record = (state, pieces[:, :tokens] if sections > 2 else pieces, u, stat, z, y)
        if step < middle:
            first_record = keep_live(live_at(step), record, first_record)
        else:
            second_record = keep_live(live_at(step), record, second_record)
        if last:
            dz, sent = result[-2:]
        else:
            state = moved(y, step, step + 1)
    u_a, y_a = first_record[2], first_record[5]
    u_b, y_b = second_record[2], second_record[5]
    y_other = swapped(y_b)
    down_out = jnp.where(lower, y_a, y_other)
    up_out = jnp.where(lower, y_other, y_a)
    needed_a = jnp.where(lower, u_a[:, :half], u_a[:, half:])
    needed_b = jnp.where(lower, u_b[:, half:], u_b[:, :half])
    sent_a = jnp.where(lower, u_a[:, half:], u_a[:, :half])
    other_b = swapped(jnp.where(lower, u_b[:, :half], u_b[:, half:]))

    dz_a = dz_b = gain_b = gain_a = None
    for step in reversed(range(1, sections)):
        source, _, _, stat, z, _ = second_record if step >= middle else first_record
        if step < sections - 1:
            dz, sent = section_call(
                scalars_at(step),
                weights,
                None,
                None,
                gains,
                grad,
                z,
                offsets,
                send_order,
                wide,
                False,
            )
        parts = reduced(sent)
        gain_row = lax.dynamic_slice_in_dim(own_gains, index_at(step), 1, axis=0)
        if step >= middle:
            dz_b = keep_live(live_at(step), dz, dz_b)
        else:
            dz_a = keep_live(live_at(step), dz, dz_a)
        finish = None
        if sections == 2 and not merged:
            finish = (parts, (source, stat, gain_row))
        else:
            du, first, second = finished(parts)
            new_grad, gain_grad = input_gradient(
                du,
                first,
                second,
                grad,
                source,
                stat[:, 0:1],
                stat[:, 1:2],
                gain_row,
                model_width,
            )
            if step >= middle:
                gain_b = keep_live(live_at(step), gain_grad, gain_b)
            else:
                gain_a = keep_live(live_at(step), gain_grad, gain_a)
            grad = moved(new_grad, step, step - 1)
    *early, token = weight_grad_call(
        scalars_at(0), 1, dz_b, swapped(dz_b), needed_b, other_b, jnp.zeros((8, LANES), F32), ()
    )
    token, down_out, up_out = lax.optimization_barrier((token, down_out, up_out))
    _, pieces, _, stat, z, _ = first_record
    first_size = len(back_groups[0]) + 1
    result = last_call(
        scalars_at(0),
        weights,
        pieces,
        stat,
        z,
        grad,
        token,
        finish,
        offsets,
        send_order,
        wide,
        first_size,
    )
    dz, gain_parts = result[0], result[1 : 1 + first_size]
    if finish is not None:
        gain_b = result[-1]
    dz_a = keep_live(live_at(0), dz, dz_a)
    sent_a, dz_a = lax.optimization_barrier((sent_a, dz_a))
    other_a = swapped(sent_a)
    dz_a_other = swapped(dz_a)
    for n, group in enumerate(back_groups):
        if n:
            gain_parts = gain_parts.reshape((len(group) + 1, -1) + gain_parts.shape[1:])
        parts = reduce_round(gain_parts, group)
        if n == 0:
            grad_first, grad_second, token = weight_grad_call(
                scalars_at(0), 0, dz_a, dz_a_other, needed_a, other_a, parts[0], early
            )
            parts.append(token)
        gain_parts = functools.reduce(jnp.add, parts)
    gain = gain_parts.reshape(1, wide)
    for bit in reversed(range(merged)):
        mine, theirs = own_part(gain, gain.shape[1] // 2, bit)
        gain = mine + from_xor(theirs, 1 << bit)
    gain_a = keep_live(live_at(0), gain, gain_a)
    gain_other = swapped(jnp.where(lower, gain_b, gain_a))
    gain_total = jnp.where(lower, gain_a, gain_b) + gain_other
    return (
        down_out[None],
        up_out[None],
        grad_first[None],
        grad_second[None],
        gain_total,
    )


def solution(mesh):
    in_specs = (
        P(None, "seq"),
        P(None, "seq"),
        P(None, "seq"),
        P(None, "seq"),
        P("section", None, "seq", None),
        P("section", None, "seq"),
    )
    out_specs = (
        P("section", None, "seq"),
        P("section", None, "seq"),
        P("section", "seq", None),
        P("section", "seq", None),
        P("section", "seq"),
    )
    return jax.shard_map(
        per_device, mesh=mesh, in_specs=in_specs, out_specs=out_specs, check_vma=False
    )
```

```python
import functools
import math

import jax
import jax.numpy as jnp
from jax import lax
from jax.experimental import pallas as pl
from jax.experimental.pallas import tpu as pltpu
from jax.sharding import PartitionSpec as P

EPS = 1e-05
F32 = jnp.float32
BF16 = jnp.bfloat16
LANES = 128
PAD_ROWS = 8
SQRT_HALF = math.sqrt(0.5)
INV_SQRT_2PI = 1.0 / math.sqrt(2.0 * math.pi)
VMEM_LIMIT = 32 * 1024 * 1024

VMEM = pl.BlockSpec(memory_space=pltpu.VMEM)
HBM = pl.BlockSpec(memory_space=pltpu.HBM)
ANY = pl.BlockSpec(memory_space=pl.ANY)
SMEM = pl.BlockSpec(memory_space=pltpu.SMEM)


def from_xor(value, distance):
    size = lax.axis_size("seq")
    return lax.ppermute(value, "seq", [(i, i ^ distance) for i in range(size)])


def swapped(value):
    size = lax.axis_size("section")
    return lax.ppermute(value, "section", [(i, size - 1 - i) for i in range(size)])


def bit_groups(low, count):
    bits = [1 << b for b in range(low, count)][::-1]
    groups = []
    while bits:
        pair, bits = bits[:2], bits[2:]
        groups.append(tuple(pair) if len(pair) == 1 else (pair[0], pair[1], pair[0] ^ pair[1]))
    return groups


def offsets_of(groups):
    offsets = [0]
    for group in groups:
        offsets = [o ^ d for d in (0,) + group for o in offsets]
    return offsets


def gather_xor(block, groups):
    held = block[None]
    for n, group in enumerate(groups):
        if n <= 1:
            early = held
        held = jnp.concatenate([held] + [from_xor(held, d) for d in group], axis=0)
    return held, early


def reduce_round(held, group):
    sent = [from_xor(held[n + 1], d) for n, d in enumerate(group)]
    return [held[0]] + sent


def in_hbm(value):
    return pltpu.with_memory_space_constraint(value, pltpu.HBM)


def gelu_and_slope(z):
    cdf = 0.5 * (1.0 + lax.erf(z * SQRT_HALF))
    slope = cdf + z * (jnp.exp(-0.5 * z * z) * INV_SQRT_2PI)
    return z * cdf, slope


def column_to_row(column):
    tokens = column.shape[0]
    rows = lax.broadcasted_iota(jnp.int32, (tokens, LANES), 0)
    lanes = lax.broadcasted_iota(jnp.int32, (tokens, LANES), 1)
    return jnp.sum(jnp.where(rows == lanes, column, 0.0), axis=0, keepdims=True)


def row_to_column(row, tokens):
    rows = lax.broadcasted_iota(jnp.int32, (tokens, LANES), 0)
    lanes = lax.broadcasted_iota(jnp.int32, (tokens, LANES), 1)
    return jnp.sum(jnp.where(rows == lanes, row, 0.0), axis=1, keepdims=True)


def two_terms(value):
    high = value.astype(BF16)
    return high, (value - high.astype(F32)).astype(BF16)


def three_terms(value):
    high, rest = value.astype(BF16), None
    rest = value - high.astype(F32)
    middle = rest.astype(BF16)
    return high, middle, (rest - middle.astype(F32)).astype(BF16)


def sums_block(first_sum, second_sum):
    row = lax.broadcasted_iota(jnp.int32, (PAD_ROWS, LANES), 0)
    block = jnp.zeros((PAD_ROWS, LANES), F32)
    n = 0
    for column in (first_sum, second_sum):
        for term in two_terms(column_to_row(column)):
            block = jnp.where(row == n, term.astype(F32), block)
            n += 1
    return block.astype(BF16)


def split_packed(total, tokens, width):
    chunks = width // LANES
    du = jnp.concatenate([total[c * tokens : (c + 1) * tokens] for c in range(chunks)], axis=1)
    tail = total[chunks * tokens : chunks * tokens + PAD_ROWS]
    first = row_to_column(tail[0:1] + tail[1:2], tokens)
    second = row_to_column(tail[2:3] + tail[3:4], tokens)
    return du, first, second


def input_gradient(du, first_sum, second_sum, dy, block, mean, scale, gain, model_width):
    hat = (block.astype(F32) - mean) * scale
    gained = du * gain
    dx = dy.astype(F32) + scale * (
        gained - first_sum / model_width - hat * (second_sum / model_width)
    )
    return dx.astype(BF16), jnp.sum(du * hat, axis=0, keepdims=True)


def section_kernel(offsets, dims, forward, unpack, backward, send_order, *refs):
    tokens, block, model_width = dims
    refs = list(refs)
    take = refs.pop
    scalars = take(0)
    weights = take(0)
    pieces = take(0) if forward else None
    own = take(0) if forward else None
    gains = None if unpack else take(0)
    dy_ref = take(0) if backward else None
    z_ref = None if forward else take(0)
    if forward:
        u_out, stat_out, z_out, y_out = take(0), take(0), take(0), take(0)
    if unpack:
        gains = take(0)
    if backward:
        dz_out, sent_out = take(0), take(0)
    me, windex = scalars[0], scalars[1]
    held = weights.at[0, windex]
    wide = block
    if forward:
        total = jnp.zeros((tokens, LANES), F32)
        squares = jnp.zeros((tokens, LANES), F32)
        for e in range(len(offsets)):
            for c in range(wide // LANES):
                part = pieces[e, 0:tokens, c * LANES : (c + 1) * LANES].astype(F32)
                total = total + part
                squares = squares + part * part
        mean = jnp.sum(total, axis=1, keepdims=True) / model_width
        var = jnp.sum(squares, axis=1, keepdims=True) / model_width - mean * mean
        scale = lax.rsqrt(var + EPS)
        lane = lax.broadcasted_iota(jnp.int32, (tokens, LANES), 1)
        stat_out[...] = jnp.where(lane == 0, mean, scale)
        for e, offset in enumerate(offsets):
            column = pl.multiple_of((me ^ offset) * wide, LANES)
            if unpack:
                terms = pieces[e, tokens : tokens + PAD_ROWS, :].astype(F32)
                gains[0:1, pl.ds(column, wide)] = terms[0:1] + terms[1:2] + terms[2:3]
                gains[1:2, pl.ds(column, wide)] = terms[3:4] + terms[4:5] + terms[5:6]
            gain = gains[pl.ds(windex, 1), pl.ds(column, wide)]
            hat = (pieces[e, 0:tokens, :].astype(F32) - mean) * scale
            u_out[:, pl.ds(column, wide)] = (hat * gain).astype(BF16)
        contract = (((1,), (1,)), ((), ()))
        if backward:
            z = lax.dot_general(u_out[...], held[...], contract, preferred_element_type=F32)
        else:
            z = lax.dot_general(held[...], u_out[...], contract, preferred_element_type=F32).T
        gelu, slope = gelu_and_slope(z)
        z_out[...] = z
        y_out[...] = (own[...].astype(F32) + gelu).astype(BF16)
    if backward:
        if not forward:
            z = z_ref[...]
            gelu, slope = gelu_and_slope(z)
        dz = (dy_ref[...].astype(F32) * slope).astype(BF16)
        dz_out[...] = dz
        second = jnp.sum(dz.astype(F32) * z, axis=1, keepdims=True)
        first = jnp.zeros((tokens, LANES), F32)
        for n, offset in enumerate(send_order):
            column = pl.multiple_of((me ^ offset) * wide, LANES)
            part = jnp.dot(dz, held[:, pl.ds(column, wide)], preferred_element_type=F32)
            gained = part * gains[pl.ds(windex, 1), pl.ds(column, wide)]
            for c in range(wide // LANES):
                first = first + gained[:, c * LANES : (c + 1) * LANES]
                sent_out[n, c * tokens : (c + 1) * tokens, :] = part[
                    :, c * LANES : (c + 1) * LANES
                ].astype(BF16)
        tail = sums_block(jnp.sum(first, axis=1, keepdims=True), second)
        rows = tokens * (wide // LANES)
        for n in range(len(send_order)):
            sent_out[n, rows : rows + PAD_ROWS, :] = tail


def section_call(scalars, weights, pieces, own, gains, dy, z, offsets, send_order, wide, unpack):
    forward, backward = pieces is not None, dy is not None
    rows, model_width = weights.shape[2:]
    tokens = (own if forward else dy).shape[0]
    operands, specs = [scalars, weights], [SMEM, VMEM]
    for value in (pieces, own, gains, dy, z):
        if value is not None:
            operands.append(value)
            specs.append(VMEM)
    outs = []
    if forward:
        outs += [
            jax.ShapeDtypeStruct((tokens, model_width), BF16),
            jax.ShapeDtypeStruct((tokens, LANES), F32),
            jax.ShapeDtypeStruct((tokens, rows), F32),
            jax.ShapeDtypeStruct((tokens, rows), BF16),
        ]
    if unpack:
        outs.append(jax.ShapeDtypeStruct((2, model_width), F32))
    if backward:
        outs += [
            jax.ShapeDtypeStruct((tokens, rows), BF16),
            jax.ShapeDtypeStruct(
                (len(send_order), tokens * (wide // LANES) + PAD_ROWS, LANES), BF16
            ),
        ]
    flops = 2 * tokens * rows * model_width * (int(forward) + int(backward))
    return pl.pallas_call(
        functools.partial(
            section_kernel,
            offsets,
            (tokens, wide, model_width),
            forward,
            unpack,
            backward,
            send_order,
        ),
        out_shape=outs,
        in_specs=specs,
        out_specs=[VMEM] * len(outs),
        compiler_params=pltpu.CompilerParams(vmem_limit_bytes=VMEM_LIMIT),
        cost_estimate=pl.CostEstimate(
            flops=flops, bytes_accessed=2 * rows * model_width, transcendentals=tokens * rows
        ),
    )(*operands)


def last_kernel(offsets, places, dims, part_count, *refs):
    tokens, wide, model_width, first_size = dims
    scalars, weights, pieces, stat, z_ref, dy_ref = refs[:6]
    refs = refs[7:]
    if part_count:
        parts, (block_ref, next_stat, next_gain), refs = (
            refs[:part_count],
            refs[part_count : part_count + 3],
            refs[part_count + 3 :],
        )
        next_gain_out = refs[-1]
    dz_out, gain_out = refs[0], refs[1 : 1 + first_size]
    me, windex = scalars[0], scalars[1]
    held = weights.at[0, windex]
    dy = dy_ref[...]
    if part_count:
        total = parts[0][...]
        for part in parts[1:]:
            total = total + part[...].astype(F32)
        du, first, second = split_packed(total, tokens, wide)
        dy, gain_grad = input_gradient(
            du,
            first,
            second,
            dy,
            block_ref[...],
            next_stat[:, 0:1],
            next_stat[:, 1:2],
            next_gain[...],
            model_width,
        )
        next_gain_out[...] = gain_grad
    slope = gelu_and_slope(z_ref[...])[1]
    dz = (dy.astype(F32) * slope).astype(BF16)
    dz_out[...] = dz
    mean, scale = stat[:, 0:1], stat[:, 1:2]
    for e, offset in enumerate(offsets):
        column = pl.multiple_of((me ^ offset) * wide, LANES)
        part = jnp.dot(dz, held[:, pl.ds(column, wide)], preferred_element_type=F32)
        hat = (pieces[e, 0:tokens, :].astype(F32) - mean) * scale
        a, b = places[e]
        gain_out[a][b : b + 1, :] = jnp.sum(part * hat, axis=0, keepdims=True)


def last_call(scalars, weights, pieces, stat, z, dy, after, finish, offsets, send_order, wide, first_size):
    rows, model_width = weights.shape[2:]
    tokens = dy.shape[0]
    rest = len(offsets) // first_size
    places = [divmod(send_order.index(o), rest) for o in offsets]
    operands = [scalars, weights, pieces, stat, z, dy, after]
    outs = [
        jax.ShapeDtypeStruct((tokens, rows), BF16),
    ] + [jax.ShapeDtypeStruct((rest, wide), F32)] * first_size
    part_count = 0
    if finish is not None:
        parts, others = finish
        part_count = len(parts)
        operands += list(parts) + list(others)
        outs.append(jax.ShapeDtypeStruct((1, rows), F32))
    return pl.pallas_call(
        functools.partial(
            last_kernel,
            offsets,
            places,
            (tokens, wide, model_width, first_size),
            part_count,
        ),
        out_shape=outs,
        in_specs=[SMEM] + [VMEM] * (len(operands) - 1),
        out_specs=[VMEM] * len(outs),
        compiler_params=pltpu.CompilerParams(vmem_limit_bytes=VMEM_LIMIT),
        cost_estimate=pl.CostEstimate(
            flops=2 * tokens * rows * model_width,
            bytes_accessed=2 * rows * model_width,
            transcendentals=tokens * rows,
        ),
    )(*operands)


def weight_grad_kernel(first_at, tiles, kept, *refs):
    scalars, dz_own, dz_other, u_own, u_other, _ = refs[:6]
    first, second, order, result, sems = refs[6 + kept :]
    tile = u_own.shape[1] // tiles
    depth = jnp.concatenate([dz_own[...], dz_other[...]], axis=0).T
    order[...] = jnp.zeros_like(order)

    def copy(n, target):
        columns = pl.ds(n * tile, tile)
        return pltpu.make_async_copy(result.at[:, columns], target.at[:, columns], sems.at[n])

    for n in range(tiles):
        columns = slice(n * tile, (n + 1) * tile)
        both = jnp.concatenate([u_own[:, columns], u_other[:, columns]], axis=0)
        result[:, columns] = jnp.dot(depth, both, preferred_element_type=F32)

        @pl.when(scalars[1] == first_at)
        def _():
            copy(n, first).start()

        @pl.when(scalars[1] != first_at)
        def _():
            copy(n, second).start()

    for n in range(tiles):
        copy(n, first).wait()


def weight_grad_call(scalars, first_at, dz_own, dz_other, u_own, u_other, after, kept):
    tokens, rows = dz_own.shape
    columns = u_own.shape[1]
    tiles = 4
    return pl.pallas_call(
        functools.partial(weight_grad_kernel, first_at, tiles, len(kept)),
        out_shape=[
            jax.ShapeDtypeStruct((rows, columns), F32),
            jax.ShapeDtypeStruct((rows, columns), F32),
            jax.ShapeDtypeStruct(after.shape, F32),
        ],
        in_specs=[SMEM] + [VMEM] * 5 + [HBM] * len(kept),
        out_specs=[HBM, HBM, VMEM],
        input_output_aliases={6 + n: n for n in range(len(kept))},
        scratch_shapes=[pltpu.VMEM((rows, columns), F32), pltpu.SemaphoreType.DMA((tiles,))],
        compiler_params=pltpu.CompilerParams(vmem_limit_bytes=VMEM_LIMIT),
        cost_estimate=pl.CostEstimate(
            flops=4 * tokens * rows * columns, bytes_accessed=4 * rows * columns, transcendentals=0
        ),
    )(scalars, dz_own, dz_other, u_own, u_other, after, *kept)


def load_kernel(weights, _, held, sems):
    copies = [
        pltpu.make_async_copy(weights.at[0, n], held.at[0, n], sems.at[n]) for n in range(2)
    ]
    for copy in copies:
        copy.start()
    for copy in copies:
        copy.wait()


def load_call(weights, after):
    return pl.pallas_call(
        load_kernel,
        out_shape=jax.ShapeDtypeStruct(weights.shape, weights.dtype),
        in_specs=[ANY, ANY],
        out_specs=VMEM,
        scratch_shapes=[pltpu.SemaphoreType.DMA((2,))],
        compiler_params=pltpu.CompilerParams(vmem_limit_bytes=VMEM_LIMIT),
        cost_estimate=pl.CostEstimate(
            flops=0, bytes_accessed=2 * weights.size, transcendentals=0
        ),
    )(in_hbm(weights), after)


def pack_kernel(scalars, *refs):
    sources, gains_source, (state, cot, payload), gains, sems = (
        refs[:4],
        refs[4],
        refs[5:8],
        refs[8],
        refs[9],
    )
    tokens = state.shape[0]
    gains_copy = pltpu.make_async_copy(gains_source, gains, sems.at[0])
    gains_copy.start()
    for n in range(2):

        @pl.when(scalars[1] == n)
        def _():
            pltpu.make_async_copy(sources[n], state, sems.at[1]).start()
            pltpu.make_async_copy(sources[2 + n], cot, sems.at[2]).start()

    gains_copy.wait()
    row = lax.broadcasted_iota(jnp.int32, (PAD_ROWS, state.shape[1]), 0)
    block = jnp.zeros((PAD_ROWS, state.shape[1]), F32)
    n = 0
    for section in range(2):
        for term in three_terms(gains[section : section + 1, :]):
            block = jnp.where(row == n, term.astype(F32), block)
            n += 1
    payload[tokens:] = block.astype(BF16)
    pltpu.make_async_copy(sources[0], state, sems.at[1]).wait()
    payload[0:tokens] = state[...]
    pltpu.make_async_copy(sources[2], cot, sems.at[2]).wait()


def pack_call(scalars, down_input, up_input, down_cot, up_cot, gains):
    tokens, block = down_input.shape
    return pl.pallas_call(
        pack_kernel,
        out_shape=[
            jax.ShapeDtypeStruct((tokens, block), BF16),
            jax.ShapeDtypeStruct((tokens, block), BF16),
            jax.ShapeDtypeStruct((tokens + PAD_ROWS, block), BF16),
        ],
        in_specs=[SMEM] + [ANY] * 5,
        out_specs=[VMEM] * 3,
        scratch_shapes=[pltpu.VMEM(gains.shape, F32), pltpu.SemaphoreType.DMA((3,))],
        compiler_params=pltpu.CompilerParams(vmem_limit_bytes=VMEM_LIMIT),
    )(scalars, *map(in_hbm, (down_input, up_input, down_cot, up_cot, gains)))


def keep_live(live, record, previous):
    if previous is None or live is None:
        return record
    return jax.tree.map(lambda fresh, older: jnp.where(live, fresh, older), record, previous)


def per_device(down_input, up_input, down_cot, up_cot, section_weights, section_gains):
    sections = lax.axis_size("section")
    middle = sections // 2
    position = lax.axis_index("section")
    seq_size = lax.axis_size("seq")
    seq_index = lax.axis_index("seq")
    lower = position < middle
    tokens, block = down_input.shape
    model_width = section_weights.shape[3]
    half = model_width // 2
    merged = 0
    while (block << merged) % LANES:
        merged += 1
    wide = block << merged
    bit_count = seq_size.bit_length() - 1
    groups = bit_groups(merged, bit_count)
    back_groups = [group[::-1] for group in groups[::-1]]
    first_groups = groups if sections > 2 else [groups[0][::-1]] + groups[1:]
    later_groups = groups if sections > 2 else [groups[0][::-1]] + groups[1:]
    offsets = [o >> merged for o in offsets_of(first_groups)]
    later_offsets = [o >> merged for o in offsets_of(later_groups)]
    send_order = [o >> merged for o in offsets_of(back_groups[::-1])]
    me = (seq_index >> merged).astype(jnp.int32)
    first_index = jnp.where(lower, 0, 1).astype(jnp.int32)
    turn = jnp.minimum(position, sections - 1 - position)

    def index_at(step):
        return first_index if step < middle else 1 - first_index

    def scalars_at(step):
        return jnp.stack([me, index_at(step)]).astype(jnp.int32)

    def live_at(step):
        if sections == 2:
            return None
        return turn == min(step, sections - 1 - step)

    def joined_halves(value, axis):
        for bit in range(merged):
            other = from_xor(value, 1 << bit)
            upper = (seq_index >> bit) & 1
            value = jnp.where(
                upper == 1,
                jnp.concatenate([other, value], axis=axis),
                jnp.concatenate([value, other], axis=axis),
            )
        return value

    def own_part(value, width, bit):
        start = ((seq_index >> bit) & 1) * width
        return (
            lax.dynamic_slice_in_dim(value, start, width, axis=1),
            lax.dynamic_slice_in_dim(value, width - start, width, axis=1),
        )

    def gathered(value, step):
        return gather_xor(joined_halves(value, 1), first_groups if step == 0 else later_groups)

    def moved(value, step, later):
        low = min(step, sections - 1 - step)
        new = min(later, sections - 1 - later)
        if low == new:
            return value
        route = [(low, new), (sections - 1 - low, sections - 1 - new)]
        return lax.ppermute(value, "section", route)

    def reduced(sent):
        parts = None
        for n, group in enumerate(back_groups):
            sent = sent.reshape((len(group) + 1, -1) + sent.shape[1:])
            parts = reduce_round(sent, group)
            if n + 1 < len(back_groups):
                total = functools.reduce(jnp.add, [p.astype(F32) for p in parts])
                sent = total.astype(BF16)
                kept = total[0]
        parts = [kept if len(back_groups) > 1 else parts[0][0].astype(F32)] + [
            p[0] for p in parts[1:]
        ]
        return parts

    def finished(parts):
        total = functools.reduce(jnp.add, [p.astype(F32) for p in parts])
        du, first, second = split_packed(total, tokens, wide)
        for bit in reversed(range(merged)):
            width = du.shape[1] // 2
            mine, theirs = own_part(du, width, bit)
            tail = jnp.concatenate(two_terms(first) + two_terms(second), axis=1)
            message = jnp.concatenate([theirs.astype(BF16), tail], axis=1)
            message = from_xor(message, 1 << bit).astype(F32)
            du = mine + message[:, :width]
            first = first + message[:, width : width + 1] + message[:, width + 1 : width + 2]
            second = second + message[:, width + 2 : width + 3] + message[:, width + 3 :]
        return du, first, second

    own_gains = section_gains[0]
    state, grad, packed = pack_call(
        scalars_at(0), down_input, up_input, down_cot, up_cot, own_gains
    )
    first_record = second_record = None
    gains = None
    for step in range(sections):
        last = step == sections - 1
        pieces, partly = gathered(packed if step == 0 else state, step)
        if step == 0:
            weights = load_call(section_weights, partly)
        result = section_call(
            scalars_at(step),
            weights,
            pieces,
            state,
            gains,
            grad if last else None,
            None,
            offsets if step == 0 else later_offsets,
            send_order,
            wide,
            step == 0,
        )
        u, stat, z, y = result[:4]
        if step == 0:
            gains = result[4]
        record = (state, pieces[:, :tokens] if sections > 2 else pieces, u, stat, z, y)
        if step < middle:
            first_record = keep_live(live_at(step), record, first_record)
        else:
            second_record = keep_live(live_at(step), record, second_record)
        if last:
            dz, sent = result[-2:]
        else:
            state = moved(y, step, step + 1)
    u_a, y_a = first_record[2], first_record[5]
    u_b, y_b = second_record[2], second_record[5]
    y_other = swapped(y_b)
    down_out = jnp.where(lower, y_a, y_other)
    up_out = jnp.where(lower, y_other, y_a)
    needed_a = jnp.where(lower, u_a[:, :half], u_a[:, half:])
    needed_b = jnp.where(lower, u_b[:, half:], u_b[:, :half])
    sent_a = jnp.where(lower, u_a[:, half:], u_a[:, :half])
    other_b = swapped(jnp.where(lower, u_b[:, :half], u_b[:, half:]))

    dz_a = dz_b = gain_b = gain_a = None
    for step in reversed(range(1, sections)):
        source, _, _, stat, z, _ = second_record if step >= middle else first_record
        if step < sections - 1:
            dz, sent = section_call(
                scalars_at(step),
                weights,
                None,
                None,
                gains,
                grad,
                z,
                offsets,
                send_order,
                wide,
                False,
            )
        parts = reduced(sent)
        gain_row = lax.dynamic_slice_in_dim(own_gains, index_at(step), 1, axis=0)
        if step >= middle:
            dz_b = keep_live(live_at(step), dz, dz_b)
        else:
            dz_a = keep_live(live_at(step), dz, dz_a)
        finish = None
        if sections == 2 and not merged:
            finish = (parts, (source, stat, gain_row))
        else:
            du, first, second = finished(parts)
            new_grad, gain_grad = input_gradient(
                du,
                first,
                second,
                grad,
                source,
                stat[:, 0:1],
                stat[:, 1:2],
                gain_row,
                model_width,
            )
            if step >= middle:
                gain_b = keep_live(live_at(step), gain_grad, gain_b)
            else:
                gain_a = keep_live(live_at(step), gain_grad, gain_a)
            grad = moved(new_grad, step, step - 1)
    *early, token = weight_grad_call(
        scalars_at(0), 1, dz_b, swapped(dz_b), needed_b, other_b, jnp.zeros((8, LANES), F32), ()
    )
    token, down_out, up_out = lax.optimization_barrier((token, down_out, up_out))
    _, pieces, _, stat, z, _ = first_record
    first_size = len(back_groups[0]) + 1
    result = last_call(
        scalars_at(0),
        weights,
        pieces,
        stat,
        z,
        grad,
        token,
        finish,
        offsets,
        send_order,
        wide,
        first_size,
    )
    dz, gain_parts = result[0], result[1 : 1 + first_size]
    if finish is not None:
        gain_b = result[-1]
    dz_a = keep_live(live_at(0), dz, dz_a)
    sent_a, dz_a = lax.optimization_barrier((sent_a, dz_a))
    other_a = swapped(sent_a)
    dz_a_other = swapped(dz_a)
    for n, group in enumerate(back_groups):
        if n:
            gain_parts = gain_parts.reshape((len(group) + 1, -1) + gain_parts.shape[1:])
        parts = reduce_round(gain_parts, group)
        if n == 0:
            grad_first, grad_second, token = weight_grad_call(
                scalars_at(0), 0, dz_a, dz_a_other, needed_a, other_a, parts[0], early
            )
            parts.append(token)
        gain_parts = functools.reduce(jnp.add, parts)
    gain = gain_parts.reshape(1, wide)
    for bit in reversed(range(merged)):
        mine, theirs = own_part(gain, gain.shape[1] // 2, bit)
        gain = mine + from_xor(theirs, 1 << bit)
    gain_a = keep_live(live_at(0), gain, gain_a)
    gain_other = swapped(jnp.where(lower, gain_b, gain_a))
    gain_total = jnp.where(lower, gain_a, gain_b) + gain_other
    return (
        down_out[None],
        up_out[None],
        grad_first[None],
        grad_second[None],
        gain_total,
    )


def solution(mesh):
    in_specs = (
        P(None, "seq"),
        P(None, "seq"),
        P(None, "seq"),
        P(None, "seq"),
        P("section", None, "seq", None),
        P("section", None, "seq"),
    )
    out_specs = (
        P("section", None, "seq"),
        P("section", None, "seq"),
        P("section", "seq", None),
        P("section", "seq", None),
        P("section", "seq"),
    )
    return jax.shard_map(
        per_device, mesh=mesh, in_specs=in_specs, out_specs=out_specs, check_vma=False
    )
```
